32 devices in a mesh: groups: 2 (over y), ep: 16 (over z, x, core), tp: 1.
Axes of the slice: x: 2, y: 2, z: 4, core: 2. Of those that a mesh axis runs over, the one named last changes fastest.
Arguments:
- queries: bfloat16 [128, 32, 128], P(('groups', 'ep'), 'tp'), parts along dimension 0, may hold values from -6 to 6
- key_cache: bfloat16 [128, 128, 2, 128], P(('groups', 'ep'), None, 'tp'), parts along dimension 0, may hold values from -6 to 6
- value_cache: bfloat16 [128, 128, 2, 128], P(('groups', 'ep'), None, 'tp'), parts along dimension 0, may hold values from -6 to 6
- new_key: bfloat16 [128, 2, 128], P(('groups', 'ep'), 'tp'), parts along dimension 0, may hold values from -6 to 6
- new_value: bfloat16 [128, 2, 128], P(('groups', 'ep'), 'tp'), parts along dimension 0, may hold values from -6 to 6
- lengths: int32 [128], P(('groups', 'ep')), parts along dimension 0, may hold values from 1 to 128, as said below
- residual: bfloat16 [512, 2048], P(('groups', 'ep'), 'tp'), parts along dimension 0, may hold values from -6 to 6
- norm_gain: float32 [2048], replicated, may hold values from 0.5 to 1.5
- routes: int32 [512, 8], P(('groups', 'ep')), parts along dimension 0, may hold values from 0 to 15, all different within a row; in each aligned block of 16 rows (0 to 15, 16 to 31, ...) at most 16 rows name the same one
- route_weights: float32 [512, 8], P(('groups', 'ep')), parts along dimension 0, may hold values from 0.05 to 0.4
- expert_in: bfloat16 [16, 2, 2048, 768], P('ep', None, None, 'tp'), may hold values from -0.125 to 0.125
- expert_down: bfloat16 [16, 768, 2048], P('ep', 'tp'), may hold values from -0.21875 to 0.21875
Outputs:
- attended: bfloat16 [128, 32, 128], P(('groups', 'ep'), 'tp'), parts along dimension 0
- moe_out: bfloat16 [512, 2048], P(('groups', 'ep'), 'tp'), parts along dimension 0
The draws below stay inside these ranges and needn't reach their ends.
There are 2 independent parts, one for each index of `groups`. The reference program is written for one: setup_inputs(seed, part) draws one part's arguments, and reference() takes and returns one part's arrays. A program takes and returns all parts, laid end to end along the dimension named above; an argument that names none is the same for every part. Nothing has to cross between parts.
Inputs may be any that keep to these rules, and one draw needn't show every extreme that they name: `routes`: each row names 8 different experts; among the 16 rows of one device (aligned blocks) no expert is named by more than 16 rows, a bound that some block reaches. `lengths`: the first row of every draw fills all 128 slots.
All inputs are finite; a program needn't handle non-finite values.
Results may differ from the reference program's by a relative error of at most 0.0075.
Values may be sent and summed in bfloat16 or wider, within the bound.
No kernel may reach another device: no remote copies, remote signals or barrier semaphores. Data moves between devices by JAX's collectives and lax.ppermute only.
A program may use at most 64 MiB of HBM per device.

```python
import math
import jax
import jax.numpy as jnp
import numpy as np
from jax import lax

D = 2048
FFH = 768
HEADS = 32
KV_HEADS = 2
HEAD_DIM = 128
TOP = 8
CTX = 128
ROWS_DEV = 16
EXPERTS = 16
CAP = 16
ATT_TOK = 64
TOKENS = 256
N_EP = 16


def draw_queries(key, part):
    key = jax.random.fold_in(key, 21)
    values = jax.random.truncated_normal(key, -6.0, 6.0, (ATT_TOK, HEADS, HEAD_DIM), jnp.float32)
    return values.astype(jnp.bfloat16)


def draw_key_cache(key, part):
    key = jax.random.fold_in(key, 22)
    values = jax.random.truncated_normal(key, -6.0, 6.0, (ATT_TOK, CTX, KV_HEADS, HEAD_DIM), jnp.float32)
    return values.astype(jnp.bfloat16)


def draw_new_key(key, part):
    key = jax.random.fold_in(key, 23)
    values = jax.random.truncated_normal(key, -6.0, 6.0, (ATT_TOK, KV_HEADS, HEAD_DIM), jnp.float32)
    return values.astype(jnp.bfloat16)


def draw_lengths(key, part):
    key = jax.random.fold_in(key, 11)
    values = jax.random.randint(key, (ATT_TOK,), 1, CTX + 1).astype(jnp.int32)
    return values.at[0].set(CTX)


def block_levels(stream_key, extent, cuts, least, high):
    loudness = 1.0
    for axis_at, shards_of in cuts:
        steps = jax.random.uniform(jax.random.fold_in(jax.random.fold_in(stream_key, 6), axis_at), (shards_of,), jnp.float32, least / len(cuts), high / len(cuts))
        loudness = loudness * jnp.repeat(jnp.exp(steps), extent[axis_at] // shards_of).reshape((-1,) + (1,) * (len(extent) - 1 - axis_at))
    return loudness


def shared_out(stream_key, own, number, rows, number_of, top, most, skew):
    ranking = jax.random.permutation(stream_key, number_of)
    heavy_load, common = portions_of(number_of, rows * top, most, skew, True), portions_of(number_of, rows * top, most, skew, False)
    places = jnp.arange(number_of)

    def named(tallies, rotation):
        used = int((tallies > 0).sum())
        fixed = max(1, used // 4)
        moved = fixed + (places - fixed + rotation * (used - fixed)) % max(1, number_of - fixed)
        return jnp.zeros((number_of,), jnp.int32).at[ranking[jnp.where(places < fixed, places, moved)]].set(jnp.asarray(tallies, jnp.int32))

    tallies = jnp.where(number % 4 == 0, named(heavy_load, number // 4), named(common, number - number // 4 - 1))
    mixed = jax.random.permutation(jax.random.fold_in(own, 3), number_of)
    donor, receiver = mixed[0:number_of // 2 * 2:2], mixed[1:number_of // 2 * 2:2]
    slack = jnp.minimum(tallies[donor] - 1, most - tallies[receiver]) // 2
    slack = jnp.where((donor == ranking[0]) | (receiver == ranking[0]) | (tallies[receiver] == 0), 0, jnp.maximum(slack, 0))
    moved = jax.random.randint(jax.random.fold_in(own, 4), (number_of // 2,), 0, 1 << 20) % (slack + 1)
    tallies = tallies.at[donor].add(-moved).at[receiver].add(moved)
    members = jnp.searchsorted(jnp.cumsum(tallies), jnp.arange(rows * top), side="right").astype(jnp.int32)
    grid = members.reshape(top, rows).T
    grid = grid[jax.random.permutation(jax.random.fold_in(own, 1), rows)]
    rotation = jax.random.randint(jax.random.fold_in(own, 2), (rows, 1), 0, top)
    return jnp.take_along_axis(grid, (jnp.arange(top)[None, :] + rotation) % top, axis=1)


def portions_of(number_of, total, reach, skew, full):
    weights = [(1 << 20) // math.isqrt(standing ** skew) + 1 for standing in range(1, number_of + 1)]
    largest = reach if full else min(reach, max(-(-total // number_of), total * weights[0] // sum(weights)))
    least = 1 if total - largest >= number_of - 1 else 0
    given, spare = [largest] + [least] * (number_of - 1), total - largest - least * (number_of - 1)
    while spare > 0:
        movable = [i for i in range(1, number_of) if given[i] < largest] or [i for i in range(1, number_of) if given[i] < reach]
        whole, remaining = sum([weights[i] for i in movable]), spare
        for i in movable:
            more = min(reach - given[i], max(1, remaining * weights[i] // whole), spare)
            given[i] = given[i] + more
            spare = spare - more
    return np.array(given)


def noise(rng, dims, scale, bound, cuts=(), kind=jnp.bfloat16):
    factor_of = block_levels(rng, dims, cuts, -0.22, 0.18) if cuts else 1.0
    values = jax.random.normal(rng, dims, jnp.float32) * scale * factor_of
    return jnp.minimum(jnp.maximum(values, -bound), bound).astype(kind)


def setup_inputs(seed: int = 0, part: int = 0) -> dict:
    arg_keys = jax.random.split(jax.random.key(seed), 13)
    part_splits = jax.random.split(jax.random.fold_in(arg_keys[12], part), 13)
    queries = draw_queries(jax.random.fold_in(jax.random.fold_in(arg_keys[12], part), 71), part)
    key_cache = draw_key_cache(jax.random.fold_in(jax.random.fold_in(arg_keys[12], part), 71), part)
    value_cache = noise(part_splits[2], (ATT_TOK, CTX, KV_HEADS, HEAD_DIM), 1.0, 6.0, ((0, 16),))
    new_key = draw_new_key(jax.random.fold_in(jax.random.fold_in(arg_keys[12], part), 71), part)
    new_value = noise(part_splits[4], (ATT_TOK, KV_HEADS, HEAD_DIM), 1.0, 6.0, ((0, 16),))
    lengths = draw_lengths(jax.random.fold_in(jax.random.fold_in(arg_keys[12], part), 71), part)
    residual = noise(part_splits[6], (TOKENS, D), 1.0, 6.0, ((0, 16),))
    norm_gain = jnp.clip(1.0 + 0.1 * jax.random.normal(arg_keys[7], (D,), jnp.float32), 0.5, 1.5)
    routes_keys = jax.random.split(jax.random.fold_in(part_splits[8], 1), TOKENS // ROWS_DEV)
    routes_turns = jax.random.permutation(jax.random.fold_in(part_splits[8], 3), TOKENS // ROWS_DEV)
    routes = jax.vmap(lambda own, number: shared_out(jax.random.fold_in(part_splits[8], 2), own, number, ROWS_DEV, EXPERTS, TOP, CAP, 2))(routes_keys, routes_turns).reshape((TOKENS, TOP))
    route_weights = jnp.clip(0.05 + 0.35 * jax.random.uniform(part_splits[9], (TOKENS, TOP), jnp.float32) ** block_levels(part_splits[9], (TOKENS, TOP), ((0, 16),), -0.2, 0.2), 0.05, 0.4)
    expert_in = noise(arg_keys[10], (EXPERTS, 2, D, FFH), D ** -0.5, 0.125, ((0, 16),))
    expert_down = noise(arg_keys[11], (EXPERTS, FFH, D), FFH ** -0.5, 0.21875, ((0, 16),))
    return {"queries": queries, "key_cache": key_cache, "value_cache": value_cache, "new_key": new_key, "new_value": new_value, "lengths": lengths, "residual": residual, "norm_gain": norm_gain, "routes": routes, "route_weights": route_weights, "expert_in": expert_in, "expert_down": expert_down}


def slot_index(routes):
    hits = (routes[:, :, None] == jnp.arange(EXPERTS)[None, None, :]).astype(jnp.int32)
    blocks = hits.reshape(N_EP, ROWS_DEV * TOP, EXPERTS)
    before = jnp.cumsum(blocks, axis=1) - blocks
    position = lax.optimization_barrier(jnp.sum(before * blocks, axis=2)).reshape(TOKENS, TOP)
    source = (jnp.arange(TOKENS, dtype=jnp.int32) // ROWS_DEV)[:, None]
    return (source * CAP + position).astype(jnp.int32)

def reference(queries, key_cache, value_cache, new_key, new_value, lengths, residual, norm_gain, routes, route_weights, expert_in, expert_down):
    group = HEADS // KV_HEADS
    scale = 1.0 / HEAD_DIM ** 0.5
    grouped = queries.astype(jnp.float32).reshape(ATT_TOK, KV_HEADS, group, HEAD_DIM)
    scores = jnp.einsum('akgd,ackd->akgc', grouped, key_cache.astype(jnp.float32)) * scale
    valid = (jnp.arange(CTX)[None, :] < lengths[:, None])[:, None, None, :]
    scores = jnp.where(valid, scores, -1e+30)
    own_score = jnp.einsum('akgd,akd->akg', grouped, new_key.astype(jnp.float32)) * scale
    largest = jnp.maximum(lax.optimization_barrier(jnp.max(scores, axis=-1)), own_score)
    cache_exp = jnp.exp(scores - largest[..., None])
    own_exp = jnp.exp(own_score - largest)
    total = lax.optimization_barrier(jnp.sum(cache_exp, axis=-1)) + own_exp
    cache_probs = (cache_exp / total[..., None]).astype(jnp.bfloat16)
    own_probs = (own_exp / total).astype(jnp.bfloat16)
    mixed = jnp.einsum('akgc,ackd->akgd', cache_probs.astype(jnp.float32), value_cache.astype(jnp.float32))
    mixed = mixed + own_probs.astype(jnp.float32)[..., None] * new_value.astype(jnp.float32)[:, :, None, :]
    attended = mixed.reshape(ATT_TOK, HEADS, HEAD_DIM).astype(jnp.bfloat16)
    wide = residual.astype(jnp.float32)
    normed = (wide * lax.rsqrt(lax.optimization_barrier(jnp.mean(wide * wide, axis=1, keepdims=True)) + 1e-06) * norm_gain).astype(jnp.bfloat16)
    slots = slot_index(routes)
    row_ids = jnp.broadcast_to(jnp.arange(TOKENS, dtype=jnp.int32)[:, None], (TOKENS, TOP))
    table = jnp.full((EXPERTS, N_EP * CAP), TOKENS, jnp.int32).at[routes, slots].set(row_ids)
    padded = jnp.concatenate([normed, jnp.zeros((1, D), jnp.bfloat16)], axis=0)

    def expert_ffn(operands):
        indices, weight_in, weight_down = operands
        chosen = padded[indices]
        gate_act = jnp.dot(chosen, weight_in[0], preferred_element_type=jnp.float32)
        up_act = jnp.dot(chosen, weight_in[1], preferred_element_type=jnp.float32)
        hidden = (jax.nn.silu(gate_act) * up_act).astype(jnp.bfloat16)
        return jnp.dot(hidden, weight_down, preferred_element_type=jnp.float32).astype(jnp.bfloat16)
    outputs = lax.map(expert_ffn, (table, expert_in, expert_down))
    picked = outputs[routes, slots].astype(jnp.float32)
    combined = lax.optimization_barrier(jnp.sum(route_weights[:, :, None] * picked, axis=1))
    moe_out = (wide + combined).astype(jnp.bfloat16)
    return (attended, moe_out)
```

```python
import jax
import jax.numpy as jnp
from jax import lax
from jax.sharding import PartitionSpec as P


def attention_block(queries, key_cache, value_cache, new_key, new_value, lengths):
    rows_here, heads_here, head_size = queries.shape
    kv_here = key_cache.shape[2]
    slots_here = key_cache.shape[1]
    group = heads_here // kv_here
    scale = 1.0 / head_size**0.5
    grouped = queries.reshape(rows_here, kv_here, group, head_size)
    scores = (
        jnp.einsum("akgd,ackd->akgc", grouped, key_cache, preferred_element_type=jnp.float32)
        * scale
    )
    valid = (jnp.arange(slots_here)[None, :] < lengths[:, None])[:, None, None, :]
    scores = jnp.where(valid, scores, -1e30)
    own_score = (
        jnp.einsum("akgd,akd->akg", grouped, new_key, preferred_element_type=jnp.float32) * scale
    )
    largest = jnp.maximum(jnp.max(scores, axis=-1), own_score)
    cache_exp = jnp.exp(scores - largest[..., None])
    own_exp = jnp.exp(own_score - largest)
    total = jnp.sum(cache_exp, axis=-1) + own_exp
    cache_probs = (cache_exp / total[..., None]).astype(jnp.bfloat16)
    own_probs = (own_exp / total).astype(jnp.bfloat16)
    mixed = jnp.einsum(
        "akgc,ackd->akgd", cache_probs, value_cache, preferred_element_type=jnp.float32
    )
    mixed = (
        mixed
        + own_probs.astype(jnp.float32)[..., None] * new_value.astype(jnp.float32)[:, :, None, :]
    )
    return mixed.reshape(rows_here, heads_here, head_size).astype(jnp.bfloat16)


def normalize(residual, norm_gain):
    wide = residual.astype(jnp.float32)
    return (
        wide * lax.rsqrt(jnp.mean(wide * wide, axis=1, keepdims=True) + 1e-06) * norm_gain
    ).astype(jnp.bfloat16)


def expert_layer_gathered(residual, norm_gain, routes, route_weights, expert_in, expert_down):
    row_count, width = residual.shape
    expert_count = lax.axis_size("ep")
    normed = normalize(residual, norm_gain)
    named = routes[:, :, None] == jnp.arange(expert_count)[None, None, :]
    weight = jnp.sum(jnp.where(named, route_weights[:, :, None], 0.0), axis=1)
    high = weight.astype(jnp.bfloat16)
    low = (weight - high.astype(jnp.float32)).astype(jnp.bfloat16)
    pad = jnp.zeros((row_count, 128 - 2 * expert_count % 128), jnp.bfloat16)
    packed = jnp.concatenate([normed, high, low, pad], axis=1)
    everyone = lax.all_gather(packed, "ep", axis=0, tiled=True)
    rows = everyone[:, :width]
    me = lax.axis_index("ep")
    pieces = everyone[:, width : width + 2 * expert_count].astype(jnp.float32)
    pieces = pieces.reshape(-1, 2, expert_count)
    mine = jnp.sum(jnp.where(jnp.arange(expert_count) == me, pieces, 0.0), axis=(1, 2))
    gate_act = jnp.dot(rows, expert_in[0, 0], preferred_element_type=jnp.float32)
    up_act = jnp.dot(rows, expert_in[0, 1], preferred_element_type=jnp.float32)
    hidden = (jax.nn.silu(gate_act) * up_act).astype(jnp.bfloat16)
    out = jnp.dot(hidden, expert_down[0], preferred_element_type=jnp.float32)
    weighted = (out * mine[:, None]).astype(jnp.bfloat16)
    combined = lax.psum_scatter(weighted, "ep", scatter_dimension=0, tiled=True)
    return (residual.astype(jnp.float32) + combined.astype(jnp.float32)).astype(jnp.bfloat16)


def expert_layer_routed(residual, norm_gain, routes, route_weights, expert_in, expert_down):
    row_count, top_count = routes.shape
    expert_count = expert_in.shape[0] * lax.axis_size("ep")
    capacity = min(row_count, max(2, 2 * row_count * top_count // expert_count))
    whole = lax.all_gather(residual, "tp", axis=1, tiled=True)
    width = whole.shape[1]
    half_width = residual.shape[1]
    normed = normalize(whole, norm_gain)
    flat_routes = routes.reshape(-1)
    hits = (flat_routes[:, None] == jnp.arange(expert_count)[None, :]).astype(jnp.int32)
    before = jnp.cumsum(hits, axis=0) - hits
    position = jnp.sum(before * hits, axis=1)
    slot_flat = flat_routes * capacity + position
    placed = (slot_flat[:, None] == jnp.arange(expert_count * capacity)[None, :]).astype(
        jnp.float32
    )
    placed = placed.reshape(row_count, top_count, expert_count * capacity)
    selector = jnp.sum(placed, axis=1).astype(jnp.bfloat16)
    buffer = jnp.einsum("rs,rd->sd", selector, normed, preferred_element_type=jnp.float32)
    buffer = buffer.astype(jnp.bfloat16).reshape(expert_count, capacity, width)
    arrived = lax.all_to_all(buffer, "ep", split_axis=0, concat_axis=0, tiled=True)
    sources = arrived.shape[0]
    flat_rows = arrived.reshape(sources * capacity, width)
    gate_act = jnp.dot(flat_rows, expert_in[0, 0], preferred_element_type=jnp.float32)
    up_act = jnp.dot(flat_rows, expert_in[0, 1], preferred_element_type=jnp.float32)
    hidden = (jax.nn.silu(gate_act) * up_act).astype(jnp.bfloat16)
    partial_value = jnp.dot(hidden, expert_down[0], preferred_element_type=jnp.float32)
    partial_value = partial_value.reshape(sources, capacity, width)
    summed = lax.psum_scatter(partial_value, "tp", scatter_dimension=2, tiled=True).astype(
        jnp.bfloat16
    )
    returned = lax.all_to_all(summed, "ep", split_axis=0, concat_axis=0, tiled=True)
    weighting = jnp.sum(placed * route_weights[:, :, None], axis=1)
    gathered_rows = returned.reshape(expert_count * capacity, half_width).astype(jnp.float32)
    combined = jnp.dot(weighting, gathered_rows, precision=lax.Precision.HIGHEST)
    return (residual.astype(jnp.float32) + combined).astype(jnp.bfloat16)


def per_device(
    queries,
    key_cache,
    value_cache,
    new_key,
    new_value,
    lengths,
    residual,
    norm_gain,
    routes,
    route_weights,
    expert_in,
    expert_down,
):
    attended = attention_block(queries, key_cache, value_cache, new_key, new_value, lengths)
    dense = lax.axis_size("tp") == 1 and lax.axis_size("ep") <= 4 * routes.shape[1]
    expert_layer = expert_layer_gathered if dense else expert_layer_routed
    moe_out = expert_layer(residual, norm_gain, routes, route_weights, expert_in, expert_down)
    return (attended, moe_out)


def solution(mesh):
    in_specs = (
        P(("groups", "ep"), "tp", None),
        P(("groups", "ep"), None, "tp", None),
        P(("groups", "ep"), None, "tp", None),
        P(("groups", "ep"), "tp", None),
        P(("groups", "ep"), "tp", None),
        P(("groups", "ep")),
        P(("groups", "ep"), "tp"),
        P(),
        P(("groups", "ep"), None),
        P(("groups", "ep"), None),
        P("ep", None, None, "tp"),
        P("ep", "tp", None),
    )
    out_specs = (P(("groups", "ep"), "tp", None), P(("groups", "ep"), "tp"))
    return jax.shard_map(
        per_device, mesh=mesh, in_specs=in_specs, out_specs=out_specs, check_vma=False
    )
```

```python
import functools

import jax
import jax.numpy as jnp
from jax import lax
from jax.experimental import pallas as pl
from jax.experimental.pallas import tpu as pltpu
from jax.sharding import PartitionSpec as P


def attention_block(queries, key_cache, value_cache, new_key, new_value, lengths):
    rows_here, heads_here, head_size = queries.shape
    kv_here = key_cache.shape[2]
    slots_here = key_cache.shape[1]
    group = heads_here // kv_here
    scale = 1.0 / head_size**0.5
    grouped = queries.reshape(rows_here, kv_here, group, head_size)
    scores = (
        jnp.einsum("akgd,ackd->akgc", grouped, key_cache, preferred_element_type=jnp.float32)
        * scale
    )
    valid = (jnp.arange(slots_here)[None, :] < lengths[:, None])[:, None, None, :]
    scores = jnp.where(valid, scores, -1e30)
    own_score = (
        jnp.einsum("akgd,akd->akg", grouped, new_key, preferred_element_type=jnp.float32) * scale
    )
    largest = jnp.maximum(jnp.max(scores, axis=-1), own_score)
    cache_exp = jnp.exp(scores - largest[..., None])
    own_exp = jnp.exp(own_score - largest)
    total = jnp.sum(cache_exp, axis=-1) + own_exp
    cache_probs = (cache_exp / total[..., None]).astype(jnp.bfloat16)
    own_probs = (own_exp / total).astype(jnp.bfloat16)
    mixed = jnp.einsum(
        "akgc,ackd->akgd", cache_probs, value_cache, preferred_element_type=jnp.float32
    )
    mixed = (
        mixed
        + own_probs.astype(jnp.float32)[..., None] * new_value.astype(jnp.float32)[:, :, None, :]
    )
    return mixed.reshape(rows_here, heads_here, head_size).astype(jnp.bfloat16)


def normalize(residual, norm_gain):
    wide = residual.astype(jnp.float32)
    return (
        wide * lax.rsqrt(jnp.mean(wide * wide, axis=1, keepdims=True) + 1e-06) * norm_gain
    ).astype(jnp.bfloat16)


def prepare_kernel(residual_ref, gain_ref, routes_ref, weights_ref, packed_ref):
    row_count, width = residual_ref.shape
    experts = lax.axis_size("ep")
    wide = residual_ref[...].astype(jnp.float32)
    mean = jnp.mean(wide * wide, axis=1, keepdims=True)
    packed_ref[:, :width] = (wide * lax.rsqrt(mean + 1e-06) * gain_ref[...]).astype(jnp.bfloat16)
    lane = lax.broadcasted_iota(jnp.int32, (row_count, packed_ref.shape[1] - width), 1)
    expert = lax.rem(lane, experts)
    weight = jnp.zeros(lane.shape, jnp.float32)
    for k in range(routes_ref.shape[1]):
        weight += jnp.where(routes_ref[:, k : k + 1] == expert, weights_ref[:, k : k + 1], 0.0)
    high = weight.astype(jnp.bfloat16).astype(jnp.float32)
    low = (weight - high).astype(jnp.bfloat16).astype(jnp.float32)
    lowest = weight - high - low
    terms = jnp.where(
        lane < experts,
        high,
        jnp.where(lane < 2 * experts, low, jnp.where(lane < 3 * experts, lowest, 0.0)),
    )
    packed_ref[:, width:] = terms.astype(jnp.bfloat16)


def ffn_kernel(block_count, *refs):
    blocks = refs[:block_count]
    in_ref, down_ref, out_ref = refs[block_count:]
    width = in_ref.shape[2]
    packed = jnp.concatenate([block[...] for block in blocks], axis=0)
    rows = packed[:, :width]
    terms = packed[:, width:].astype(jnp.float32)
    lane = lax.broadcasted_iota(jnp.int32, terms.shape, 1)
    mine = lax.rem(lane, lax.axis_size("ep")) == lax.axis_index("ep")
    weight = jnp.sum(jnp.where(mine, terms, 0.0), axis=1, keepdims=True)
    gate = jnp.dot(rows, in_ref[0, 0], preferred_element_type=jnp.float32)
    up = jnp.dot(rows, in_ref[0, 1], preferred_element_type=jnp.float32)
    hidden = (gate / (1.0 + jnp.exp(-gate)) * up).astype(jnp.bfloat16)
    out = jnp.dot(hidden, down_ref[0], preferred_element_type=jnp.float32)
    out_ref[...] = (out * weight).astype(jnp.bfloat16).reshape(out_ref.shape)


def pair_kernel(own_ref, other_ref, *out_refs):
    for i, out_ref in enumerate(out_refs):
        total = own_ref[i].astype(jnp.float32) + other_ref[i].astype(jnp.float32)
        out_ref[...] = total.astype(jnp.bfloat16)


def total_kernel(residual_ref, *refs):
    out_ref = refs[-1]
    total = residual_ref[...].astype(jnp.float32)
    for ref in refs[:-1]:
        total += ref[...].astype(jnp.float32)
    out_ref[...] = total.astype(jnp.bfloat16)


def expert_layer_gathered(residual, norm_gain, routes, route_weights, expert_in, expert_down):
    row_count, width = residual.shape
    devices = lax.axis_size("ep")
    pairs = devices // 2
    extra = -(-3 * devices // 128) * 128
    vmem = pltpu.VMEM
    params = pltpu.CompilerParams(vmem_limit_bytes=32 * 1024 * 1024)

    def swap(value, bits):
        return lax.ppermute(value, "ep", [(i, i ^ bits) for i in range(devices)])

    packed = pl.pallas_call(
        prepare_kernel,
        out_shape=vmem((row_count, width + extra), jnp.bfloat16),
        name="prepare",
    )(residual, norm_gain.reshape(1, -1), routes, route_weights)
    near = [packed] + [swap(packed, 2 * d) for d in range(1, pairs)]
    far = [swap(block, 1) for block in near]
    expert_in = pltpu.with_memory_space_constraint(expert_in, vmem)
    expert_down = pltpu.with_memory_space_constraint(expert_down, vmem)
    ffn = pl.pallas_call(
        functools.partial(ffn_kernel, pairs),
        out_shape=vmem((pairs, row_count, width), jnp.bfloat16),
        compiler_params=params,
        name="ffn",
    )
    far_out = ffn(*far, expert_in, expert_down)
    arrived = swap(far_out, 1)
    near_out = ffn(*near, expert_in, expert_down)
    summed = pl.pallas_call(
        pair_kernel,
        out_shape=[vmem((row_count, width), jnp.bfloat16)] * pairs,
        name="pair_sum",
    )(near_out, arrived)
    returned = [summed[0]] + [swap(summed[d], 2 * d) for d in range(1, pairs)]
    return pl.pallas_call(
        total_kernel,
        out_shape=jax.ShapeDtypeStruct((row_count, width), jnp.bfloat16),
        name="total",
    )(residual, *returned)


def expert_layer_routed(residual, norm_gain, routes, route_weights, expert_in, expert_down):
    row_count, top_count = routes.shape
    expert_count = expert_in.shape[0] * lax.axis_size("ep")
    capacity = min(row_count, max(2, 2 * row_count * top_count // expert_count))
    whole = lax.all_gather(residual, "tp", axis=1, tiled=True)
    width = whole.shape[1]
    half_width = residual.shape[1]
    normed = normalize(whole, norm_gain)
    flat_routes = routes.reshape(-1)
    hits = (flat_routes[:, None] == jnp.arange(expert_count)[None, :]).astype(jnp.int32)
    before = jnp.cumsum(hits, axis=0) - hits
    position = jnp.sum(before * hits, axis=1)
    slot_flat = flat_routes * capacity + position
    placed = (slot_flat[:, None] == jnp.arange(expert_count * capacity)[None, :]).astype(
        jnp.float32
    )
    placed = placed.reshape(row_count, top_count, expert_count * capacity)
    selector = jnp.sum(placed, axis=1).astype(jnp.bfloat16)
    buffer = jnp.einsum("rs,rd->sd", selector, normed, preferred_element_type=jnp.float32)
    buffer = buffer.astype(jnp.bfloat16).reshape(expert_count, capacity, width)
    arrived = lax.all_to_all(buffer, "ep", split_axis=0, concat_axis=0, tiled=True)
    sources = arrived.shape[0]
    flat_rows = arrived.reshape(sources * capacity, width)
    gate_act = jnp.dot(flat_rows, expert_in[0, 0], preferred_element_type=jnp.float32)
    up_act = jnp.dot(flat_rows, expert_in[0, 1], preferred_element_type=jnp.float32)
    hidden = (jax.nn.silu(gate_act) * up_act).astype(jnp.bfloat16)
    partial_value = jnp.dot(hidden, expert_down[0], preferred_element_type=jnp.float32)
    partial_value = partial_value.reshape(sources, capacity, width)
    summed = lax.psum_scatter(partial_value, "tp", scatter_dimension=2, tiled=True).astype(
        jnp.bfloat16
    )
    returned = lax.all_to_all(summed, "ep", split_axis=0, concat_axis=0, tiled=True)
    weighting = jnp.sum(placed * route_weights[:, :, None], axis=1)
    gathered_rows = returned.reshape(expert_count * capacity, half_width).astype(jnp.float32)
    combined = jnp.dot(weighting, gathered_rows, precision=lax.Precision.HIGHEST)
    return (residual.astype(jnp.float32) + combined).astype(jnp.bfloat16)


def per_device(
    queries,
    key_cache,
    value_cache,
    new_key,
    new_value,
    lengths,
    residual,
    norm_gain,
    routes,
    route_weights,
    expert_in,
    expert_down,
):
    attended = attention_block(queries, key_cache, value_cache, new_key, new_value, lengths)
    dense = lax.axis_size("tp") == 1 and lax.axis_size("ep") <= 4 * routes.shape[1]
    expert_layer = expert_layer_gathered if dense else expert_layer_routed
    moe_out = expert_layer(residual, norm_gain, routes, route_weights, expert_in, expert_down)
    return (attended, moe_out)


def solution(mesh):
    in_specs = (
        P(("groups", "ep"), "tp", None),
        P(("groups", "ep"), None, "tp", None),
        P(("groups", "ep"), None, "tp", None),
        P(("groups", "ep"), "tp", None),
        P(("groups", "ep"), "tp", None),
        P(("groups", "ep")),
        P(("groups", "ep"), "tp"),
        P(),
        P(("groups", "ep"), None),
        P(("groups", "ep"), None),
        P("ep", None, None, "tp"),
        P("ep", "tp", None),
    )
    out_specs = (P(("groups", "ep"), "tp", None), P(("groups", "ep"), "tp"))
    return jax.shard_map(
        per_device, mesh=mesh, in_specs=in_specs, out_specs=out_specs, check_vma=False
    )
```

```python
import functools

import jax
import jax.numpy as jnp
from jax import lax
from jax.experimental import pallas as pl
from jax.experimental.pallas import tpu as pltpu
from jax.sharding import PartitionSpec as P


def attention_block(queries, key_cache, value_cache, new_key, new_value, lengths):
    rows_here, heads_here, head_size = queries.shape
    kv_here = key_cache.shape[2]
    slots_here = key_cache.shape[1]
    group = heads_here // kv_here
    scale = 1.0 / head_size**0.5
    grouped = queries.reshape(rows_here, kv_here, group, head_size)
    scores = (
        jnp.einsum("akgd,ackd->akgc", grouped, key_cache, preferred_element_type=jnp.float32)
        * scale
    )
    valid = (jnp.arange(slots_here)[None, :] < lengths[:, None])[:, None, None, :]
    scores = jnp.where(valid, scores, -1e30)
    own_score = (
        jnp.einsum("akgd,akd->akg", grouped, new_key, preferred_element_type=jnp.float32) * scale
    )
    largest = jnp.maximum(jnp.max(scores, axis=-1), own_score)
    cache_exp = jnp.exp(scores - largest[..., None])
    own_exp = jnp.exp(own_score - largest)
    total = jnp.sum(cache_exp, axis=-1) + own_exp
    cache_probs = (cache_exp / total[..., None]).astype(jnp.bfloat16)
    own_probs = (own_exp / total).astype(jnp.bfloat16)
    mixed = jnp.einsum(
        "akgc,ackd->akgd", cache_probs, value_cache, preferred_element_type=jnp.float32
    )
    mixed = (
        mixed
        + own_probs.astype(jnp.float32)[..., None] * new_value.astype(jnp.float32)[:, :, None, :]
    )
    return mixed.reshape(rows_here, heads_here, head_size).astype(jnp.bfloat16)


def normalize(residual, norm_gain):
    wide = residual.astype(jnp.float32)
    return (
        wide * lax.rsqrt(jnp.mean(wide * wide, axis=1, keepdims=True) + 1e-06) * norm_gain
    ).astype(jnp.bfloat16)


def attend_kernel(
    lengths_hbm,
    queries_hbm,
    keys_hbm,
    values_hbm,
    new_keys_hbm,
    new_values_hbm,
    in_ref,
    down_ref,
    attended_ref,
    held_in_ref,
    held_down_ref,
    lengths_ref,
    queries_ref,
    keys_ref,
    values_ref,
    new_keys_ref,
    new_values_ref,
    sems,
    load_sems,
):
    loads = load(
        (lengths_hbm, queries_hbm, keys_hbm, values_hbm, new_keys_hbm, new_values_hbm),
        (lengths_ref, queries_ref, keys_ref, values_ref, new_keys_ref, new_values_ref),
        load_sems,
    )
    copies = []
    for source, target in ((in_ref, held_in_ref), (down_ref, held_down_ref)):
        lines = source.shape[-2] // 2
        for outer in range(source.shape[1] if len(source.shape) == 4 else 1):
            for half in range(2):
                at = (0, outer) if len(source.shape) == 4 else (0,)
                at = at + (pl.ds(half * lines, lines),)
                copies.append(
                    pltpu.make_async_copy(source.at[at], target.at[at], sems.at[len(copies)])
                )
    for copy in copies:
        copy.start()
    row_count, heads, head_size = queries_ref.shape
    kv_heads = new_keys_ref.shape[0] // row_count
    group = heads // kv_heads
    scale = 1.0 / head_size**0.5
    across = (((1,), (1,)), ((), ()))

    def grids(columns):
        shape = (heads, columns)
        head = lax.broadcasted_iota(jnp.int32, shape, 0) // group
        return head, lax.broadcasted_iota(jnp.int32, shape, 1)

    head, column = grids(keys_ref.shape[1])
    own_head, own_column = grids(new_keys_ref.shape[0])
    same_head = column % kv_heads == head
    slot = column // kv_heads
    for copy in loads:
        copy.wait()
    for a in range(row_count):
        query = queries_ref[a]
        scores = lax.dot_general(query, keys_ref[a], across, preferred_element_type=jnp.float32)
        scores = jnp.where(same_head & (slot < lengths_ref[a]), scores * scale, -1e30)
        own = lax.dot_general(
            query, new_keys_ref[...], across, preferred_element_type=jnp.float32
        )
        own = jnp.where(own_column == own_head + a * kv_heads, own * scale, -1e30)
        largest = jnp.maximum(
            jnp.max(scores, axis=1, keepdims=True), jnp.max(own, axis=1, keepdims=True)
        )
        scores = jnp.exp(scores - largest)
        own = jnp.exp(own - largest)
        total = jnp.sum(scores, axis=1, keepdims=True) + jnp.sum(own, axis=1, keepdims=True)
        mixed = jnp.dot(
            (scores / total).astype(jnp.bfloat16),
            values_ref[a],
            preferred_element_type=jnp.float32,
        ) + jnp.dot(
            (own / total).astype(jnp.bfloat16),
            new_values_ref[...],
            preferred_element_type=jnp.float32,
        )
        attended_ref[a] = mixed.astype(jnp.bfloat16)
    for copy in copies:
        copy.wait()


def attend_and_hold(
    queries, key_cache, value_cache, new_key, new_value, lengths, expert_in, expert_down
):
    rows_here, slots_here, kv_here, head_size = key_cache.shape
    lines = (rows_here, slots_here * kv_here, head_size)
    vmem = pltpu.VMEM
    return pl.pallas_call(
        attend_kernel,
        out_shape=[
            jax.ShapeDtypeStruct(queries.shape, jnp.bfloat16),
            vmem(expert_in.shape, jnp.bfloat16),
            vmem(expert_down.shape, jnp.bfloat16),
        ],
        in_specs=[pl.BlockSpec(memory_space=pltpu.HBM)] * 8,
        scratch_shapes=[
            pltpu.SMEM(lengths.shape, jnp.int32),
            vmem(queries.shape, jnp.bfloat16),
            vmem(lines, jnp.bfloat16),
            vmem(lines, jnp.bfloat16),
            vmem((rows_here * kv_here, head_size), jnp.bfloat16),
            vmem((rows_here * kv_here, head_size), jnp.bfloat16),
            pltpu.SemaphoreType.DMA((2 * expert_in.shape[1] + 2,)),
            pltpu.SemaphoreType.DMA((6,)),
        ],
        cost_estimate=pl.CostEstimate(
            flops=0,
            bytes_accessed=2 * (expert_in.size + expert_down.size),
            transcendentals=0,
        ),
        compiler_params=pltpu.CompilerParams(vmem_limit_bytes=4 * 1024 * 1024),
        name="attend",
    )(
        stay(lengths),
        stay(queries),
        stay(key_cache.reshape(lines)),
        stay(value_cache.reshape(lines)),
        stay(new_key.reshape(-1, head_size)),
        stay(new_value.reshape(-1, head_size)),
        stay(expert_in),
        stay(expert_down),
    )


def load(sources, targets, sems):
    copies = [
        pltpu.make_async_copy(source, target, sems.at[i])
        for i, (source, target) in enumerate(zip(sources, targets))
    ]
    for copy in copies:
        copy.start()
    return copies


def stay(array):
    return pltpu.with_memory_space_constraint(array, pltpu.HBM)


def prepare_kernel(*refs):
    packed_ref, residual_ref, gain_ref, routes_ref, weights_ref, sems = refs[4:]
    for copy in load(refs[:4], refs[5:9], sems):
        copy.wait()
    row_count, width = residual_ref.shape
    experts = lax.axis_size("ep")
    lanes = packed_ref.shape[1] - width
    wide = residual_ref[...].astype(jnp.float32)
    mean = jnp.mean(wide * wide, axis=1, keepdims=True)
    packed_ref[:, :width] = (wide * lax.rsqrt(mean + 1e-06) * gain_ref[...]).astype(jnp.bfloat16)
    line = lax.broadcasted_iota(jnp.int32, (lanes, row_count), 0)
    expert = lax.rem(line, experts)
    weight = jnp.zeros(line.shape, jnp.float32)
    for k in range(routes_ref.shape[0]):
        weight += jnp.where(routes_ref[k : k + 1, :] == expert, weights_ref[k : k + 1, :], 0.0)
    high = weight.astype(jnp.bfloat16).astype(jnp.float32)
    low = (weight - high).astype(jnp.bfloat16).astype(jnp.float32)
    lowest = weight - high - low
    terms = jnp.where(
        line < experts,
        high,
        jnp.where(line < 2 * experts, low, jnp.where(line < 3 * experts, lowest, 0.0)),
    )
    at = lax.broadcasted_iota(jnp.int32, (row_count, row_count), 0)
    same = at == lax.broadcasted_iota(jnp.int32, (row_count, row_count), 1)
    turned = lax.dot_general(
        same.astype(jnp.bfloat16),
        terms.astype(jnp.bfloat16),
        (((1,), (1,)), ((), ())),
        preferred_element_type=jnp.float32,
    )
    packed_ref[:, width:] = turned.astype(jnp.bfloat16)


def ffn_kernel(block_count, *refs):
    blocks = refs[:block_count]
    in_ref, down_ref, near_ref, far_ref = refs[block_count:]
    width = in_ref.shape[2]
    packed = jnp.concatenate([block[...] for block in blocks], axis=0)
    rows = packed[:, :width]
    terms = packed[:, width:].astype(jnp.float32)
    lane = lax.broadcasted_iota(jnp.int32, terms.shape, 1)
    mine = lax.rem(lane, lax.axis_size("ep")) == lax.axis_index("ep")
    weight = jnp.sum(jnp.where(mine, terms, 0.0), axis=1, keepdims=True)
    gate = jnp.dot(rows, in_ref[0, 0], preferred_element_type=jnp.float32)
    up = jnp.dot(rows, in_ref[0, 1], preferred_element_type=jnp.float32)
    hidden = (gate / (1.0 + jnp.exp(-gate)) * up).astype(jnp.bfloat16)
    out = jnp.dot(hidden, down_ref[0], preferred_element_type=jnp.float32)
    out = (out * weight).astype(jnp.bfloat16).reshape((2,) + near_ref.shape)
    near_ref[...] = out[0]
    far_ref[...] = out[1]


def pair_kernel(own_ref, other_ref, keep_ref, send_ref):
    half = keep_ref.shape[0]
    keep_ref[...] = own_ref[:half].astype(jnp.float32) + other_ref[:half].astype(jnp.float32)
    send = own_ref[half:].astype(jnp.float32) + other_ref[half:].astype(jnp.float32)
    send_ref[...] = send.astype(jnp.bfloat16)


def square_kernel(own_ref, other_ref, *out_refs):
    for i, out_ref in enumerate(out_refs):
        total = own_ref[i] + other_ref[i].astype(jnp.float32)
        out_ref[...] = total.astype(out_ref.dtype)


def total_kernel(residual_ref, *refs):
    out_ref = refs[-1]
    total = residual_ref[...].astype(jnp.float32)
    for ref in refs[:-1]:
        total += ref[...].astype(jnp.float32)
    out_ref[...] = total.astype(jnp.bfloat16)


def small(kernel, out_shape, name, mebibytes=4):
    return pl.pallas_call(
        kernel,
        out_shape=out_shape,
        compiler_params=pltpu.CompilerParams(vmem_limit_bytes=mebibytes * 1024 * 1024),
        name=name,
    )


def from_hbm(kernel, out_shape, name, *arrays):
    return pl.pallas_call(
        kernel,
        out_shape=out_shape,
        in_specs=[pl.BlockSpec(memory_space=pltpu.HBM)] * len(arrays),
        scratch_shapes=[pltpu.VMEM(array.shape, array.dtype) for array in arrays]
        + [pltpu.SemaphoreType.DMA((len(arrays),))],
        compiler_params=pltpu.CompilerParams(vmem_limit_bytes=4 * 1024 * 1024),
        name=name,
    )(*(stay(array) for array in arrays))


def expert_layer_gathered(residual, norm_gain, routes, route_weights, expert_in, expert_down):
    row_count, width = residual.shape
    devices = lax.axis_size("ep")
    squares = devices // 4
    extra = -(-3 * devices // 128) * 128
    vmem = pltpu.VMEM

    def swap(value, bits):
        return lax.ppermute(value, "ep", [(i, i ^ bits) for i in range(devices)])

    packed = from_hbm(
        prepare_kernel,
        vmem((row_count, width + extra), jnp.bfloat16),
        "prepare",
        residual,
        norm_gain.reshape(1, -1),
        routes.T,
        route_weights.T,
    )
    along = {d: swap(packed, 4 * d) for d in range(squares - 1, 0, -1)}
    along[0] = packed
    across = {d: swap(along[d], 2) for d in range(squares - 1, -1, -1)}
    far_along = {d: swap(along[d], 1) for d in range(squares - 1, -1, -1)}
    far_across = {d: swap(across[d], 1) for d in range(squares - 1, -1, -1)}
    expert_in = pltpu.with_memory_space_constraint(expert_in, vmem)
    expert_down = pltpu.with_memory_space_constraint(expert_down, vmem)

    def part(members):
        half = len(members)
        blocks = [source[d] for source in (along, across, far_along, far_across) for d in members]
        whole = (2 * half, row_count, width)
        near_out, far_out = small(
            functools.partial(ffn_kernel, len(blocks)), [vmem(whole, jnp.bfloat16)] * 2, "ffn", 16
        )(*blocks, expert_in, expert_down)
        shape = (half, row_count, width)
        keep, send = small(
            pair_kernel, [vmem(shape, jnp.float32), vmem(shape, jnp.bfloat16)], "pair_sum"
        )(near_out, swap(far_out, 1))
        outs = [vmem((row_count, width), jnp.bfloat16 if d else jnp.float32) for d in members]
        sums = small(square_kernel, outs, "square_sum")(keep, swap(send, 2))
        return [swap(value, 4 * d) if d else value for d, value in zip(members, sums)]

    later = part(list(range(squares - 1, squares // 2 - 1, -1)))
    sooner = part(list(range(squares // 2 - 1, -1, -1)))
    return small(total_kernel, jax.ShapeDtypeStruct((row_count, width), jnp.bfloat16), "total")(
        residual, *sooner, *later
    )


def expert_layer_routed(residual, norm_gain, routes, route_weights, expert_in, expert_down):
    row_count, top_count = routes.shape
    expert_count = expert_in.shape[0] * lax.axis_size("ep")
    capacity = min(row_count, max(2, 2 * row_count * top_count // expert_count))
    whole = lax.all_gather(residual, "tp", axis=1, tiled=True)
    width = whole.shape[1]
    half_width = residual.shape[1]
    normed = normalize(whole, norm_gain)
    flat_routes = routes.reshape(-1)
    hits = (flat_routes[:, None] == jnp.arange(expert_count)[None, :]).astype(jnp.int32)
    before = jnp.cumsum(hits, axis=0) - hits
    position = jnp.sum(before * hits, axis=1)
    slot_flat = flat_routes * capacity + position
    placed = (slot_flat[:, None] == jnp.arange(expert_count * capacity)[None, :]).astype(
        jnp.float32
    )
    placed = placed.reshape(row_count, top_count, expert_count * capacity)
    selector = jnp.sum(placed, axis=1).astype(jnp.bfloat16)
    buffer = jnp.einsum("rs,rd->sd", selector, normed, preferred_element_type=jnp.float32)
    buffer = buffer.astype(jnp.bfloat16).reshape(expert_count, capacity, width)
    arrived = lax.all_to_all(buffer, "ep", split_axis=0, concat_axis=0, tiled=True)
    sources = arrived.shape[0]
    flat_rows = arrived.reshape(sources * capacity, width)
    gate_act = jnp.dot(flat_rows, expert_in[0, 0], preferred_element_type=jnp.float32)
    up_act = jnp.dot(flat_rows, expert_in[0, 1], preferred_element_type=jnp.float32)
    hidden = (jax.nn.silu(gate_act) * up_act).astype(jnp.bfloat16)
    partial_value = jnp.dot(hidden, expert_down[0], preferred_element_type=jnp.float32)
    partial_value = partial_value.reshape(sources, capacity, width)
    summed = lax.psum_scatter(partial_value, "tp", scatter_dimension=2, tiled=True).astype(
        jnp.bfloat16
    )
    returned = lax.all_to_all(summed, "ep", split_axis=0, concat_axis=0, tiled=True)
    weighting = jnp.sum(placed * route_weights[:, :, None], axis=1)
    gathered_rows = returned.reshape(expert_count * capacity, half_width).astype(jnp.float32)
    combined = jnp.dot(weighting, gathered_rows, precision=lax.Precision.HIGHEST)
    return (residual.astype(jnp.float32) + combined).astype(jnp.bfloat16)


def per_device(
    queries,
    key_cache,
    value_cache,
    new_key,
    new_value,
    lengths,
    residual,
    norm_gain,
    routes,
    route_weights,
    expert_in,
    expert_down,
):
    devices = lax.axis_size("ep")
    dense = lax.axis_size("tp") == 1 and 8 <= devices <= 4 * routes.shape[1] and devices & (devices - 1) == 0
    attention = (queries, key_cache, value_cache, new_key, new_value, lengths)
    layer = (residual, norm_gain, routes, route_weights)
    if dense:
        attended, *experts = attend_and_hold(*attention, expert_in, expert_down)
        return (attended, expert_layer_gathered(*layer, *experts))
    attended = attention_block(*attention)
    return (attended, expert_layer_routed(*layer, expert_in, expert_down))


def solution(mesh):
    in_specs = (
        P(("groups", "ep"), "tp", None),
        P(("groups", "ep"), None, "tp", None),
        P(("groups", "ep"), None, "tp", None),
        P(("groups", "ep"), "tp", None),
        P(("groups", "ep"), "tp", None),
        P(("groups", "ep")),
        P(("groups", "ep"), "tp"),
        P(),
        P(("groups", "ep"), None),
        P(("groups", "ep"), None),
        P("ep", None, None, "tp"),
        P("ep", "tp", None),
    )
    out_specs = (P(("groups", "ep"), "tp", None), P(("groups", "ep"), "tp"))
    return jax.shard_map(
        per_device, mesh=mesh, in_specs=in_specs, out_specs=out_specs, check_vma=False
    )
```

```python
import functools

import jax
import jax.numpy as jnp
from jax import lax
from jax.experimental import pallas as pl
from jax.experimental.pallas import tpu as pltpu
from jax.sharding import PartitionSpec as P


def attention_block(queries, key_cache, value_cache, new_key, new_value, lengths):
    rows_here, heads_here, head_size = queries.shape
    kv_here = key_cache.shape[2]
    slots_here = key_cache.shape[1]
    group = heads_here // kv_here
    scale = 1.0 / head_size**0.5
    grouped = queries.reshape(rows_here, kv_here, group, head_size)
    scores = (
        jnp.einsum("akgd,ackd->akgc", grouped, key_cache, preferred_element_type=jnp.float32)
        * scale
    )
    valid = (jnp.arange(slots_here)[None, :] < lengths[:, None])[:, None, None, :]
    scores = jnp.where(valid, scores, -1e30)
    own_score = (
        jnp.einsum("akgd,akd->akg", grouped, new_key, preferred_element_type=jnp.float32) * scale
    )
    largest = jnp.maximum(jnp.max(scores, axis=-1), own_score)
    cache_exp = jnp.exp(scores - largest[..., None])
    own_exp = jnp.exp(own_score - largest)
    total = jnp.sum(cache_exp, axis=-1) + own_exp
    cache_probs = (cache_exp / total[..., None]).astype(jnp.bfloat16)
    own_probs = (own_exp / total).astype(jnp.bfloat16)
    mixed = jnp.einsum(
        "akgc,ackd->akgd", cache_probs, value_cache, preferred_element_type=jnp.float32
    )
    mixed = (
        mixed
        + own_probs.astype(jnp.float32)[..., None] * new_value.astype(jnp.float32)[:, :, None, :]
    )
    return mixed.reshape(rows_here, heads_here, head_size).astype(jnp.bfloat16)


def normalize(residual, norm_gain):
    wide = residual.astype(jnp.float32)
    return (
        wide * lax.rsqrt(jnp.mean(wide * wide, axis=1, keepdims=True) + 1e-06) * norm_gain
    ).astype(jnp.bfloat16)


def load(sources, targets, sems):
    copies = [
        pltpu.make_async_copy(source, target, sems.at[i])
        for i, (source, target) in enumerate(zip(sources, targets))
    ]
    for copy in copies:
        copy.start()
    return copies


def stay(array):
    return pltpu.with_memory_space_constraint(array, pltpu.HBM)


HERE = pl.BlockSpec(memory_space=pltpu.VMEM)
ANYWHERE = pl.BlockSpec(memory_space=pl.ANY)


def params(mebibytes=4):
    return pltpu.CompilerParams(vmem_limit_bytes=mebibytes * 1024 * 1024)


def from_hbm(kernel, out_shape, name, arrays, after=()):
    return pl.pallas_call(
        kernel,
        out_shape=out_shape,
        in_specs=[pl.BlockSpec(memory_space=pltpu.HBM)] * len(arrays) + [ANYWHERE] * len(after),
        scratch_shapes=[
            (pltpu.VMEM if array.ndim > 1 else pltpu.SMEM)(array.shape, array.dtype)
            for array in arrays
        ]
        + [pltpu.SemaphoreType.DMA((len(arrays),))],
        compiler_params=params(),
        name=name,
    )(*(stay(array) for array in arrays), *after)


def attend_kernel(*refs):
    attended_ref = refs[-8]
    lengths_ref, queries_ref, keys_ref, values_ref, new_keys_ref, new_values_ref = refs[-7:-1]
    copies = load(refs[:6], refs[-7:-1], refs[-1])
    row_count, heads, head_size = queries_ref.shape
    kv_heads = new_keys_ref.shape[0] // row_count
    group = heads // kv_heads
    scale = 1.0 / head_size**0.5
    across = (((1,), (1,)), ((), ()))

    def grids(columns):
        shape = (heads, columns)
        head = lax.broadcasted_iota(jnp.int32, shape, 0) // group
        return head, lax.broadcasted_iota(jnp.int32, shape, 1)

    head, column = grids(keys_ref.shape[1])
    own_head, own_column = grids(new_keys_ref.shape[0])
    same_head = column % kv_heads == head
    slot = column // kv_heads
    for copy in copies:
        copy.wait()
    for a in range(row_count):
        query = queries_ref[a]
        scores = lax.dot_general(query, keys_ref[a], across, preferred_element_type=jnp.float32)
        scores = jnp.where(same_head & (slot < lengths_ref[a]), scores * scale, -1e30)
        own = lax.dot_general(
            query, new_keys_ref[...], across, preferred_element_type=jnp.float32
        )
        own = jnp.where(own_column == own_head + a * kv_heads, own * scale, -1e30)
        largest = jnp.maximum(
            jnp.max(scores, axis=1, keepdims=True), jnp.max(own, axis=1, keepdims=True)
        )
        scores = jnp.exp(scores - largest)
        own = jnp.exp(own - largest)
        total = jnp.sum(scores, axis=1, keepdims=True) + jnp.sum(own, axis=1, keepdims=True)
        mixed = jnp.dot(
            (scores / total).astype(jnp.bfloat16),
            values_ref[a],
            preferred_element_type=jnp.float32,
        ) + jnp.dot(
            (own / total).astype(jnp.bfloat16),
            new_values_ref[...],
            preferred_element_type=jnp.float32,
        )
        attended_ref[a] = mixed.astype(jnp.bfloat16)


def attend(queries, key_cache, value_cache, new_key, new_value, lengths, after):
    rows_here, slots_here, kv_here, head_size = key_cache.shape
    lines = (rows_here, slots_here * kv_here, head_size)
    arrays = (
        lengths,
        queries,
        key_cache.reshape(lines),
        value_cache.reshape(lines),
        new_key.reshape(-1, head_size),
        new_value.reshape(-1, head_size),
    )
    out_shape = jax.ShapeDtypeStruct(queries.shape, jnp.bfloat16)
    return from_hbm(attend_kernel, out_shape, "attend", arrays, after)


def hold_kernel(pieces, source_ref, *refs):
    target_ref, sems = refs[-2:]
    lines = source_ref.shape[0] // pieces
    at = [pl.ds(i * lines, lines) for i in range(pieces)]
    for copy in load([source_ref.at[i] for i in at], [target_ref.at[i] for i in at], sems):
        copy.wait()


def hold(array, after, pieces=4):
    flat = array.reshape(-1, array.shape[-1])
    held = pl.pallas_call(
        functools.partial(hold_kernel, pieces),
        out_shape=pltpu.VMEM(flat.shape, flat.dtype),
        in_specs=[pl.BlockSpec(memory_space=pltpu.HBM)] + [ANYWHERE] * len(after),
        scratch_shapes=[pltpu.SemaphoreType.DMA((pieces,))],
        cost_estimate=pl.CostEstimate(flops=0, bytes_accessed=2 * flat.size, transcendentals=0),
        compiler_params=params(),
        name="hold",
    )(stay(flat), *after)
    return held


def prepare_kernel(*refs):
    packed_ref, residual_ref, gain_ref, routes_ref, weights_ref, sems = refs[4:]
    for copy in load(refs[:4], refs[5:9], sems):
        copy.wait()
    row_count, width = residual_ref.shape
    experts = lax.axis_size("ep")
    lanes = packed_ref.shape[1] - width
    wide = residual_ref[...].astype(jnp.float32)
    mean = jnp.mean(wide * wide, axis=1, keepdims=True)
    packed_ref[:, :width] = (wide * lax.rsqrt(mean + 1e-06) * gain_ref[...]).astype(jnp.bfloat16)
    line = lax.broadcasted_iota(jnp.int32, (lanes, row_count), 0)
    expert = lax.rem(line, experts)
    weight = jnp.zeros(line.shape, jnp.float32)
    for k in range(routes_ref.shape[0]):
        weight += jnp.where(routes_ref[k : k + 1, :] == expert, weights_ref[k : k + 1, :], 0.0)
    high = weight.astype(jnp.bfloat16).astype(jnp.float32)
    low = (weight - high).astype(jnp.bfloat16).astype(jnp.float32)
    lowest = weight - high - low
    terms = jnp.where(
        line < experts,
        high,
        jnp.where(line < 2 * experts, low, jnp.where(line < 3 * experts, lowest, 0.0)),
    )
    at = lax.broadcasted_iota(jnp.int32, (row_count, row_count), 0)
    same = at == lax.broadcasted_iota(jnp.int32, (row_count, row_count), 1)
    turned = lax.dot_general(
        same.astype(jnp.bfloat16),
        terms.astype(jnp.bfloat16),
        (((1,), (1,)), ((), ())),
        preferred_element_type=jnp.float32,
    )
    packed_ref[:, width:] = turned.astype(jnp.bfloat16)


def stack_kernel(first_ref, second_ref, *refs):
    refs[-1][0] = first_ref[...]
    refs[-1][1] = second_ref[...]


def relay_kernel(block_ref, *refs):
    refs[-1][...] = block_ref[...]


def ffn_kernel(near_a, near_b, far_a, far_b, in_ref, down_ref, *refs):
    near_ref, far_ref = refs[-2:]
    blocks, row_count, width = near_ref.shape
    packed = [block[...] for block in (near_a, near_b, far_a, far_b)]
    packed = jnp.concatenate(packed, axis=0).reshape(2 * blocks * row_count, -1)
    rows = packed[:, :width]
    terms = packed[:, width:].astype(jnp.float32)
    lane = lax.broadcasted_iota(jnp.int32, terms.shape, 1)
    mine = lax.rem(lane, lax.axis_size("ep")) == lax.axis_index("ep")
    weight = jnp.sum(jnp.where(mine, terms, 0.0), axis=1, keepdims=True)
    gate = jnp.dot(rows, in_ref[:width], preferred_element_type=jnp.float32)
    up = jnp.dot(rows, in_ref[width:], preferred_element_type=jnp.float32)
    hidden = (gate / (1.0 + jnp.exp(-gate)) * up).astype(jnp.bfloat16)
    out = jnp.dot(hidden, down_ref[...], preferred_element_type=jnp.float32)
    out = (out * weight).astype(jnp.bfloat16).reshape((2,) + near_ref.shape)
    near_ref[...] = out[0]
    far_ref[...] = out[1]


def pair_kernel(own_ref, other_ref, *refs):
    keep_ref, send_ref = refs[-2:]
    half = keep_ref.shape[0]
    keep_ref[...] = own_ref[:half].astype(jnp.float32) + other_ref[:half].astype(jnp.float32)
    send = own_ref[half:].astype(jnp.float32) + other_ref[half:].astype(jnp.float32)
    send_ref[...] = send.astype(jnp.bfloat16)


def add_kernel(own_ref, other_ref, out_ref):
    out_ref[...] = (own_ref[...] + other_ref[...].astype(jnp.float32)).astype(out_ref.dtype)


def fold_kernel(first_ref, second_ref, third_ref, keep_ref, send_ref):
    total = first_ref[...] + second_ref[...].astype(jnp.float32) + third_ref[...].astype(jnp.float32)
    keep_ref[...] = total[0]
    send_ref[...] = total[1].astype(jnp.bfloat16)


def total_kernel(residual_ref, own_ref, other_ref, out_ref):
    total = residual_ref[...].astype(jnp.float32) + own_ref[...] + other_ref[...].astype(jnp.float32)
    out_ref[...] = total.astype(jnp.bfloat16)


def in_vmem(kernel, out_shape, name, arrays, after=(), mebibytes=4):
    return pl.pallas_call(
        kernel,
        out_shape=out_shape,
        in_specs=[HERE] * len(arrays) + [ANYWHERE] * len(after),
        compiler_params=params(mebibytes),
        name=name,
    )(*arrays, *after)


def layer_gathered(attention, residual, norm_gain, routes, route_weights, expert_in, expert_down):
    row_count, width = residual.shape
    devices = lax.axis_size("ep")
    core, side, near, far = 1, 2, 4, 8
    extra = -(-3 * devices // 128) * 128
    vmem = pltpu.VMEM
    two = (2, row_count, width)
    four = (4, row_count, width)

    def swap(value, bit):
        return lax.ppermute(value, "ep", [(i, i ^ bit) for i in range(devices)])

    packed = from_hbm(
        prepare_kernel,
        vmem((row_count, width + extra), jnp.bfloat16),
        "prepare",
        (residual, norm_gain.reshape(1, -1), routes.T, route_weights.T),
    )
    opposite = swap(packed, far)
    held_in = hold(expert_in, (packed,))
    first = in_vmem(
        stack_kernel,
        vmem((2,) + packed.shape, jnp.bfloat16),
        "stack",
        (packed, opposite),
        (held_in,),
    )
    second = swap(first, near)
    first_side = swap(first, side)
    held_down = hold(expert_down, (first,))
    first_far = [swap(first, core), swap(first_side, core)]
    ready = in_vmem(
        relay_kernel,
        vmem(first.shape, jnp.bfloat16),
        "relay",
        (second,),
        (first_side, held_down),
    )
    second_side = swap(ready, side)
    second_far = [swap(second, core), swap(second_side, core)]

    def ffn(blocks, after=()):
        return in_vmem(
            ffn_kernel,
            [vmem(four, jnp.bfloat16)] * 2,
            "ffn",
            (*blocks, held_in, held_down),
            after,
            mebibytes=16,
        )

    def pair_sum(near_out, far_out, after=()):
        shapes = [vmem(two, jnp.float32), vmem(two, jnp.bfloat16)]
        return in_vmem(pair_kernel, shapes, "pair_sum", (near_out, swap(far_out, core)), after)

    first_keep, first_send = pair_sum(*ffn((first, first_side, *first_far)))
    first_back = swap(first_send, side)
    second_outs = ffn((second, second_side, *second_far), (first_send,))
    second_keep, second_send = pair_sum(*second_outs, (first_back,))
    second_back = swap(second_send, side)
    attended = attend(*attention, (second_send,))
    second_sum = in_vmem(
        add_kernel, vmem(two, jnp.bfloat16), "side_sum", (second_keep, second_back)
    )
    near_back = swap(second_sum, near)
    own, send = in_vmem(
        fold_kernel,
        [vmem(two[1:], jnp.float32), vmem(two[1:], jnp.bfloat16)],
        "near_sum",
        (first_keep, first_back, near_back),
    )
    moe_out = in_vmem(
        total_kernel,
        jax.ShapeDtypeStruct((row_count, width), jnp.bfloat16),
        "total",
        (residual, own, swap(send, far)),
    )
    return attended, moe_out


def expert_layer_routed(residual, norm_gain, routes, route_weights, expert_in, expert_down):
    row_count, top_count = routes.shape
    expert_count = expert_in.shape[0] * lax.axis_size("ep")
    capacity = min(row_count, max(2, 2 * row_count * top_count // expert_count))
    whole = lax.all_gather(residual, "tp", axis=1, tiled=True)
    width = whole.shape[1]
    half_width = residual.shape[1]
    normed = normalize(whole, norm_gain)
    flat_routes = routes.reshape(-1)
    hits = (flat_routes[:, None] == jnp.arange(expert_count)[None, :]).astype(jnp.int32)
    before = jnp.cumsum(hits, axis=0) - hits
    position = jnp.sum(before * hits, axis=1)
    slot_flat = flat_routes * capacity + position
    placed = (slot_flat[:, None] == jnp.arange(expert_count * capacity)[None, :]).astype(
        jnp.float32
    )
    placed = placed.reshape(row_count, top_count, expert_count * capacity)
    selector = jnp.sum(placed, axis=1).astype(jnp.bfloat16)
    buffer = jnp.einsum("rs,rd->sd", selector, normed, preferred_element_type=jnp.float32)
    buffer = buffer.astype(jnp.bfloat16).reshape(expert_count, capacity, width)
    arrived = lax.all_to_all(buffer, "ep", split_axis=0, concat_axis=0, tiled=True)
    sources = arrived.shape[0]
    flat_rows = arrived.reshape(sources * capacity, width)
    gate_act = jnp.dot(flat_rows, expert_in[0, 0], preferred_element_type=jnp.float32)
    up_act = jnp.dot(flat_rows, expert_in[0, 1], preferred_element_type=jnp.float32)
    hidden = (jax.nn.silu(gate_act) * up_act).astype(jnp.bfloat16)
    partial_value = jnp.dot(hidden, expert_down[0], preferred_element_type=jnp.float32)
    partial_value = partial_value.reshape(sources, capacity, width)
    summed = lax.psum_scatter(partial_value, "tp", scatter_dimension=2, tiled=True).astype(
        jnp.bfloat16
    )
    returned = lax.all_to_all(summed, "ep", split_axis=0, concat_axis=0, tiled=True)
    weighting = jnp.sum(placed * route_weights[:, :, None], axis=1)
    gathered_rows = returned.reshape(expert_count * capacity, half_width).astype(jnp.float32)
    combined = jnp.dot(weighting, gathered_rows, precision=lax.Precision.HIGHEST)
    return (residual.astype(jnp.float32) + combined).astype(jnp.bfloat16)


def per_device(
    queries,
    key_cache,
    value_cache,
    new_key,
    new_value,
    lengths,
    residual,
    norm_gain,
    routes,
    route_weights,
    expert_in,
    expert_down,
):
    devices = lax.axis_size("ep")
    dense = lax.axis_size("tp") == 1 and devices == 16
    attention = (queries, key_cache, value_cache, new_key, new_value, lengths)
    layer = (residual, norm_gain, routes, route_weights)
    if dense:
        return layer_gathered(attention, *layer, expert_in, expert_down)
    attended = attention_block(*attention)
    return (attended, expert_layer_routed(*layer, expert_in, expert_down))


def solution(mesh):
    in_specs = (
        P(("groups", "ep"), "tp", None),
        P(("groups", "ep"), None, "tp", None),
        P(("groups", "ep"), None, "tp", None),
        P(("groups", "ep"), "tp", None),
        P(("groups", "ep"), "tp", None),
        P(("groups", "ep")),
        P(("groups", "ep"), "tp"),
        P(),
        P(("groups", "ep"), None),
        P(("groups", "ep"), None),
        P("ep", None, None, "tp"),
        P("ep", "tp", None),
    )
    out_specs = (P(("groups", "ep"), "tp", None), P(("groups", "ep"), "tp"))
    return jax.shard_map(
        per_device, mesh=mesh, in_specs=in_specs, out_specs=out_specs, check_vma=False
    )
```

```python
import functools

import jax
import jax.numpy as jnp
from jax import lax
from jax.experimental import pallas as pl
from jax.experimental.pallas import tpu as pltpu
from jax.sharding import PartitionSpec as P


def attention_block(queries, key_cache, value_cache, new_key, new_value, lengths):
    rows_here, heads_here, head_size = queries.shape
    kv_here = key_cache.shape[2]
    slots_here = key_cache.shape[1]
    group = heads_here // kv_here
    scale = 1.0 / head_size**0.5
    grouped = queries.reshape(rows_here, kv_here, group, head_size)
    scores = (
        jnp.einsum("akgd,ackd->akgc", grouped, key_cache, preferred_element_type=jnp.float32)
        * scale
    )
    valid = (jnp.arange(slots_here)[None, :] < lengths[:, None])[:, None, None, :]
    scores = jnp.where(valid, scores, -1e30)
    own_score = (
        jnp.einsum("akgd,akd->akg", grouped, new_key, preferred_element_type=jnp.float32) * scale
    )
    largest = jnp.maximum(jnp.max(scores, axis=-1), own_score)
    cache_exp = jnp.exp(scores - largest[..., None])
    own_exp = jnp.exp(own_score - largest)
    total = jnp.sum(cache_exp, axis=-1) + own_exp
    cache_probs = (cache_exp / total[..., None]).astype(jnp.bfloat16)
    own_probs = (own_exp / total).astype(jnp.bfloat16)
    mixed = jnp.einsum(
        "akgc,ackd->akgd", cache_probs, value_cache, preferred_element_type=jnp.float32
    )
    mixed = (
        mixed
        + own_probs.astype(jnp.float32)[..., None] * new_value.astype(jnp.float32)[:, :, None, :]
    )
    return mixed.reshape(rows_here, heads_here, head_size).astype(jnp.bfloat16)


def normalize(residual, norm_gain):
    wide = residual.astype(jnp.float32)
    return (
        wide * lax.rsqrt(jnp.mean(wide * wide, axis=1, keepdims=True) + 1e-06) * norm_gain
    ).astype(jnp.bfloat16)


def load(sources, targets, sems):
    copies = [
        pltpu.make_async_copy(source, target, sems.at[i])
        for i, (source, target) in enumerate(zip(sources, targets))
    ]
    for copy in copies:
        copy.start()
    return copies


def stay(array):
    return pltpu.with_memory_space_constraint(array, pltpu.HBM)


HERE = pl.BlockSpec(memory_space=pltpu.VMEM)
ANYWHERE = pl.BlockSpec(memory_space=pl.ANY)


def params(mebibytes=4):
    return pltpu.CompilerParams(vmem_limit_bytes=mebibytes * 1024 * 1024)


def cost(flops=0, bytes_accessed=0):
    return pl.CostEstimate(flops=flops, bytes_accessed=bytes_accessed, transcendentals=0)


def from_hbm(kernel, out_shape, name, arrays, after=(), cost_estimate=None):
    return pl.pallas_call(
        kernel,
        out_shape=out_shape,
        in_specs=[pl.BlockSpec(memory_space=pltpu.HBM)] * len(arrays) + [ANYWHERE] * len(after),
        scratch_shapes=[
            (pltpu.VMEM if array.ndim > 1 else pltpu.SMEM)(array.shape, array.dtype)
            for array in arrays
        ]
        + [pltpu.SemaphoreType.DMA((len(arrays),))],
        compiler_params=params(),
        cost_estimate=cost_estimate,
        name=name,
    )(*(stay(array) for array in arrays), *after)


def attend_kernel(*refs):
    attended_ref = refs[-8]
    lengths_ref, queries_ref, keys_ref, values_ref, new_keys_ref, new_values_ref = refs[-7:-1]
    copies = load(refs[:6], refs[-7:-1], refs[-1])
    row_count, heads, head_size = queries_ref.shape
    kv_heads = new_keys_ref.shape[0] // row_count
    group = heads // kv_heads
    scale = 1.0 / head_size**0.5
    across = (((1,), (1,)), ((), ()))

    def grids(columns):
        shape = (heads, columns)
        head = lax.broadcasted_iota(jnp.int32, shape, 0) // group
        return head, lax.broadcasted_iota(jnp.int32, shape, 1)

    head, column = grids(keys_ref.shape[1])
    own_head, own_column = grids(new_keys_ref.shape[0])
    same_head = column % kv_heads == head
    slot = column // kv_heads
    for copy in copies:
        copy.wait()
    for a in range(row_count):
        query = queries_ref[a]
        scores = lax.dot_general(query, keys_ref[a], across, preferred_element_type=jnp.float32)
        scores = jnp.where(same_head & (slot < lengths_ref[a]), scores * scale, -1e30)
        own = lax.dot_general(
            query, new_keys_ref[...], across, preferred_element_type=jnp.float32
        )
        own = jnp.where(own_column == own_head + a * kv_heads, own * scale, -1e30)
        largest = jnp.maximum(
            jnp.max(scores, axis=1, keepdims=True), jnp.max(own, axis=1, keepdims=True)
        )
        scores = jnp.exp(scores - largest)
        own = jnp.exp(own - largest)
        total = jnp.sum(scores, axis=1, keepdims=True) + jnp.sum(own, axis=1, keepdims=True)
        mixed = jnp.dot(
            (scores / total).astype(jnp.bfloat16),
            values_ref[a],
            preferred_element_type=jnp.float32,
        ) + jnp.dot(
            (own / total).astype(jnp.bfloat16),
            new_values_ref[...],
            preferred_element_type=jnp.float32,
        )
        attended_ref[a] = mixed.astype(jnp.bfloat16)


def attend(queries, key_cache, value_cache, new_key, new_value, lengths, after):
    rows_here, slots_here, kv_here, head_size = key_cache.shape
    lines = (rows_here, slots_here * kv_here, head_size)
    arrays = (
        lengths,
        queries,
        key_cache.reshape(lines),
        value_cache.reshape(lines),
        new_key.reshape(-1, head_size),
        new_value.reshape(-1, head_size),
    )
    out_shape = jax.ShapeDtypeStruct(queries.shape, jnp.bfloat16)
    work = cost(0, 16 * key_cache.size * key_cache.dtype.itemsize)
    return from_hbm(attend_kernel, out_shape, "attend", arrays, after, work)


def hold_kernel(count, pieces, *refs):
    sources, targets, sems = refs[:count], refs[-1 - count : -1], refs[-1]
    starts, ends = [], []
    for source, target in zip(sources, targets):
        lines = source.shape[0] // pieces
        for i in range(pieces):
            starts.append(source.at[pl.ds(i * lines, lines)])
            ends.append(target.at[pl.ds(i * lines, lines)])
    for copy in load(starts, ends, sems):
        copy.wait()


def hold(arrays, after, pieces=4):
    flat = [array.reshape(-1, array.shape[-1]) for array in arrays]
    size = sum(array.size for array in flat)
    return pl.pallas_call(
        functools.partial(hold_kernel, len(flat), pieces),
        out_shape=[pltpu.VMEM(array.shape, array.dtype) for array in flat],
        in_specs=[pl.BlockSpec(memory_space=pltpu.HBM)] * len(flat) + [ANYWHERE] * len(after),
        scratch_shapes=[pltpu.SemaphoreType.DMA((pieces * len(flat),))],
        cost_estimate=cost(0, 2 * size),
        compiler_params=params(),
        name="hold",
    )(*(stay(array) for array in flat), *after)


def prepare_kernel(*refs):
    packed_ref, residual_ref, gain_ref, routes_ref, weights_ref, sems = refs[4:]
    for copy in load(refs[:4], refs[5:9], sems):
        copy.wait()
    row_count, width = residual_ref.shape
    experts = lax.axis_size("ep")
    lanes = packed_ref.shape[1] - width
    wide = residual_ref[...].astype(jnp.float32)
    mean = jnp.mean(wide * wide, axis=1, keepdims=True)
    packed_ref[:, :width] = (wide * lax.rsqrt(mean + 1e-06) * gain_ref[...]).astype(jnp.bfloat16)
    line = lax.broadcasted_iota(jnp.int32, (lanes, row_count), 0)
    expert = lax.rem(line, experts)
    weight = jnp.zeros(line.shape, jnp.float32)
    for k in range(routes_ref.shape[0]):
        weight += jnp.where(routes_ref[k : k + 1, :] == expert, weights_ref[k : k + 1, :], 0.0)
    high = weight.astype(jnp.bfloat16).astype(jnp.float32)
    low = (weight - high).astype(jnp.bfloat16).astype(jnp.float32)
    lowest = weight - high - low
    terms = jnp.where(
        line < experts,
        high,
        jnp.where(line < 2 * experts, low, jnp.where(line < 3 * experts, lowest, 0.0)),
    )
    at = lax.broadcasted_iota(jnp.int32, (row_count, row_count), 0)
    same = at == lax.broadcasted_iota(jnp.int32, (row_count, row_count), 1)
    turned = lax.dot_general(
        same.astype(jnp.bfloat16),
        terms.astype(jnp.bfloat16),
        (((1,), (1,)), ((), ())),
        preferred_element_type=jnp.float32,
    )
    packed_ref[:, width:] = turned.astype(jnp.bfloat16)


def stack_kernel(*refs):
    for i in range(refs[-1].shape[0]):
        refs[-1][i] = refs[i][...]


def ffn_kernel(block_count, *refs):
    blocks = refs[:block_count]
    in_ref, down_ref = refs[block_count : block_count + 2]
    near_ref, far_ref = refs[-2:]
    width = down_ref.shape[1]
    packed = jnp.concatenate(
        [block[...].reshape(-1, block.shape[-1]) for block in blocks], axis=0
    )
    rows = packed[:, :width]
    terms = packed[:, width:].astype(jnp.float32)
    lane = lax.broadcasted_iota(jnp.int32, terms.shape, 1)
    mine = lax.rem(lane, lax.axis_size("ep")) == lax.axis_index("ep")
    weight = jnp.sum(jnp.where(mine, terms, 0.0), axis=1, keepdims=True)
    gate = jnp.dot(rows, in_ref[:width], preferred_element_type=jnp.float32)
    up = jnp.dot(rows, in_ref[width:], preferred_element_type=jnp.float32)
    hidden = (gate / (1.0 + jnp.exp(-gate)) * up).astype(jnp.bfloat16)
    out = jnp.dot(hidden, down_ref[...], preferred_element_type=jnp.float32)
    out = (out * weight).astype(jnp.bfloat16).reshape((2,) + near_ref.shape)
    near_ref[...] = out[0]
    far_ref[...] = out[1]


def pair_kernel(own_ref, other_ref, keep_ref, send_ref):
    half = keep_ref.shape[0]
    keep_ref[...] = own_ref[:half].astype(jnp.float32) + other_ref[:half].astype(jnp.float32)
    send = own_ref[half:].astype(jnp.float32) + other_ref[half:].astype(jnp.float32)
    send_ref[...] = send.astype(jnp.bfloat16)


def square_kernel(own_ref, other_ref, *out_refs):
    for i, out_ref in enumerate(out_refs):
        total = own_ref[i] + other_ref[i].astype(jnp.float32)
        out_ref[...] = total.astype(out_ref.dtype)


def total_kernel(residual_ref, *refs):
    total = residual_ref[...].astype(jnp.float32)
    for ref in refs[:-1]:
        total += ref[...].astype(jnp.float32)
    refs[-1][...] = total.astype(jnp.bfloat16)


def in_vmem(kernel, out_shape, name, arrays, after=(), mebibytes=4, cost_estimate=None):
    return pl.pallas_call(
        kernel,
        out_shape=out_shape,
        in_specs=[HERE] * len(arrays) + [ANYWHERE] * len(after),
        compiler_params=params(mebibytes),
        cost_estimate=cost_estimate,
        name=name,
    )(*arrays, *after)


def layer_gathered(attention, residual, norm_gain, routes, route_weights, expert_in, expert_down):
    row_count, width = residual.shape
    devices = lax.axis_size("ep")
    core, side, line = 1, 2, 4
    extra = -(-3 * devices // 128) * 128
    vmem = pltpu.VMEM
    one = (row_count, width)
    block = vmem((row_count, width + extra), jnp.bfloat16)

    def swap(value, bits):
        return lax.ppermute(value, "ep", [(i, i ^ bits) for i in range(devices)])

    def stack(members, after=()):
        shape = vmem((len(members), row_count, width + extra), jnp.bfloat16)
        return in_vmem(stack_kernel, shape, "stack", members, after)

    packed = from_hbm(
        prepare_kernel,
        block,
        "prepare",
        (residual, norm_gain.reshape(1, -1), routes.T, route_weights.T),
    )
    first, third, second = (swap(packed, d * line) for d in (1, 3, 2))
    across = swap(packed, side)
    held = hold((expert_in, expert_down), (packed,))

    diagonal = swap(across, line)
    early = stack((second, third), (diagonal, held[0]))
    early_side = swap(early, side)
    early_far = swap(early, core)
    late = stack((packed, across, first, diagonal), (early,))
    late_far = swap(late, core)
    early_side_far = swap(early_side, core)

    def ffn(members, after=()):
        return in_vmem(
            functools.partial(ffn_kernel, len(members)),
            [vmem((4,) + one, jnp.bfloat16)] * 2,
            "ffn",
            (*members, *held),
            after,
            mebibytes=16,
            cost_estimate=cost(8 * row_count * 2 * sum(h.size for h in held), 2 * held[0].size),
        )

    def pair_sum(near_out, far_out):
        shapes = [vmem((2,) + one, jnp.float32), vmem((2,) + one, jnp.bfloat16)]
        return in_vmem(pair_kernel, shapes, "pair_sum", (near_out, swap(far_out, core)))

    early_members = (early, early_side, early_far, early_side_far)
    early_keep, early_send = pair_sum(*ffn(early_members, (late_far,)))
    early_sums = in_vmem(
        square_kernel,
        [vmem(one, jnp.bfloat16)] * 2,
        "square_sum",
        (early_keep, swap(early_send, side)),
    )
    back = [swap(early_sums[1], 3 * line), swap(early_sums[0], 2 * line)]
    attended = attend(*attention, tuple(early_sums))
    late_keep, late_send = pair_sum(*ffn((late, late_far)))
    own, across_sum = in_vmem(
        square_kernel,
        [vmem(one, jnp.float32), vmem(one, jnp.bfloat16)],
        "line_sum",
        (late_keep, swap(late_send, line)),
    )
    moe_out = in_vmem(
        total_kernel,
        jax.ShapeDtypeStruct(one, jnp.bfloat16),
        "total",
        (residual, own, *back, swap(across_sum, side)),
    )
    return attended, moe_out


def expert_layer_routed(residual, norm_gain, routes, route_weights, expert_in, expert_down):
    row_count, top_count = routes.shape
    expert_count = expert_in.shape[0] * lax.axis_size("ep")
    capacity = min(row_count, max(2, 2 * row_count * top_count // expert_count))
    whole = lax.all_gather(residual, "tp", axis=1, tiled=True)
    width = whole.shape[1]
    half_width = residual.shape[1]
    normed = normalize(whole, norm_gain)
    flat_routes = routes.reshape(-1)
    hits = (flat_routes[:, None] == jnp.arange(expert_count)[None, :]).astype(jnp.int32)
    before = jnp.cumsum(hits, axis=0) - hits
    position = jnp.sum(before * hits, axis=1)
    slot_flat = flat_routes * capacity + position
    placed = (slot_flat[:, None] == jnp.arange(expert_count * capacity)[None, :]).astype(
        jnp.float32
    )
    placed = placed.reshape(row_count, top_count, expert_count * capacity)
    selector = jnp.sum(placed, axis=1).astype(jnp.bfloat16)
    buffer = jnp.einsum("rs,rd->sd", selector, normed, preferred_element_type=jnp.float32)
    buffer = buffer.astype(jnp.bfloat16).reshape(expert_count, capacity, width)
    arrived = lax.all_to_all(buffer, "ep", split_axis=0, concat_axis=0, tiled=True)
    sources = arrived.shape[0]
    flat_rows = arrived.reshape(sources * capacity, width)
    gate_act = jnp.dot(flat_rows, expert_in[0, 0], preferred_element_type=jnp.float32)
    up_act = jnp.dot(flat_rows, expert_in[0, 1], preferred_element_type=jnp.float32)
    hidden = (jax.nn.silu(gate_act) * up_act).astype(jnp.bfloat16)
    partial_value = jnp.dot(hidden, expert_down[0], preferred_element_type=jnp.float32)
    partial_value = partial_value.reshape(sources, capacity, width)
    summed = lax.psum_scatter(partial_value, "tp", scatter_dimension=2, tiled=True).astype(
        jnp.bfloat16
    )
    returned = lax.all_to_all(summed, "ep", split_axis=0, concat_axis=0, tiled=True)
    weighting = jnp.sum(placed * route_weights[:, :, None], axis=1)
    gathered_rows = returned.reshape(expert_count * capacity, half_width).astype(jnp.float32)
    combined = jnp.dot(weighting, gathered_rows, precision=lax.Precision.HIGHEST)
    return (residual.astype(jnp.float32) + combined).astype(jnp.bfloat16)


def per_device(
    queries,
    key_cache,
    value_cache,
    new_key,
    new_value,
    lengths,
    residual,
    norm_gain,
    routes,
    route_weights,
    expert_in,
    expert_down,
):
    devices = lax.axis_size("ep")
    dense = lax.axis_size("tp") == 1 and devices == 16
    attention = (queries, key_cache, value_cache, new_key, new_value, lengths)
    layer = (residual, norm_gain, routes, route_weights)
    if dense:
        return layer_gathered(attention, *layer, expert_in, expert_down)
    attended = attention_block(*attention)
    return (attended, expert_layer_routed(*layer, expert_in, expert_down))


def solution(mesh):
    in_specs = (
        P(("groups", "ep"), "tp", None),
        P(("groups", "ep"), None, "tp", None),
        P(("groups", "ep"), None, "tp", None),
        P(("groups", "ep"), "tp", None),
        P(("groups", "ep"), "tp", None),
        P(("groups", "ep")),
        P(("groups", "ep"), "tp"),
        P(),
        P(("groups", "ep"), None),
        P(("groups", "ep"), None),
        P("ep", None, None, "tp"),
        P("ep", "tp", None),
    )
    out_specs = (P(("groups", "ep"), "tp", None), P(("groups", "ep"), "tp"))
    return jax.shard_map(
        per_device, mesh=mesh, in_specs=in_specs, out_specs=out_specs, check_vma=False
    )
```

```python
import functools

import jax
import jax.numpy as jnp
from jax import lax
from jax.experimental import pallas as pl
from jax.experimental.pallas import tpu as pltpu
from jax.sharding import PartitionSpec as P


def attention_block(queries, key_cache, value_cache, new_key, new_value, lengths):
    rows_here, heads_here, head_size = queries.shape
    kv_here = key_cache.shape[2]
    slots_here = key_cache.shape[1]
    group = heads_here // kv_here
    scale = 1.0 / head_size**0.5
    grouped = queries.reshape(rows_here, kv_here, group, head_size)
    scores = (
        jnp.einsum("akgd,ackd->akgc", grouped, key_cache, preferred_element_type=jnp.float32)
        * scale
    )
    valid = (jnp.arange(slots_here)[None, :] < lengths[:, None])[:, None, None, :]
    scores = jnp.where(valid, scores, -1e30)
    own_score = (
        jnp.einsum("akgd,akd->akg", grouped, new_key, preferred_element_type=jnp.float32) * scale
    )
    largest = jnp.maximum(jnp.max(scores, axis=-1), own_score)
    cache_exp = jnp.exp(scores - largest[..., None])
    own_exp = jnp.exp(own_score - largest)
    total = jnp.sum(cache_exp, axis=-1) + own_exp
    cache_probs = (cache_exp / total[..., None]).astype(jnp.bfloat16)
    own_probs = (own_exp / total).astype(jnp.bfloat16)
    mixed = jnp.einsum(
        "akgc,ackd->akgd", cache_probs, value_cache, preferred_element_type=jnp.float32
    )
    mixed = (
        mixed
        + own_probs.astype(jnp.float32)[..., None] * new_value.astype(jnp.float32)[:, :, None, :]
    )
    return mixed.reshape(rows_here, heads_here, head_size).astype(jnp.bfloat16)


def normalize(residual, norm_gain):
    wide = residual.astype(jnp.float32)
    return (
        wide * lax.rsqrt(jnp.mean(wide * wide, axis=1, keepdims=True) + 1e-06) * norm_gain
    ).astype(jnp.bfloat16)


def load(sources, targets, sems):
    copies = [
        pltpu.make_async_copy(source, target, sems.at[i])
        for i, (source, target) in enumerate(zip(sources, targets))
    ]
    for copy in copies:
        copy.start()
    return copies


def stay(array):
    return pltpu.with_memory_space_constraint(array, pltpu.HBM)


HERE = pl.BlockSpec(memory_space=pltpu.VMEM)
ANYWHERE = pl.BlockSpec(memory_space=pl.ANY)


def params(mebibytes=4):
    return pltpu.CompilerParams(vmem_limit_bytes=mebibytes * 1024 * 1024)


def cost(flops=0, bytes_accessed=0):
    return pl.CostEstimate(flops=flops, bytes_accessed=bytes_accessed, transcendentals=0)


def from_hbm(kernel, out_shape, name, arrays, after=(), cost_estimate=None):
    return pl.pallas_call(
        kernel,
        out_shape=out_shape,
        in_specs=[pl.BlockSpec(memory_space=pltpu.HBM)] * len(arrays) + [ANYWHERE] * len(after),
        scratch_shapes=[
            (pltpu.VMEM if array.ndim > 1 else pltpu.SMEM)(array.shape, array.dtype)
            for array in arrays
        ]
        + [pltpu.SemaphoreType.DMA((len(arrays),))],
        compiler_params=params(),
        cost_estimate=cost_estimate,
        name=name,
    )(*(stay(array) for array in arrays), *after)


def attend_kernel(*refs):
    attended_ref = refs[-8]
    lengths_ref, queries_ref, keys_ref, values_ref, new_keys_ref, new_values_ref = refs[-7:-1]
    copies = load(refs[:6], refs[-7:-1], refs[-1])
    row_count, heads, head_size = queries_ref.shape
    kv_heads = new_keys_ref.shape[0] // row_count
    group = heads // kv_heads
    scale = 1.0 / head_size**0.5
    across = (((1,), (1,)), ((), ()))

    def grids(columns):
        shape = (heads, columns)
        head = lax.broadcasted_iota(jnp.int32, shape, 0) // group
        return head, lax.broadcasted_iota(jnp.int32, shape, 1)

    head, column = grids(keys_ref.shape[1])
    own_head, own_column = grids(new_keys_ref.shape[0])
    same_head = column % kv_heads == head
    slot = column // kv_heads
    for copy in copies:
        copy.wait()
    for a in range(row_count):
        query = queries_ref[a]
        scores = lax.dot_general(query, keys_ref[a], across, preferred_element_type=jnp.float32)
        scores = jnp.where(same_head & (slot < lengths_ref[a]), scores * scale, -1e30)
        own = lax.dot_general(
            query, new_keys_ref[...], across, preferred_element_type=jnp.float32
        )
        own = jnp.where(own_column == own_head + a * kv_heads, own * scale, -1e30)
        largest = jnp.maximum(
            jnp.max(scores, axis=1, keepdims=True), jnp.max(own, axis=1, keepdims=True)
        )
        scores = jnp.exp(scores - largest)
        own = jnp.exp(own - largest)
        total = jnp.sum(scores, axis=1, keepdims=True) + jnp.sum(own, axis=1, keepdims=True)
        mixed = jnp.dot(
            (scores / total).astype(jnp.bfloat16),
            values_ref[a],
            preferred_element_type=jnp.float32,
        ) + jnp.dot(
            (own / total).astype(jnp.bfloat16),
            new_values_ref[...],
            preferred_element_type=jnp.float32,
        )
        attended_ref[a] = mixed.astype(jnp.bfloat16)


def attend(queries, key_cache, value_cache, new_key, new_value, lengths, after):
    rows_here, slots_here, kv_here, head_size = key_cache.shape
    lines = (rows_here, slots_here * kv_here, head_size)
    arrays = (
        lengths,
        queries,
        key_cache.reshape(lines),
        value_cache.reshape(lines),
        new_key.reshape(-1, head_size),
        new_value.reshape(-1, head_size),
    )
    out_shape = jax.ShapeDtypeStruct(queries.shape, jnp.bfloat16)
    work = cost(0, 16 * key_cache.size * key_cache.dtype.itemsize)
    return from_hbm(attend_kernel, out_shape, "attend", arrays, after, work)


def hold_kernel(count, pieces, *refs):
    sources, targets, sems = refs[:count], refs[-1 - count : -1], refs[-1]
    starts, ends = [], []
    for source, target in zip(sources, targets):
        lines = source.shape[0] // pieces
        for i in range(pieces):
            starts.append(source.at[pl.ds(i * lines, lines)])
            ends.append(target.at[pl.ds(i * lines, lines)])
    for copy in load(starts, ends, sems):
        copy.wait()


def hold(arrays, after, pieces=4):
    flat = [array.reshape(-1, array.shape[-1]) for array in arrays]
    size = sum(array.size for array in flat)
    return pl.pallas_call(
        functools.partial(hold_kernel, len(flat), pieces),
        out_shape=[pltpu.VMEM(array.shape, array.dtype) for array in flat],
        in_specs=[pl.BlockSpec(memory_space=pltpu.HBM)] * len(flat) + [ANYWHERE] * len(after),
        scratch_shapes=[pltpu.SemaphoreType.DMA((pieces * len(flat),))],
        cost_estimate=cost(0, 2 * size),
        compiler_params=params(),
        name="hold",
    )(*(stay(array) for array in flat), *after)


def prepare_kernel(*refs):
    packed_ref, residual_ref, gain_ref, routes_ref, weights_ref, sems = refs[4:]
    for copy in load(refs[:4], refs[5:9], sems):
        copy.wait()
    row_count, width = residual_ref.shape
    experts = lax.axis_size("ep")
    lanes = packed_ref.shape[1] - width
    wide = residual_ref[...].astype(jnp.float32)
    mean = jnp.mean(wide * wide, axis=1, keepdims=True)
    packed_ref[:, :width] = (wide * lax.rsqrt(mean + 1e-06) * gain_ref[...]).astype(jnp.bfloat16)
    line = lax.broadcasted_iota(jnp.int32, (lanes, row_count), 0)
    expert = lax.rem(line, experts)
    weight = jnp.zeros(line.shape, jnp.float32)
    for k in range(routes_ref.shape[0]):
        weight += jnp.where(routes_ref[k : k + 1, :] == expert, weights_ref[k : k + 1, :], 0.0)
    high = weight.astype(jnp.bfloat16).astype(jnp.float32)
    low = (weight - high).astype(jnp.bfloat16).astype(jnp.float32)
    lowest = weight - high - low
    terms = jnp.where(
        line < experts,
        high,
        jnp.where(line < 2 * experts, low, jnp.where(line < 3 * experts, lowest, 0.0)),
    )
    at = lax.broadcasted_iota(jnp.int32, (row_count, row_count), 0)
    same = at == lax.broadcasted_iota(jnp.int32, (row_count, row_count), 1)
    turned = lax.dot_general(
        same.astype(jnp.bfloat16),
        terms.astype(jnp.bfloat16),
        (((1,), (1,)), ((), ())),
        preferred_element_type=jnp.float32,
    )
    packed_ref[:, width:] = turned.astype(jnp.bfloat16)


def stack_kernel(*refs):
    for i in range(refs[-1].shape[0]):
        refs[-1][i] = refs[i][...]


def relay_kernel(in_ref, *refs):
    refs[-1][...] = in_ref[...]


def ffn_kernel(block_count, *refs):
    blocks = refs[:block_count]
    in_ref, down_ref = refs[block_count : block_count + 2]
    near_ref, far_ref = refs[-2:]
    width = down_ref.shape[1]
    packed = jnp.concatenate(
        [block[...].reshape(-1, block.shape[-1]) for block in blocks], axis=0
    )
    rows = packed[:, :width]
    terms = packed[:, width:].astype(jnp.float32)
    lane = lax.broadcasted_iota(jnp.int32, terms.shape, 1)
    mine = lax.rem(lane, lax.axis_size("ep")) == lax.axis_index("ep")
    weight = jnp.sum(jnp.where(mine, terms, 0.0), axis=1, keepdims=True)
    gate = jnp.dot(rows, in_ref[:width], preferred_element_type=jnp.float32)
    up = jnp.dot(rows, in_ref[width:], preferred_element_type=jnp.float32)
    hidden = (gate / (1.0 + jnp.exp(-gate)) * up).astype(jnp.bfloat16)
    out = jnp.dot(hidden, down_ref[...], preferred_element_type=jnp.float32)
    out = (out * weight).astype(jnp.bfloat16).reshape((2,) + near_ref.shape)
    near_ref[...] = out[0]
    far_ref[...] = out[1]


def pair_kernel(own_ref, other_ref, keep_ref, send_ref):
    half = keep_ref.shape[0]
    keep_ref[...] = own_ref[:half].astype(jnp.float32) + other_ref[:half].astype(jnp.float32)
    send = own_ref[half:].astype(jnp.float32) + other_ref[half:].astype(jnp.float32)
    send_ref[...] = send.astype(jnp.bfloat16)


def square_kernel(own_ref, other_ref, *out_refs):
    for i, out_ref in enumerate(out_refs):
        total = own_ref[i] + other_ref[i].astype(jnp.float32)
        out_ref[...] = total.astype(out_ref.dtype)


def total_kernel(residual_ref, *refs):
    total = residual_ref[...].astype(jnp.float32)
    for ref in refs[:-1]:
        total += ref[...].astype(jnp.float32)
    refs[-1][...] = total.astype(jnp.bfloat16)


def in_vmem(kernel, out_shape, name, arrays, after=(), mebibytes=4, cost_estimate=None):
    return pl.pallas_call(
        kernel,
        out_shape=out_shape,
        in_specs=[HERE] * len(arrays) + [ANYWHERE] * len(after),
        compiler_params=params(mebibytes),
        cost_estimate=cost_estimate,
        name=name,
    )(*arrays, *after)


def layer_gathered(attention, residual, norm_gain, routes, route_weights, expert_in, expert_down):
    row_count, width = residual.shape
    devices = lax.axis_size("ep")
    core, side, line = 1, 2, 4
    extra = -(-3 * devices // 128) * 128
    vmem = pltpu.VMEM
    one = (row_count, width)
    block = vmem((row_count, width + extra), jnp.bfloat16)

    def swap(value, bits):
        return lax.ppermute(value, "ep", [(i, i ^ bits) for i in range(devices)])

    def stack(members, after=()):
        shape = vmem((len(members), row_count, width + extra), jnp.bfloat16)
        return in_vmem(stack_kernel, shape, "stack", members, after)

    packed = from_hbm(
        prepare_kernel,
        block,
        "prepare",
        (residual, norm_gain.reshape(1, -1), routes.T, route_weights.T),
    )
    first, third, second = (swap(packed, d * line) for d in (1, 3, 2))
    across = swap(packed, side)
    diagonal = swap(across, line)
    early = stack((second, third), (diagonal,))
    held = hold((expert_in, expert_down), (early,))
    early_side = swap(early, side)
    early_far = swap(early, core)
    late = stack((packed, across, first, diagonal), (early,))
    late_far = swap(late, core)
    shape = vmem(early.shape, early.dtype)
    relayed = in_vmem(relay_kernel, shape, "relay", (early_side,), held[:1])
    early_side_far = swap(relayed, core)

    def ffn(members, after=()):
        return in_vmem(
            functools.partial(ffn_kernel, len(members)),
            [vmem((4,) + one, jnp.bfloat16)] * 2,
            "ffn",
            (*members, *held),
            after,
            mebibytes=16,
            cost_estimate=cost(8 * row_count * 2 * sum(h.size for h in held), 2 * held[0].size),
        )

    def pair_sum(near_out, far_out):
        shapes = [vmem((2,) + one, jnp.float32), vmem((2,) + one, jnp.bfloat16)]
        return in_vmem(pair_kernel, shapes, "pair_sum", (near_out, swap(far_out, core)))

    early_members = (early, early_side, early_far, early_side_far)
    early_keep, early_send = pair_sum(*ffn(early_members, (late_far,)))
    early_sums = in_vmem(
        square_kernel,
        [vmem(one, jnp.bfloat16)] * 2,
        "square_sum",
        (early_keep, swap(early_send, side)),
    )
    back = [swap(early_sums[1], 3 * line), swap(early_sums[0], 2 * line)]
    attended = attend(*attention, tuple(early_sums))
    late_keep, late_send = pair_sum(*ffn((late, late_far)))
    own, across_sum = in_vmem(
        square_kernel,
        [vmem(one, jnp.float32), vmem(one, jnp.bfloat16)],
        "line_sum",
        (late_keep, swap(late_send, line)),
    )
    moe_out = in_vmem(
        total_kernel,
        jax.ShapeDtypeStruct(one, jnp.bfloat16),
        "total",
        (residual, own, *back, swap(across_sum, side)),
    )
    return attended, moe_out


def expert_layer_routed(residual, norm_gain, routes, route_weights, expert_in, expert_down):
    row_count, top_count = routes.shape
    expert_count = expert_in.shape[0] * lax.axis_size("ep")
    capacity = min(row_count, max(2, 2 * row_count * top_count // expert_count))
    whole = lax.all_gather(residual, "tp", axis=1, tiled=True)
    width = whole.shape[1]
    half_width = residual.shape[1]
    normed = normalize(whole, norm_gain)
    flat_routes = routes.reshape(-1)
    hits = (flat_routes[:, None] == jnp.arange(expert_count)[None, :]).astype(jnp.int32)
    before = jnp.cumsum(hits, axis=0) - hits
    position = jnp.sum(before * hits, axis=1)
    slot_flat = flat_routes * capacity + position
    placed = (slot_flat[:, None] == jnp.arange(expert_count * capacity)[None, :]).astype(
        jnp.float32
    )
    placed = placed.reshape(row_count, top_count, expert_count * capacity)
    selector = jnp.sum(placed, axis=1).astype(jnp.bfloat16)
    buffer = jnp.einsum("rs,rd->sd", selector, normed, preferred_element_type=jnp.float32)
    buffer = buffer.astype(jnp.bfloat16).reshape(expert_count, capacity, width)
    arrived = lax.all_to_all(buffer, "ep", split_axis=0, concat_axis=0, tiled=True)
    sources = arrived.shape[0]
    flat_rows = arrived.reshape(sources * capacity, width)
    gate_act = jnp.dot(flat_rows, expert_in[0, 0], preferred_element_type=jnp.float32)
    up_act = jnp.dot(flat_rows, expert_in[0, 1], preferred_element_type=jnp.float32)
    hidden = (jax.nn.silu(gate_act) * up_act).astype(jnp.bfloat16)
    partial_value = jnp.dot(hidden, expert_down[0], preferred_element_type=jnp.float32)
    partial_value = partial_value.reshape(sources, capacity, width)
    summed = lax.psum_scatter(partial_value, "tp", scatter_dimension=2, tiled=True).astype(
        jnp.bfloat16
    )
    returned = lax.all_to_all(summed, "ep", split_axis=0, concat_axis=0, tiled=True)
    weighting = jnp.sum(placed * route_weights[:, :, None], axis=1)
    gathered_rows = returned.reshape(expert_count * capacity, half_width).astype(jnp.float32)
    combined = jnp.dot(weighting, gathered_rows, precision=lax.Precision.HIGHEST)
    return (residual.astype(jnp.float32) + combined).astype(jnp.bfloat16)


def per_device(
    queries,
    key_cache,
    value_cache,
    new_key,
    new_value,
    lengths,
    residual,
    norm_gain,
    routes,
    route_weights,
    expert_in,
    expert_down,
):
    devices = lax.axis_size("ep")
    dense = lax.axis_size("tp") == 1 and devices == 16
    attention = (queries, key_cache, value_cache, new_key, new_value, lengths)
    layer = (residual, norm_gain, routes, route_weights)
    if dense:
        return layer_gathered(attention, *layer, expert_in, expert_down)
    attended = attention_block(*attention)
    return (attended, expert_layer_routed(*layer, expert_in, expert_down))


def solution(mesh):
    in_specs = (
        P(("groups", "ep"), "tp", None),
        P(("groups", "ep"), None, "tp", None),
        P(("groups", "ep"), None, "tp", None),
        P(("groups", "ep"), "tp", None),
        P(("groups", "ep"), "tp", None),
        P(("groups", "ep")),
        P(("groups", "ep"), "tp"),
        P(),
        P(("groups", "ep"), None),
        P(("groups", "ep"), None),
        P("ep", None, None, "tp"),
        P("ep", "tp", None),
    )
    out_specs = (P(("groups", "ep"), "tp", None), P(("groups", "ep"), "tp"))
    return jax.shard_map(
        per_device, mesh=mesh, in_specs=in_specs, out_specs=out_specs, check_vma=False
    )
```

```python
import functools

import jax
import jax.numpy as jnp
from jax import lax
from jax.experimental import pallas as pl
from jax.experimental.pallas import tpu as pltpu
from jax.sharding import PartitionSpec as P


def attention_block(queries, key_cache, value_cache, new_key, new_value, lengths):
    rows_here, heads_here, head_size = queries.shape
    kv_here = key_cache.shape[2]
    slots_here = key_cache.shape[1]
    group = heads_here // kv_here
    scale = 1.0 / head_size**0.5
    grouped = queries.reshape(rows_here, kv_here, group, head_size)
    scores = (
        jnp.einsum("akgd,ackd->akgc", grouped, key_cache, preferred_element_type=jnp.float32)
        * scale
    )
    valid = (jnp.arange(slots_here)[None, :] < lengths[:, None])[:, None, None, :]
    scores = jnp.where(valid, scores, -1e30)
    own_score = (
        jnp.einsum("akgd,akd->akg", grouped, new_key, preferred_element_type=jnp.float32) * scale
    )
    largest = jnp.maximum(jnp.max(scores, axis=-1), own_score)
    cache_exp = jnp.exp(scores - largest[..., None])
    own_exp = jnp.exp(own_score - largest)
    total = jnp.sum(cache_exp, axis=-1) + own_exp
    cache_probs = (cache_exp / total[..., None]).astype(jnp.bfloat16)
    own_probs = (own_exp / total).astype(jnp.bfloat16)
    mixed = jnp.einsum(
        "akgc,ackd->akgd", cache_probs, value_cache, preferred_element_type=jnp.float32
    )
    mixed = (
        mixed
        + own_probs.astype(jnp.float32)[..., None] * new_value.astype(jnp.float32)[:, :, None, :]
    )
    return mixed.reshape(rows_here, heads_here, head_size).astype(jnp.bfloat16)


def normalize(residual, norm_gain):
    wide = residual.astype(jnp.float32)
    return (
        wide * lax.rsqrt(jnp.mean(wide * wide, axis=1, keepdims=True) + 1e-06) * norm_gain
    ).astype(jnp.bfloat16)


def load(sources, targets, sems):
    copies = [
        pltpu.make_async_copy(source, target, sems.at[i])
        for i, (source, target) in enumerate(zip(sources, targets))
    ]
    for copy in copies:
        copy.start()
    return copies


def stay(array):
    return pltpu.with_memory_space_constraint(array, pltpu.HBM)


HERE = pl.BlockSpec(memory_space=pltpu.VMEM)
ANYWHERE = pl.BlockSpec(memory_space=pl.ANY)


def params(mebibytes=4):
    return pltpu.CompilerParams(vmem_limit_bytes=mebibytes * 1024 * 1024)


def cost(flops=0, bytes_accessed=0):
    return pl.CostEstimate(flops=flops, bytes_accessed=bytes_accessed, transcendentals=0)


def from_hbm(kernel, out_shape, name, arrays, after=(), cost_estimate=None):
    return pl.pallas_call(
        kernel,
        out_shape=out_shape,
        in_specs=[pl.BlockSpec(memory_space=pltpu.HBM)] * len(arrays) + [ANYWHERE] * len(after),
        scratch_shapes=[
            (pltpu.VMEM if array.ndim > 1 else pltpu.SMEM)(array.shape, array.dtype)
            for array in arrays
        ]
        + [pltpu.SemaphoreType.DMA((len(arrays),))],
        compiler_params=params(),
        cost_estimate=cost_estimate,
        name=name,
    )(*(stay(array) for array in arrays), *after)


def attend_kernel(*refs):
    attended_ref = refs[-8]
    lengths_ref, queries_ref, keys_ref, values_ref, new_keys_ref, new_values_ref = refs[-7:-1]
    copies = load(refs[:6], refs[-7:-1], refs[-1])
    row_count, heads, head_size = queries_ref.shape
    kv_heads = new_keys_ref.shape[0] // row_count
    group = heads // kv_heads
    scale = 1.0 / head_size**0.5
    across = (((1,), (1,)), ((), ()))

    def grids(columns):
        shape = (heads, columns)
        head = lax.broadcasted_iota(jnp.int32, shape, 0) // group
        return head, lax.broadcasted_iota(jnp.int32, shape, 1)

    head, column = grids(keys_ref.shape[1])
    own_head, own_column = grids(new_keys_ref.shape[0])
    same_head = column % kv_heads == head
    slot = column // kv_heads
    for copy in copies:
        copy.wait()
    for a in range(row_count):
        query = queries_ref[a]
        scores = lax.dot_general(query, keys_ref[a], across, preferred_element_type=jnp.float32)
        scores = jnp.where(same_head & (slot < lengths_ref[a]), scores * scale, -1e30)
        own = lax.dot_general(
            query, new_keys_ref[...], across, preferred_element_type=jnp.float32
        )
        own = jnp.where(own_column == own_head + a * kv_heads, own * scale, -1e30)
        largest = jnp.maximum(
            jnp.max(scores, axis=1, keepdims=True), jnp.max(own, axis=1, keepdims=True)
        )
        scores = jnp.exp(scores - largest)
        own = jnp.exp(own - largest)
        total = jnp.sum(scores, axis=1, keepdims=True) + jnp.sum(own, axis=1, keepdims=True)
        mixed = jnp.dot(
            (scores / total).astype(jnp.bfloat16),
            values_ref[a],
            preferred_element_type=jnp.float32,
        ) + jnp.dot(
            (own / total).astype(jnp.bfloat16),
            new_values_ref[...],
            preferred_element_type=jnp.float32,
        )
        attended_ref[a] = mixed.astype(jnp.bfloat16)


def attend(queries, key_cache, value_cache, new_key, new_value, lengths, after):
    rows_here, slots_here, kv_here, head_size = key_cache.shape
    lines = (rows_here, slots_here * kv_here, head_size)
    arrays = (
        lengths,
        queries,
        key_cache.reshape(lines),
        value_cache.reshape(lines),
        new_key.reshape(-1, head_size),
        new_value.reshape(-1, head_size),
    )
    out_shape = jax.ShapeDtypeStruct(queries.shape, jnp.bfloat16)
    work = cost(0, 16 * key_cache.size * key_cache.dtype.itemsize)
    return from_hbm(attend_kernel, out_shape, "attend", arrays, after, work)


def hold_kernel(count, pieces, *refs):
    sources, targets, sems = refs[:count], refs[-1 - count : -1], refs[-1]
    starts, ends = [], []
    for source, target in zip(sources, targets):
        lines = source.shape[0] // pieces
        for i in range(pieces):
            starts.append(source.at[pl.ds(i * lines, lines)])
            ends.append(target.at[pl.ds(i * lines, lines)])
    for copy in load(starts, ends, sems):
        copy.wait()


def hold(arrays, after, pieces=4):
    flat = [array.reshape(-1, array.shape[-1]) for array in arrays]
    size = sum(array.size for array in flat)
    return pl.pallas_call(
        functools.partial(hold_kernel, len(flat), pieces),
        out_shape=[pltpu.VMEM(array.shape, array.dtype) for array in flat],
        in_specs=[pl.BlockSpec(memory_space=pltpu.HBM)] * len(flat) + [ANYWHERE] * len(after),
        scratch_shapes=[pltpu.SemaphoreType.DMA((pieces * len(flat),))],
        cost_estimate=cost(0, 2 * size),
        compiler_params=params(),
        name="hold",
    )(*(stay(array) for array in flat), *after)


def prepare_kernel(*refs):
    packed_ref, residual_ref, gain_ref, routes_ref, weights_ref, sems = refs[4:]
    for copy in load(refs[:4], refs[5:9], sems):
        copy.wait()
    row_count, width = residual_ref.shape
    experts = lax.axis_size("ep")
    lanes = packed_ref.shape[1] - width
    wide = residual_ref[...].astype(jnp.float32)
    mean = jnp.mean(wide * wide, axis=1, keepdims=True)
    packed_ref[:, :width] = (wide * lax.rsqrt(mean + 1e-06) * gain_ref[...]).astype(jnp.bfloat16)
    line = lax.broadcasted_iota(jnp.int32, (lanes, row_count), 0)
    expert = lax.rem(line, experts)
    weight = jnp.zeros(line.shape, jnp.float32)
    for k in range(routes_ref.shape[0]):
        weight += jnp.where(routes_ref[k : k + 1, :] == expert, weights_ref[k : k + 1, :], 0.0)
    high = weight.astype(jnp.bfloat16).astype(jnp.float32)
    low = (weight - high).astype(jnp.bfloat16).astype(jnp.float32)
    lowest = weight - high - low
    terms = jnp.where(
        line < experts,
        high,
        jnp.where(line < 2 * experts, low, jnp.where(line < 3 * experts, lowest, 0.0)),
    )
    at = lax.broadcasted_iota(jnp.int32, (row_count, row_count), 0)
    same = at == lax.broadcasted_iota(jnp.int32, (row_count, row_count), 1)
    turned = lax.dot_general(
        same.astype(jnp.bfloat16),
        terms.astype(jnp.bfloat16),
        (((1,), (1,)), ((), ())),
        preferred_element_type=jnp.float32,
    )
    packed_ref[:, width:] = turned.astype(jnp.bfloat16)


def stack_kernel(*refs):
    for i in range(refs[-1].shape[0]):
        refs[-1][i] = refs[i][...]


def relay_kernel(in_ref, *refs):
    refs[-1][...] = in_ref[...]


def ffn_kernel(block_count, *refs):
    blocks = refs[:block_count]
    in_ref, down_ref = refs[block_count : block_count + 2]
    near_ref, far_ref = refs[-2:]
    width = down_ref.shape[1]
    packed = jnp.concatenate(
        [block[...].reshape(-1, block.shape[-1]) for block in blocks], axis=0
    )
    rows = packed[:, :width]
    terms = packed[:, width:].astype(jnp.float32)
    lane = lax.broadcasted_iota(jnp.int32, terms.shape, 1)
    mine = lax.rem(lane, lax.axis_size("ep")) == lax.axis_index("ep")
    weight = jnp.sum(jnp.where(mine, terms, 0.0), axis=1, keepdims=True)
    gate = jnp.dot(rows, in_ref[:width], preferred_element_type=jnp.float32)
    up = jnp.dot(rows, in_ref[width:], preferred_element_type=jnp.float32)
    hidden = (gate / (1.0 + jnp.exp(-gate)) * up).astype(jnp.bfloat16)
    out = jnp.dot(hidden, down_ref[...], preferred_element_type=jnp.float32)
    out = (out * weight).astype(jnp.bfloat16).reshape((2,) + near_ref.shape)
    near_ref[...] = out[0]
    far_ref[...] = out[1]


def pair_kernel(own_ref, other_ref, keep_ref, send_ref):
    half = keep_ref.shape[0]
    keep_ref[...] = own_ref[:half].astype(jnp.float32) + other_ref[:half].astype(jnp.float32)
    send = own_ref[half:].astype(jnp.float32) + other_ref[half:].astype(jnp.float32)
    send_ref[...] = send.astype(jnp.bfloat16)


def line_sum_kernel(own_ref, other_ref, *out_refs):
    for i, out_ref in enumerate(out_refs):
        total = own_ref[i] + other_ref[i].astype(jnp.float32)
        out_ref[...] = total.astype(out_ref.dtype)


def square_kernel(own_ref, other_ref, *refs):
    out_ref = refs[-1]
    me = lax.axis_index("ep") // 4
    for i in range(2):
        total = own_ref[i] + other_ref[i].astype(jnp.float32)
        out_ref[me ^ (2 + i)] = total.astype(out_ref.dtype)
        out_ref[me ^ i] = jnp.zeros(out_ref.shape[1:], out_ref.dtype)


def total_kernel(residual_ref, own_ref, across_ref, arrived_ref, out_ref):
    me = lax.axis_index("ep") // 4
    total = residual_ref[...].astype(jnp.float32) + own_ref[...]
    for ref in (across_ref, arrived_ref.at[me ^ 2], arrived_ref.at[me ^ 3]):
        total += ref[...].astype(jnp.float32)
    out_ref[...] = total.astype(jnp.bfloat16)


def in_vmem(kernel, out_shape, name, arrays, after=(), mebibytes=4, cost_estimate=None):
    return pl.pallas_call(
        kernel,
        out_shape=out_shape,
        in_specs=[HERE] * len(arrays) + [ANYWHERE] * len(after),
        compiler_params=params(mebibytes),
        cost_estimate=cost_estimate,
        name=name,
    )(*arrays, *after)


def layer_gathered(attention, residual, norm_gain, routes, route_weights, expert_in, expert_down):
    row_count, width = residual.shape
    devices = lax.axis_size("ep")
    core, side, line = 1, 2, 4
    extra = -(-3 * devices // 128) * 128
    vmem = pltpu.VMEM
    one = (row_count, width)
    block = vmem((row_count, width + extra), jnp.bfloat16)

    def swap(value, bits):
        return lax.ppermute(value, "ep", [(i, i ^ bits) for i in range(devices)])

    def stack(members, after=()):
        shape = vmem((len(members), row_count, width + extra), jnp.bfloat16)
        return in_vmem(stack_kernel, shape, "stack", members, after)

    def exchange(value):
        lines = [[first + line * i for i in range(4)] for first in range(line)]
        return lax.all_to_all(value, "ep", 0, 0, axis_index_groups=lines, tiled=True)

    packed = from_hbm(
        prepare_kernel,
        block,
        "prepare",
        (residual, norm_gain.reshape(1, -1), routes.T, route_weights.T),
    )
    first, third, second = (swap(packed, d * line) for d in (1, 3, 2))
    across = swap(packed, side)
    diagonal = swap(across, line)
    early = stack((second, third), (diagonal,))
    held = hold((expert_in, expert_down), (early,))
    early_side = swap(early, side)
    early_far = swap(early, core)
    late = stack((packed, across, first, diagonal), (early,))
    late_far = swap(late, core)
    shape = vmem(early.shape, early.dtype)
    relayed = in_vmem(relay_kernel, shape, "relay", (early_side,), held[:1])
    early_side_far = swap(relayed, core)

    def ffn(members, after=()):
        return in_vmem(
            functools.partial(ffn_kernel, len(members)),
            [vmem((4,) + one, jnp.bfloat16)] * 2,
            "ffn",
            (*members, *held),
            after,
            mebibytes=16,
            cost_estimate=cost(8 * row_count * 2 * sum(h.size for h in held), 2 * held[0].size),
        )

    def pair_sum(near_out, far_out):
        shapes = [vmem((2,) + one, jnp.float32), vmem((2,) + one, jnp.bfloat16)]
        return in_vmem(pair_kernel, shapes, "pair_sum", (near_out, swap(far_out, core)))

    early_members = (early, early_side, early_far, early_side_far)
    early_keep, early_send = pair_sum(*ffn(early_members, (late_far,)))
    attended = attend(*attention, (early_send,))
    early_sums = in_vmem(
        square_kernel,
        vmem((4,) + one, jnp.bfloat16),
        "square_sum",
        (early_keep, swap(early_send, side)),
        (stay(attended),),
    )
    back = exchange(early_sums)
    late_keep, late_send = pair_sum(*ffn((late, late_far)))
    own, across_sum = in_vmem(
        line_sum_kernel,
        [vmem(one, jnp.float32), vmem(one, jnp.bfloat16)],
        "line_sum",
        (late_keep, swap(late_send, line)),
    )
    moe_out = in_vmem(
        total_kernel,
        jax.ShapeDtypeStruct(one, jnp.bfloat16),
        "total",
        (residual, own, swap(across_sum, side), back),
    )
    return attended, moe_out


def expert_layer_routed(residual, norm_gain, routes, route_weights, expert_in, expert_down):
    row_count, top_count = routes.shape
    expert_count = expert_in.shape[0] * lax.axis_size("ep")
    capacity = min(row_count, max(2, 2 * row_count * top_count // expert_count))
    whole = lax.all_gather(residual, "tp", axis=1, tiled=True)
    width = whole.shape[1]
    half_width = residual.shape[1]
    normed = normalize(whole, norm_gain)
    flat_routes = routes.reshape(-1)
    hits = (flat_routes[:, None] == jnp.arange(expert_count)[None, :]).astype(jnp.int32)
    before = jnp.cumsum(hits, axis=0) - hits
    position = jnp.sum(before * hits, axis=1)
    slot_flat = flat_routes * capacity + position
    placed = (slot_flat[:, None] == jnp.arange(expert_count * capacity)[None, :]).astype(
        jnp.float32
    )
    placed = placed.reshape(row_count, top_count, expert_count * capacity)
    selector = jnp.sum(placed, axis=1).astype(jnp.bfloat16)
    buffer = jnp.einsum("rs,rd->sd", selector, normed, preferred_element_type=jnp.float32)
    buffer = buffer.astype(jnp.bfloat16).reshape(expert_count, capacity, width)
    arrived = lax.all_to_all(buffer, "ep", split_axis=0, concat_axis=0, tiled=True)
    sources = arrived.shape[0]
    flat_rows = arrived.reshape(sources * capacity, width)
    gate_act = jnp.dot(flat_rows, expert_in[0, 0], preferred_element_type=jnp.float32)
    up_act = jnp.dot(flat_rows, expert_in[0, 1], preferred_element_type=jnp.float32)
    hidden = (jax.nn.silu(gate_act) * up_act).astype(jnp.bfloat16)
    partial_value = jnp.dot(hidden, expert_down[0], preferred_element_type=jnp.float32)
    partial_value = partial_value.reshape(sources, capacity, width)
    summed = lax.psum_scatter(partial_value, "tp", scatter_dimension=2, tiled=True).astype(
        jnp.bfloat16
    )
    returned = lax.all_to_all(summed, "ep", split_axis=0, concat_axis=0, tiled=True)
    weighting = jnp.sum(placed * route_weights[:, :, None], axis=1)
    gathered_rows = returned.reshape(expert_count * capacity, half_width).astype(jnp.float32)
    combined = jnp.dot(weighting, gathered_rows, precision=lax.Precision.HIGHEST)
    return (residual.astype(jnp.float32) + combined).astype(jnp.bfloat16)


def per_device(
    queries,
    key_cache,
    value_cache,
    new_key,
    new_value,
    lengths,
    residual,
    norm_gain,
    routes,
    route_weights,
    expert_in,
    expert_down,
):
    devices = lax.axis_size("ep")
    dense = lax.axis_size("tp") == 1 and devices == 16
    attention = (queries, key_cache, value_cache, new_key, new_value, lengths)
    layer = (residual, norm_gain, routes, route_weights)
    if dense:
        return layer_gathered(attention, *layer, expert_in, expert_down)
    attended = attention_block(*attention)
    return (attended, expert_layer_routed(*layer, expert_in, expert_down))


def solution(mesh):
    in_specs = (
        P(("groups", "ep"), "tp", None),
        P(("groups", "ep"), None, "tp", None),
        P(("groups", "ep"), None, "tp", None),
        P(("groups", "ep"), "tp", None),
        P(("groups", "ep"), "tp", None),
        P(("groups", "ep")),
        P(("groups", "ep"), "tp"),
        P(),
        P(("groups", "ep"), None),
        P(("groups", "ep"), None),
        P("ep", None, None, "tp"),
        P("ep", "tp", None),
    )
    out_specs = (P(("groups", "ep"), "tp", None), P(("groups", "ep"), "tp"))
    return jax.shard_map(
        per_device, mesh=mesh, in_specs=in_specs, out_specs=out_specs, check_vma=False
    )
```

```python
import functools

import jax
import jax.numpy as jnp
from jax import lax
from jax.experimental import pallas as pl
from jax.experimental.pallas import tpu as pltpu
from jax.sharding import PartitionSpec as P


def attention_block(queries, key_cache, value_cache, new_key, new_value, lengths):
    rows_here, heads_here, head_size = queries.shape
    kv_here = key_cache.shape[2]
    slots_here = key_cache.shape[1]
    group = heads_here // kv_here
    scale = 1.0 / head_size**0.5
    grouped = queries.reshape(rows_here, kv_here, group, head_size)
    scores = (
        jnp.einsum("akgd,ackd->akgc", grouped, key_cache, preferred_element_type=jnp.float32)
        * scale
    )
    valid = (jnp.arange(slots_here)[None, :] < lengths[:, None])[:, None, None, :]
    scores = jnp.where(valid, scores, -1e30)
    own_score = (
        jnp.einsum("akgd,akd->akg", grouped, new_key, preferred_element_type=jnp.float32) * scale
    )
    largest = jnp.maximum(jnp.max(scores, axis=-1), own_score)
    cache_exp = jnp.exp(scores - largest[..., None])
    own_exp = jnp.exp(own_score - largest)
    total = jnp.sum(cache_exp, axis=-1) + own_exp
    cache_probs = (cache_exp / total[..., None]).astype(jnp.bfloat16)
    own_probs = (own_exp / total).astype(jnp.bfloat16)
    mixed = jnp.einsum(
        "akgc,ackd->akgd", cache_probs, value_cache, preferred_element_type=jnp.float32
    )
    mixed = (
        mixed
        + own_probs.astype(jnp.float32)[..., None] * new_value.astype(jnp.float32)[:, :, None, :]
    )
    return mixed.reshape(rows_here, heads_here, head_size).astype(jnp.bfloat16)


def normalize(residual, norm_gain):
    wide = residual.astype(jnp.float32)
    return (
        wide * lax.rsqrt(jnp.mean(wide * wide, axis=1, keepdims=True) + 1e-06) * norm_gain
    ).astype(jnp.bfloat16)


def load(sources, targets, sems):
    copies = [
        pltpu.make_async_copy(source, target, sems.at[i])
        for i, (source, target) in enumerate(zip(sources, targets))
    ]
    for copy in copies:
        copy.start()
    return copies


def stay(array):
    return pltpu.with_memory_space_constraint(array, pltpu.HBM)


HERE = pl.BlockSpec(memory_space=pltpu.VMEM)
ANYWHERE = pl.BlockSpec(memory_space=pl.ANY)


def params(mebibytes=4):
    return pltpu.CompilerParams(vmem_limit_bytes=mebibytes * 1024 * 1024)


def cost(flops=0, bytes_accessed=0):
    return pl.CostEstimate(flops=flops, bytes_accessed=bytes_accessed, transcendentals=0)


def from_hbm(kernel, out_shape, name, arrays, after=(), cost_estimate=None):
    return pl.pallas_call(
        kernel,
        out_shape=out_shape,
        in_specs=[pl.BlockSpec(memory_space=pltpu.HBM)] * len(arrays) + [ANYWHERE] * len(after),
        scratch_shapes=[
            (pltpu.VMEM if array.ndim > 1 else pltpu.SMEM)(array.shape, array.dtype)
            for array in arrays
        ]
        + [pltpu.SemaphoreType.DMA((len(arrays),))],
        compiler_params=params(),
        cost_estimate=cost_estimate,
        name=name,
    )(*(stay(array) for array in arrays), *after)


def attend_kernel(*refs):
    attended_ref = refs[-8]
    lengths_ref, queries_ref, keys_ref, values_ref, new_keys_ref, new_values_ref = refs[-7:-1]
    copies = load(refs[:6], refs[-7:-1], refs[-1])
    row_count, heads, head_size = queries_ref.shape
    kv_heads = new_keys_ref.shape[0] // row_count
    group = heads // kv_heads
    scale = 1.0 / head_size**0.5
    across = (((1,), (1,)), ((), ()))

    def grids(columns):
        shape = (heads, columns)
        head = lax.broadcasted_iota(jnp.int32, shape, 0) // group
        return head, lax.broadcasted_iota(jnp.int32, shape, 1)

    head, column = grids(keys_ref.shape[1])
    own_head, own_column = grids(new_keys_ref.shape[0])
    same_head = column % kv_heads == head
    slot = column // kv_heads
    for copy in copies:
        copy.wait()
    for a in range(row_count):
        query = queries_ref[a]
        scores = lax.dot_general(query, keys_ref[a], across, preferred_element_type=jnp.float32)
        scores = jnp.where(same_head & (slot < lengths_ref[a]), scores * scale, -1e30)
        own = lax.dot_general(
            query, new_keys_ref[...], across, preferred_element_type=jnp.float32
        )
        own = jnp.where(own_column == own_head + a * kv_heads, own * scale, -1e30)
        largest = jnp.maximum(
            jnp.max(scores, axis=1, keepdims=True), jnp.max(own, axis=1, keepdims=True)
        )
        scores = jnp.exp(scores - largest)
        own = jnp.exp(own - largest)
        total = jnp.sum(scores, axis=1, keepdims=True) + jnp.sum(own, axis=1, keepdims=True)
        mixed = jnp.dot(
            (scores / total).astype(jnp.bfloat16),
            values_ref[a],
            preferred_element_type=jnp.float32,
        ) + jnp.dot(
            (own / total).astype(jnp.bfloat16),
            new_values_ref[...],
            preferred_element_type=jnp.float32,
        )
        attended_ref[a] = mixed.astype(jnp.bfloat16)


def attend(queries, key_cache, value_cache, new_key, new_value, lengths, after):
    rows_here, slots_here, kv_here, head_size = key_cache.shape
    lines = (rows_here, slots_here * kv_here, head_size)
    arrays = (
        lengths,
        queries,
        key_cache.reshape(lines),
        value_cache.reshape(lines),
        new_key.reshape(-1, head_size),
        new_value.reshape(-1, head_size),
    )
    out_shape = jax.ShapeDtypeStruct(queries.shape, jnp.bfloat16)
    work = cost(0, 16 * key_cache.size * key_cache.dtype.itemsize)
    return from_hbm(attend_kernel, out_shape, "attend", arrays, after, work)


def hold_kernel(count, pieces, *refs):
    sources, targets, sems = refs[:count], refs[-1 - count : -1], refs[-1]
    starts, ends = [], []
    for source, target in zip(sources, targets):
        lines = source.shape[0] // pieces
        for i in range(pieces):
            starts.append(source.at[pl.ds(i * lines, lines)])
            ends.append(target.at[pl.ds(i * lines, lines)])
    for copy in load(starts, ends, sems):
        copy.wait()


def hold(arrays, after, pieces=4):
    flat = [array.reshape(-1, array.shape[-1]) for array in arrays]
    size = sum(array.size for array in flat)
    return pl.pallas_call(
        functools.partial(hold_kernel, len(flat), pieces),
        out_shape=[pltpu.VMEM(array.shape, array.dtype) for array in flat],
        in_specs=[pl.BlockSpec(memory_space=pltpu.HBM)] * len(flat) + [ANYWHERE] * len(after),
        scratch_shapes=[pltpu.SemaphoreType.DMA((pieces * len(flat),))],
        cost_estimate=cost(0, 2 * size),
        compiler_params=params(),
        name="hold",
    )(*(stay(array) for array in flat), *after)


def prepare_kernel(*refs):
    packed_ref, residual_ref, gain_ref, routes_ref, weights_ref, sems = refs[4:]
    for copy in load(refs[:4], refs[5:9], sems):
        copy.wait()
    row_count, width = residual_ref.shape
    experts = lax.axis_size("ep")
    lanes = packed_ref.shape[1] - width
    wide = residual_ref[...].astype(jnp.float32)
    mean = jnp.mean(wide * wide, axis=1, keepdims=True)
    packed_ref[:, :width] = (wide * lax.rsqrt(mean + 1e-06) * gain_ref[...]).astype(jnp.bfloat16)
    line = lax.broadcasted_iota(jnp.int32, (lanes, row_count), 0)
    expert = lax.rem(line, experts)
    weight = jnp.zeros(line.shape, jnp.float32)
    for k in range(routes_ref.shape[0]):
        weight += jnp.where(routes_ref[k : k + 1, :] == expert, weights_ref[k : k + 1, :], 0.0)
    high = weight.astype(jnp.bfloat16).astype(jnp.float32)
    low = (weight - high).astype(jnp.bfloat16).astype(jnp.float32)
    lowest = weight - high - low
    terms = jnp.where(
        line < experts,
        high,
        jnp.where(line < 2 * experts, low, jnp.where(line < 3 * experts, lowest, 0.0)),
    )
    at = lax.broadcasted_iota(jnp.int32, (row_count, row_count), 0)
    same = at == lax.broadcasted_iota(jnp.int32, (row_count, row_count), 1)
    turned = lax.dot_general(
        same.astype(jnp.bfloat16),
        terms.astype(jnp.bfloat16),
        (((1,), (1,)), ((), ())),
        preferred_element_type=jnp.float32,
    )
    packed_ref[:, width:] = turned.astype(jnp.bfloat16)


def stack_kernel(*refs):
    for i in range(refs[-1].shape[0]):
        refs[-1][i] = refs[i][...]


def relay_kernel(in_ref, *refs):
    refs[-1][...] = in_ref[...]


def ffn_kernel(takes, *refs):
    in_ref, down_ref = refs[4:6]
    near_ref, far_ref = refs[-2:]
    width = down_ref.shape[1]
    packed = jnp.concatenate(
        [refs[i][b] for i, start, stop in takes for b in range(start, stop)], axis=0
    )
    rows = packed[:, :width]
    terms = packed[:, width:].astype(jnp.float32)
    lane = lax.broadcasted_iota(jnp.int32, terms.shape, 1)
    mine = lax.rem(lane, lax.axis_size("ep")) == lax.axis_index("ep")
    weight = jnp.sum(jnp.where(mine, terms, 0.0), axis=1, keepdims=True)
    gate = jnp.dot(rows, in_ref[:width], preferred_element_type=jnp.float32)
    up = jnp.dot(rows, in_ref[width:], preferred_element_type=jnp.float32)
    hidden = (gate / (1.0 + jnp.exp(-gate)) * up).astype(jnp.bfloat16)
    out = jnp.dot(hidden, down_ref[...], preferred_element_type=jnp.float32)
    out = (out * weight).astype(jnp.bfloat16).reshape((2,) + near_ref.shape)
    near_ref[...] = out[0]
    far_ref[...] = out[1]


def pair_kernel(own_ref, other_ref, *refs):
    keep_ref, send_ref = refs[-2:]
    half = keep_ref.shape[0]
    keep_ref[...] = own_ref[:half].astype(jnp.float32) + other_ref[:half].astype(jnp.float32)
    send = own_ref[half:].astype(jnp.float32) + other_ref[half:].astype(jnp.float32)
    send_ref[...] = send.astype(jnp.bfloat16)


def square_kernel(own_ref, other_ref, *out_refs):
    for i, out_ref in enumerate(out_refs):
        total = own_ref[i] + other_ref[i].astype(jnp.float32)
        out_ref[...] = total.astype(out_ref.dtype)


def total_kernel(residual_ref, *refs):
    total = residual_ref[...].astype(jnp.float32)
    for ref in refs[:-1]:
        total += ref[...].astype(jnp.float32)
    refs[-1][...] = total.astype(jnp.bfloat16)


def in_vmem(kernel, out_shape, name, arrays, after=(), mebibytes=4, cost_estimate=None):
    return pl.pallas_call(
        kernel,
        out_shape=out_shape,
        in_specs=[HERE] * len(arrays) + [ANYWHERE] * len(after),
        compiler_params=params(mebibytes),
        cost_estimate=cost_estimate,
        name=name,
    )(*arrays, *after)


def layer_gathered(attention, residual, norm_gain, routes, route_weights, expert_in, expert_down):
    row_count, width = residual.shape
    devices = lax.axis_size("ep")
    core, side, line = 1, 2, 4
    extra = -(-3 * devices // 128) * 128
    vmem = pltpu.VMEM
    one = (row_count, width)
    block = vmem((row_count, width + extra), jnp.bfloat16)

    def swap(value, bits):
        return lax.ppermute(value, "ep", [(i, i ^ bits) for i in range(devices)])

    def relay(value, after):
        return in_vmem(relay_kernel, vmem(value.shape, value.dtype), "relay", (value,), after)

    def stack(members, after=()):
        shape = vmem((len(members), row_count, width + extra), jnp.bfloat16)
        return in_vmem(stack_kernel, shape, "stack", members, after)

    packed = from_hbm(
        prepare_kernel,
        block,
        "prepare",
        (residual, norm_gain.reshape(1, -1), routes.T, route_weights.T),
    )
    third, second, first = (swap(packed, d * line) for d in (3, 2, 1))
    across = swap(packed, side)
    along = stack((second, third, first))
    along_side = swap(along, side)
    near = stack((second, third, first, packed, across))
    near_far = swap(near, core)
    held = hold((expert_in, expert_down), (along,))
    along_side_far = swap(relay(along_side, held[:1]), core)

    def ffn(near_takes, side_takes, after=()):
        takes = [(i, *t) for i in (0, 2) for t in near_takes]
        takes[len(near_takes) : len(near_takes)] = [(1, *t) for t in side_takes]
        takes += [(3, *t) for t in side_takes]
        return in_vmem(
            functools.partial(ffn_kernel, takes),
            [vmem((4,) + one, jnp.bfloat16)] * 2,
            "ffn",
            (near, along_side, near_far, along_side_far, *held),
            after,
            mebibytes=16,
            cost_estimate=cost(8 * row_count * 2 * sum(h.size for h in held), 2 * held[0].size),
        )

    def pair_sum(near_out, far_out, after=()):
        shapes = [vmem((2,) + one, jnp.float32), vmem((2,) + one, jnp.bfloat16)]
        return in_vmem(pair_kernel, shapes, "pair_sum", (near_out, swap(far_out, core)), after)

    early_outs = ffn([(0, 2)], [(0, 2)])
    early_keep, early_send = pair_sum(*early_outs)
    early_sums = in_vmem(
        square_kernel,
        [vmem(one, jnp.bfloat16)] * 2,
        "square_sum",
        (early_keep, swap(early_send, side)),
    )
    attended = attend(*attention, tuple(early_sums))
    back = [swap(early_sums[1], 3 * line), swap(early_sums[0], 2 * line)]
    late_outs = ffn([(3, 5), (2, 3)], [(2, 3)], early_outs[:1])
    late_keep, late_send = pair_sum(*late_outs)
    own, across_sum = in_vmem(
        square_kernel,
        [vmem(one, jnp.float32), vmem(one, jnp.bfloat16)],
        "line_sum",
        (late_keep, swap(late_send, line)),
    )
    moe_out = in_vmem(
        total_kernel,
        jax.ShapeDtypeStruct(one, jnp.bfloat16),
        "total",
        (residual, own, *back, swap(across_sum, side)),
    )
    return attended, moe_out


def expert_layer_routed(residual, norm_gain, routes, route_weights, expert_in, expert_down):
    row_count, top_count = routes.shape
    expert_count = expert_in.shape[0] * lax.axis_size("ep")
    capacity = min(row_count, max(2, 2 * row_count * top_count // expert_count))
    whole = lax.all_gather(residual, "tp", axis=1, tiled=True)
    width = whole.shape[1]
    half_width = residual.shape[1]
    normed = normalize(whole, norm_gain)
    flat_routes = routes.reshape(-1)
    hits = (flat_routes[:, None] == jnp.arange(expert_count)[None, :]).astype(jnp.int32)
    before = jnp.cumsum(hits, axis=0) - hits
    position = jnp.sum(before * hits, axis=1)
    slot_flat = flat_routes * capacity + position
    placed = (slot_flat[:, None] == jnp.arange(expert_count * capacity)[None, :]).astype(
        jnp.float32
    )
    placed = placed.reshape(row_count, top_count, expert_count * capacity)
    selector = jnp.sum(placed, axis=1).astype(jnp.bfloat16)
    buffer = jnp.einsum("rs,rd->sd", selector, normed, preferred_element_type=jnp.float32)
    buffer = buffer.astype(jnp.bfloat16).reshape(expert_count, capacity, width)
    arrived = lax.all_to_all(buffer, "ep", split_axis=0, concat_axis=0, tiled=True)
    sources = arrived.shape[0]
    flat_rows = arrived.reshape(sources * capacity, width)
    gate_act = jnp.dot(flat_rows, expert_in[0, 0], preferred_element_type=jnp.float32)
    up_act = jnp.dot(flat_rows, expert_in[0, 1], preferred_element_type=jnp.float32)
    hidden = (jax.nn.silu(gate_act) * up_act).astype(jnp.bfloat16)
    partial_value = jnp.dot(hidden, expert_down[0], preferred_element_type=jnp.float32)
    partial_value = partial_value.reshape(sources, capacity, width)
    summed = lax.psum_scatter(partial_value, "tp", scatter_dimension=2, tiled=True).astype(
        jnp.bfloat16
    )
    returned = lax.all_to_all(summed, "ep", split_axis=0, concat_axis=0, tiled=True)
    weighting = jnp.sum(placed * route_weights[:, :, None], axis=1)
    gathered_rows = returned.reshape(expert_count * capacity, half_width).astype(jnp.float32)
    combined = jnp.dot(weighting, gathered_rows, precision=lax.Precision.HIGHEST)
    return (residual.astype(jnp.float32) + combined).astype(jnp.bfloat16)


def per_device(
    queries,
    key_cache,
    value_cache,
    new_key,
    new_value,
    lengths,
    residual,
    norm_gain,
    routes,
    route_weights,
    expert_in,
    expert_down,
):
    devices = lax.axis_size("ep")
    dense = lax.axis_size("tp") == 1 and devices == 16
    attention = (queries, key_cache, value_cache, new_key, new_value, lengths)
    layer = (residual, norm_gain, routes, route_weights)
    if dense:
        return layer_gathered(attention, *layer, expert_in, expert_down)
    attended = attention_block(*attention)
    return (attended, expert_layer_routed(*layer, expert_in, expert_down))


def solution(mesh):
    in_specs = (
        P(("groups", "ep"), "tp", None),
        P(("groups", "ep"), None, "tp", None),
        P(("groups", "ep"), None, "tp", None),
        P(("groups", "ep"), "tp", None),
        P(("groups", "ep"), "tp", None),
        P(("groups", "ep")),
        P(("groups", "ep"), "tp"),
        P(),
        P(("groups", "ep"), None),
        P(("groups", "ep"), None),
        P("ep", None, None, "tp"),
        P("ep", "tp", None),
    )
    out_specs = (P(("groups", "ep"), "tp", None), P(("groups", "ep"), "tp"))
    return jax.shard_map(
        per_device, mesh=mesh, in_specs=in_specs, out_specs=out_specs, check_vma=False
    )
```

```python
import functools

import jax
import jax.numpy as jnp
from jax import lax
from jax.experimental import pallas as pl
from jax.experimental.pallas import tpu as pltpu
from jax.sharding import PartitionSpec as P


def attention_block(queries, key_cache, value_cache, new_key, new_value, lengths):
    rows_here, heads_here, head_size = queries.shape
    kv_here = key_cache.shape[2]
    slots_here = key_cache.shape[1]
    group = heads_here // kv_here
    scale = 1.0 / head_size**0.5
    grouped = queries.reshape(rows_here, kv_here, group, head_size)
    scores = (
        jnp.einsum("akgd,ackd->akgc", grouped, key_cache, preferred_element_type=jnp.float32)
        * scale
    )
    valid = (jnp.arange(slots_here)[None, :] < lengths[:, None])[:, None, None, :]
    scores = jnp.where(valid, scores, -1e30)
    own_score = (
        jnp.einsum("akgd,akd->akg", grouped, new_key, preferred_element_type=jnp.float32) * scale
    )
    largest = jnp.maximum(jnp.max(scores, axis=-1), own_score)
    cache_exp = jnp.exp(scores - largest[..., None])
    own_exp = jnp.exp(own_score - largest)
    total = jnp.sum(cache_exp, axis=-1) + own_exp
    cache_probs = (cache_exp / total[..., None]).astype(jnp.bfloat16)
    own_probs = (own_exp / total).astype(jnp.bfloat16)
    mixed = jnp.einsum(
        "akgc,ackd->akgd", cache_probs, value_cache, preferred_element_type=jnp.float32
    )
    mixed = (
        mixed
        + own_probs.astype(jnp.float32)[..., None] * new_value.astype(jnp.float32)[:, :, None, :]
    )
    return mixed.reshape(rows_here, heads_here, head_size).astype(jnp.bfloat16)


def normalize(residual, norm_gain):
    wide = residual.astype(jnp.float32)
    return (
        wide * lax.rsqrt(jnp.mean(wide * wide, axis=1, keepdims=True) + 1e-06) * norm_gain
    ).astype(jnp.bfloat16)


def load(sources, targets, sems):
    copies = [
        pltpu.make_async_copy(source, target, sems.at[i])
        for i, (source, target) in enumerate(zip(sources, targets))
    ]
    for copy in copies:
        copy.start()
    return copies


def stay(array):
    return pltpu.with_memory_space_constraint(array, pltpu.HBM)


HERE = pl.BlockSpec(memory_space=pltpu.VMEM)
ANYWHERE = pl.BlockSpec(memory_space=pl.ANY)


def params(mebibytes=4):
    return pltpu.CompilerParams(vmem_limit_bytes=mebibytes * 1024 * 1024)


def cost(flops=0, bytes_accessed=0):
    return pl.CostEstimate(flops=flops, bytes_accessed=bytes_accessed, transcendentals=0)


def from_hbm(kernel, out_shape, name, arrays, after=(), cost_estimate=None):
    return pl.pallas_call(
        kernel,
        out_shape=out_shape,
        in_specs=[pl.BlockSpec(memory_space=pltpu.HBM)] * len(arrays) + [ANYWHERE] * len(after),
        scratch_shapes=[
            (pltpu.VMEM if array.ndim > 1 else pltpu.SMEM)(array.shape, array.dtype)
            for array in arrays
        ]
        + [pltpu.SemaphoreType.DMA((len(arrays),))],
        compiler_params=params(),
        cost_estimate=cost_estimate,
        name=name,
    )(*(stay(array) for array in arrays), *after)


def attend_kernel(*refs):
    attended_ref = refs[-8]
    lengths_ref, queries_ref, keys_ref, values_ref, new_keys_ref, new_values_ref = refs[-7:-1]
    copies = load(refs[:6], refs[-7:-1], refs[-1])
    row_count, heads, head_size = queries_ref.shape
    kv_heads = new_keys_ref.shape[0] // row_count
    group = heads // kv_heads
    scale = 1.0 / head_size**0.5
    across = (((1,), (1,)), ((), ()))

    def grids(columns):
        shape = (heads, columns)
        head = lax.broadcasted_iota(jnp.int32, shape, 0) // group
        return head, lax.broadcasted_iota(jnp.int32, shape, 1)

    head, column = grids(keys_ref.shape[1])
    own_head, own_column = grids(new_keys_ref.shape[0])
    same_head = column % kv_heads == head
    slot = column // kv_heads
    for copy in copies:
        copy.wait()
    for a in range(row_count):
        query = queries_ref[a]
        scores = lax.dot_general(query, keys_ref[a], across, preferred_element_type=jnp.float32)
        scores = jnp.where(same_head & (slot < lengths_ref[a]), scores * scale, -1e30)
        own = lax.dot_general(
            query, new_keys_ref[...], across, preferred_element_type=jnp.float32
        )
        own = jnp.where(own_column == own_head + a * kv_heads, own * scale, -1e30)
        largest = jnp.maximum(
            jnp.max(scores, axis=1, keepdims=True), jnp.max(own, axis=1, keepdims=True)
        )
        scores = jnp.exp(scores - largest)
        own = jnp.exp(own - largest)
        total = jnp.sum(scores, axis=1, keepdims=True) + jnp.sum(own, axis=1, keepdims=True)
        mixed = jnp.dot(
            (scores / total).astype(jnp.bfloat16),
            values_ref[a],
            preferred_element_type=jnp.float32,
        ) + jnp.dot(
            (own / total).astype(jnp.bfloat16),
            new_values_ref[...],
            preferred_element_type=jnp.float32,
        )
        attended_ref[a] = mixed.astype(jnp.bfloat16)


def attend(queries, key_cache, value_cache, new_key, new_value, lengths, after):
    rows_here, slots_here, kv_here, head_size = key_cache.shape
    lines = (rows_here, slots_here * kv_here, head_size)
    arrays = (
        lengths,
        queries,
        key_cache.reshape(lines),
        value_cache.reshape(lines),
        new_key.reshape(-1, head_size),
        new_value.reshape(-1, head_size),
    )
    out_shape = jax.ShapeDtypeStruct(queries.shape, jnp.bfloat16)
    work = cost(0, 16 * key_cache.size * key_cache.dtype.itemsize)
    return from_hbm(attend_kernel, out_shape, "attend", arrays, after, work)


def hold_kernel(count, pieces, *refs):
    sources, targets, sems = refs[:count], refs[-1 - count : -1], refs[-1]
    starts, ends = [], []
    for source, target in zip(sources, targets):
        lines = source.shape[0] // pieces
        for i in range(pieces):
            starts.append(source.at[pl.ds(i * lines, lines)])
            ends.append(target.at[pl.ds(i * lines, lines)])
    for copy in load(starts, ends, sems):
        copy.wait()


def hold(arrays, after, pieces=4):
    flat = [array.reshape(-1, array.shape[-1]) for array in arrays]
    size = sum(array.size for array in flat)
    return pl.pallas_call(
        functools.partial(hold_kernel, len(flat), pieces),
        out_shape=[pltpu.VMEM(array.shape, array.dtype) for array in flat],
        in_specs=[pl.BlockSpec(memory_space=pltpu.HBM)] * len(flat) + [ANYWHERE] * len(after),
        scratch_shapes=[pltpu.SemaphoreType.DMA((pieces * len(flat),))],
        cost_estimate=cost(0, 2 * size),
        compiler_params=params(),
        name="hold",
    )(*(stay(array) for array in flat), *after)


def prepare_kernel(*refs):
    packed_ref, residual_ref, gain_ref, routes_ref, weights_ref, sems = refs[4:]
    for copy in load(refs[:4], refs[5:9], sems):
        copy.wait()
    row_count, width = residual_ref.shape
    experts = lax.axis_size("ep")
    lanes = packed_ref.shape[1] - width
    wide = residual_ref[...].astype(jnp.float32)
    mean = jnp.mean(wide * wide, axis=1, keepdims=True)
    packed_ref[:, :width] = (wide * lax.rsqrt(mean + 1e-06) * gain_ref[...]).astype(jnp.bfloat16)
    line = lax.broadcasted_iota(jnp.int32, (lanes, row_count), 0)
    expert = lax.rem(line, experts)
    weight = jnp.zeros(line.shape, jnp.float32)
    for k in range(routes_ref.shape[0]):
        weight += jnp.where(routes_ref[k : k + 1, :] == expert, weights_ref[k : k + 1, :], 0.0)
    high = weight.astype(jnp.bfloat16).astype(jnp.float32)
    low = (weight - high).astype(jnp.bfloat16).astype(jnp.float32)
    lowest = weight - high - low
    terms = jnp.where(
        line < experts,
        high,
        jnp.where(line < 2 * experts, low, jnp.where(line < 3 * experts, lowest, 0.0)),
    )
    at = lax.broadcasted_iota(jnp.int32, (row_count, row_count), 0)
    same = at == lax.broadcasted_iota(jnp.int32, (row_count, row_count), 1)
    turned = lax.dot_general(
        same.astype(jnp.bfloat16),
        terms.astype(jnp.bfloat16),
        (((1,), (1,)), ((), ())),
        preferred_element_type=jnp.float32,
    )
    packed_ref[:, width:] = turned.astype(jnp.bfloat16)


def stack_kernel(*refs):
    for i in range(refs[-1].shape[0]):
        refs[-1][i] = refs[i][...]


def relay_kernel(in_ref, *refs):
    refs[-1][...] = in_ref[...]


def ffn_kernel(takes, *refs):
    in_ref, down_ref = refs[4:6]
    near_ref, far_ref = refs[-2:]
    width = down_ref.shape[1]
    packed = jnp.concatenate(
        [refs[i][b] for i, start, stop in takes for b in range(start, stop)], axis=0
    )
    rows = packed[:, :width]
    terms = packed[:, width:].astype(jnp.float32)
    lane = lax.broadcasted_iota(jnp.int32, terms.shape, 1)
    mine = lax.rem(lane, lax.axis_size("ep")) == lax.axis_index("ep")
    weight = jnp.sum(jnp.where(mine, terms, 0.0), axis=1, keepdims=True)
    gate = jnp.dot(rows, in_ref[:width], preferred_element_type=jnp.float32)
    up = jnp.dot(rows, in_ref[width:], preferred_element_type=jnp.float32)
    hidden = (gate / (1.0 + jnp.exp(-gate)) * up).astype(jnp.bfloat16)
    out = jnp.dot(hidden, down_ref[...], preferred_element_type=jnp.float32)
    out = (out * weight).astype(jnp.bfloat16).reshape((2,) + near_ref.shape)
    near_ref[...] = out[0]
    far_ref[...] = out[1]


def pair_kernel(own_ref, other_ref, *refs):
    keep_ref, send_ref = refs[-2:]
    half = keep_ref.shape[0]
    keep_ref[...] = own_ref[:half].astype(jnp.float32) + other_ref[:half].astype(jnp.float32)
    send = own_ref[half:].astype(jnp.float32) + other_ref[half:].astype(jnp.float32)
    send_ref[...] = send.astype(jnp.bfloat16)


def square_kernel(own_ref, other_ref, *out_refs):
    for i, out_ref in enumerate(out_refs):
        total = own_ref[i] + other_ref[i].astype(jnp.float32)
        out_ref[...] = total.astype(out_ref.dtype)


def total_kernel(residual_ref, *refs):
    total = residual_ref[...].astype(jnp.float32)
    for ref in refs[:-1]:
        total += ref[...].astype(jnp.float32)
    refs[-1][...] = total.astype(jnp.bfloat16)


def in_vmem(kernel, out_shape, name, arrays, after=(), mebibytes=4, cost_estimate=None):
    return pl.pallas_call(
        kernel,
        out_shape=out_shape,
        in_specs=[HERE] * len(arrays) + [ANYWHERE] * len(after),
        compiler_params=params(mebibytes),
        cost_estimate=cost_estimate,
        name=name,
    )(*arrays, *after)


def layer_gathered(attention, residual, norm_gain, routes, route_weights, expert_in, expert_down):
    row_count, width = residual.shape
    devices = lax.axis_size("ep")
    core, side, line = 1, 2, 4
    extra = -(-3 * devices // 128) * 128
    vmem = pltpu.VMEM
    one = (row_count, width)
    block = vmem((row_count, width + extra), jnp.bfloat16)

    def swap(value, bits):
        return lax.ppermute(value, "ep", [(i, i ^ bits) for i in range(devices)])

    def relay(value, after):
        return in_vmem(relay_kernel, vmem(value.shape, value.dtype), "relay", (value,), after)

    def stack(members, after=()):
        shape = vmem((len(members), row_count, width + extra), jnp.bfloat16)
        return in_vmem(stack_kernel, shape, "stack", members, after)

    packed = from_hbm(
        prepare_kernel,
        block,
        "prepare",
        (residual, norm_gain.reshape(1, -1), routes.T, route_weights.T),
    )
    second, third, first = (swap(packed, d * line) for d in (2, 3, 1))
    across = swap(packed, side)
    attended = attend(*attention, (packed,))
    along = stack((second, third, first), (stay(attended),))
    along_side = swap(along, side)
    near = stack((second, third, first, packed, across))
    near_far = swap(near, core)
    held = hold((expert_in, expert_down), (along,))
    along_side_far = swap(relay(along_side, held[:1]), core)

    def ffn(near_takes, side_takes, after=()):
        takes = [(i, *t) for i in (0, 2) for t in near_takes]
        takes[len(near_takes) : len(near_takes)] = [(1, *t) for t in side_takes]
        takes += [(3, *t) for t in side_takes]
        return in_vmem(
            functools.partial(ffn_kernel, takes),
            [vmem((4,) + one, jnp.bfloat16)] * 2,
            "ffn",
            (near, along_side, near_far, along_side_far, *held),
            after,
            mebibytes=16,
            cost_estimate=cost(8 * row_count * 2 * sum(h.size for h in held), 2 * held[0].size),
        )

    def pair_sum(near_out, far_out, after=()):
        shapes = [vmem((2,) + one, jnp.float32), vmem((2,) + one, jnp.bfloat16)]
        return in_vmem(pair_kernel, shapes, "pair_sum", (near_out, swap(far_out, core)), after)

    early_outs = ffn([(0, 2)], [(0, 2)])
    early_keep, early_send = pair_sum(*early_outs)
    early_sums = in_vmem(
        square_kernel,
        [vmem(one, jnp.bfloat16)] * 2,
        "square_sum",
        (early_keep, swap(early_send, side)),
    )
    back = [swap(early_sums[0], 2 * line), swap(early_sums[1], 3 * line)]
    late_outs = ffn([(3, 5), (2, 3)], [(2, 3)], early_outs[:1])
    late_keep, late_send = pair_sum(*late_outs)
    own, across_sum = in_vmem(
        square_kernel,
        [vmem(one, jnp.float32), vmem(one, jnp.bfloat16)],
        "line_sum",
        (late_keep, swap(late_send, line)),
    )
    moe_out = in_vmem(
        total_kernel,
        jax.ShapeDtypeStruct(one, jnp.bfloat16),
        "total",
        (residual, own, *back, swap(across_sum, side)),
    )
    return attended, moe_out


def expert_layer_routed(residual, norm_gain, routes, route_weights, expert_in, expert_down):
    row_count, top_count = routes.shape
    expert_count = expert_in.shape[0] * lax.axis_size("ep")
    capacity = min(row_count, max(2, 2 * row_count * top_count // expert_count))
    whole = lax.all_gather(residual, "tp", axis=1, tiled=True)
    width = whole.shape[1]
    half_width = residual.shape[1]
    normed = normalize(whole, norm_gain)
    flat_routes = routes.reshape(-1)
    hits = (flat_routes[:, None] == jnp.arange(expert_count)[None, :]).astype(jnp.int32)
    before = jnp.cumsum(hits, axis=0) - hits
    position = jnp.sum(before * hits, axis=1)
    slot_flat = flat_routes * capacity + position
    placed = (slot_flat[:, None] == jnp.arange(expert_count * capacity)[None, :]).astype(
        jnp.float32
    )
    placed = placed.reshape(row_count, top_count, expert_count * capacity)
    selector = jnp.sum(placed, axis=1).astype(jnp.bfloat16)
    buffer = jnp.einsum("rs,rd->sd", selector, normed, preferred_element_type=jnp.float32)
    buffer = buffer.astype(jnp.bfloat16).reshape(expert_count, capacity, width)
    arrived = lax.all_to_all(buffer, "ep", split_axis=0, concat_axis=0, tiled=True)
    sources = arrived.shape[0]
    flat_rows = arrived.reshape(sources * capacity, width)
    gate_act = jnp.dot(flat_rows, expert_in[0, 0], preferred_element_type=jnp.float32)
    up_act = jnp.dot(flat_rows, expert_in[0, 1], preferred_element_type=jnp.float32)
    hidden = (jax.nn.silu(gate_act) * up_act).astype(jnp.bfloat16)
    partial_value = jnp.dot(hidden, expert_down[0], preferred_element_type=jnp.float32)
    partial_value = partial_value.reshape(sources, capacity, width)
    summed = lax.psum_scatter(partial_value, "tp", scatter_dimension=2, tiled=True).astype(
        jnp.bfloat16
    )
    returned = lax.all_to_all(summed, "ep", split_axis=0, concat_axis=0, tiled=True)
    weighting = jnp.sum(placed * route_weights[:, :, None], axis=1)
    gathered_rows = returned.reshape(expert_count * capacity, half_width).astype(jnp.float32)
    combined = jnp.dot(weighting, gathered_rows, precision=lax.Precision.HIGHEST)
    return (residual.astype(jnp.float32) + combined).astype(jnp.bfloat16)


def per_device(
    queries,
    key_cache,
    value_cache,
    new_key,
    new_value,
    lengths,
    residual,
    norm_gain,
    routes,
    route_weights,
    expert_in,
    expert_down,
):
    devices = lax.axis_size("ep")
    dense = lax.axis_size("tp") == 1 and devices == 16
    attention = (queries, key_cache, value_cache, new_key, new_value, lengths)
    layer = (residual, norm_gain, routes, route_weights)
    if dense:
        return layer_gathered(attention, *layer, expert_in, expert_down)
    attended = attention_block(*attention)
    return (attended, expert_layer_routed(*layer, expert_in, expert_down))


def solution(mesh):
    in_specs = (
        P(("groups", "ep"), "tp", None),
        P(("groups", "ep"), None, "tp", None),
        P(("groups", "ep"), None, "tp", None),
        P(("groups", "ep"), "tp", None),
        P(("groups", "ep"), "tp", None),
        P(("groups", "ep")),
        P(("groups", "ep"), "tp"),
        P(),
        P(("groups", "ep"), None),
        P(("groups", "ep"), None),
        P("ep", None, None, "tp"),
        P("ep", "tp", None),
    )
    out_specs = (P(("groups", "ep"), "tp", None), P(("groups", "ep"), "tp"))
    return jax.shard_map(
        per_device, mesh=mesh, in_specs=in_specs, out_specs=out_specs, check_vma=False
    )
```

```python
import functools

import jax
import jax.numpy as jnp
from jax import lax
from jax.experimental import pallas as pl
from jax.experimental.pallas import tpu as pltpu
from jax.sharding import PartitionSpec as P


def attention_block(queries, key_cache, value_cache, new_key, new_value, lengths):
    rows_here, heads_here, head_size = queries.shape
    kv_here = key_cache.shape[2]
    slots_here = key_cache.shape[1]
    group = heads_here // kv_here
    scale = 1.0 / head_size**0.5
    grouped = queries.reshape(rows_here, kv_here, group, head_size)
    scores = (
        jnp.einsum("akgd,ackd->akgc", grouped, key_cache, preferred_element_type=jnp.float32)
        * scale
    )
    valid = (jnp.arange(slots_here)[None, :] < lengths[:, None])[:, None, None, :]
    scores = jnp.where(valid, scores, -1e30)
    own_score = (
        jnp.einsum("akgd,akd->akg", grouped, new_key, preferred_element_type=jnp.float32) * scale
    )
    largest = jnp.maximum(jnp.max(scores, axis=-1), own_score)
    cache_exp = jnp.exp(scores - largest[..., None])
    own_exp = jnp.exp(own_score - largest)
    total = jnp.sum(cache_exp, axis=-1) + own_exp
    cache_probs = (cache_exp / total[..., None]).astype(jnp.bfloat16)
    own_probs = (own_exp / total).astype(jnp.bfloat16)
    mixed = jnp.einsum(
        "akgc,ackd->akgd", cache_probs, value_cache, preferred_element_type=jnp.float32
    )
    mixed = (
        mixed
        + own_probs.astype(jnp.float32)[..., None] * new_value.astype(jnp.float32)[:, :, None, :]
    )
    return mixed.reshape(rows_here, heads_here, head_size).astype(jnp.bfloat16)


def normalize(residual, norm_gain):
    wide = residual.astype(jnp.float32)
    return (
        wide * lax.rsqrt(jnp.mean(wide * wide, axis=1, keepdims=True) + 1e-06) * norm_gain
    ).astype(jnp.bfloat16)


def load(sources, targets, sems):
    copies = [
        pltpu.make_async_copy(source, target, sems.at[i])
        for i, (source, target) in enumerate(zip(sources, targets))
    ]
    for copy in copies:
        copy.start()
    return copies


def stay(array):
    return pltpu.with_memory_space_constraint(array, pltpu.HBM)


HERE = pl.BlockSpec(memory_space=pltpu.VMEM)
ANYWHERE = pl.BlockSpec(memory_space=pl.ANY)


def params(mebibytes=4):
    return pltpu.CompilerParams(vmem_limit_bytes=mebibytes * 1024 * 1024)


def cost(flops=0, bytes_accessed=0):
    return pl.CostEstimate(flops=flops, bytes_accessed=bytes_accessed, transcendentals=0)


def from_hbm(kernel, out_shape, name, arrays, after=(), cost_estimate=None):
    return pl.pallas_call(
        kernel,
        out_shape=out_shape,
        in_specs=[pl.BlockSpec(memory_space=pltpu.HBM)] * len(arrays) + [ANYWHERE] * len(after),
        scratch_shapes=[
            (pltpu.VMEM if array.ndim > 1 else pltpu.SMEM)(array.shape, array.dtype)
            for array in arrays
        ]
        + [pltpu.SemaphoreType.DMA((len(arrays),))],
        compiler_params=params(),
        cost_estimate=cost_estimate,
        name=name,
    )(*(stay(array) for array in arrays), *after)


def attend_kernel(*refs):
    attended_ref = refs[-8]
    lengths_ref, queries_ref, keys_ref, values_ref, new_keys_ref, new_values_ref = refs[-7:-1]
    copies = load(refs[:6], refs[-7:-1], refs[-1])
    row_count, heads, head_size = queries_ref.shape
    kv_heads = new_keys_ref.shape[0] // row_count
    group = heads // kv_heads
    scale = 1.0 / head_size**0.5
    across = (((1,), (1,)), ((), ()))

    def grids(columns):
        shape = (heads, columns)
        head = lax.broadcasted_iota(jnp.int32, shape, 0) // group
        return head, lax.broadcasted_iota(jnp.int32, shape, 1)

    head, column = grids(keys_ref.shape[1])
    own_head, own_column = grids(new_keys_ref.shape[0])
    same_head = column % kv_heads == head
    slot = column // kv_heads
    for copy in copies:
        copy.wait()
    for a in range(row_count):
        query = queries_ref[a]
        scores = lax.dot_general(query, keys_ref[a], across, preferred_element_type=jnp.float32)
        scores = jnp.where(same_head & (slot < lengths_ref[a]), scores * scale, -1e30)
        own = lax.dot_general(
            query, new_keys_ref[...], across, preferred_element_type=jnp.float32
        )
        own = jnp.where(own_column == own_head + a * kv_heads, own * scale, -1e30)
        largest = jnp.maximum(
            jnp.max(scores, axis=1, keepdims=True), jnp.max(own, axis=1, keepdims=True)
        )
        scores = jnp.exp(scores - largest)
        own = jnp.exp(own - largest)
        total = jnp.sum(scores, axis=1, keepdims=True) + jnp.sum(own, axis=1, keepdims=True)
        mixed = jnp.dot(
            (scores / total).astype(jnp.bfloat16),
            values_ref[a],
            preferred_element_type=jnp.float32,
        ) + jnp.dot(
            (own / total).astype(jnp.bfloat16),
            new_values_ref[...],
            preferred_element_type=jnp.float32,
        )
        attended_ref[a] = mixed.astype(jnp.bfloat16)


def attend(queries, key_cache, value_cache, new_key, new_value, lengths, after):
    rows_here, slots_here, kv_here, head_size = key_cache.shape
    lines = (rows_here, slots_here * kv_here, head_size)
    arrays = (
        lengths,
        queries,
        key_cache.reshape(lines),
        value_cache.reshape(lines),
        new_key.reshape(-1, head_size),
        new_value.reshape(-1, head_size),
    )
    out_shape = jax.ShapeDtypeStruct(queries.shape, jnp.bfloat16)
    work = cost(0, 16 * key_cache.size * key_cache.dtype.itemsize)
    return from_hbm(attend_kernel, out_shape, "attend", arrays, after, work)


def hold_kernel(count, pieces, *refs):
    sources, targets, sems = refs[:count], refs[-1 - count : -1], refs[-1]
    starts, ends = [], []
    for source, target in zip(sources, targets):
        lines = source.shape[0] // pieces
        for i in range(pieces):
            starts.append(source.at[pl.ds(i * lines, lines)])
            ends.append(target.at[pl.ds(i * lines, lines)])
    for copy in load(starts, ends, sems):
        copy.wait()


def hold(arrays, after, pieces=4):
    flat = [array.reshape(-1, array.shape[-1]) for array in arrays]
    size = sum(array.size for array in flat)
    return pl.pallas_call(
        functools.partial(hold_kernel, len(flat), pieces),
        out_shape=[pltpu.VMEM(array.shape, array.dtype) for array in flat],
        in_specs=[pl.BlockSpec(memory_space=pltpu.HBM)] * len(flat) + [ANYWHERE] * len(after),
        scratch_shapes=[pltpu.SemaphoreType.DMA((pieces * len(flat),))],
        cost_estimate=cost(0, 2 * size),
        compiler_params=params(),
        name="hold",
    )(*(stay(array) for array in flat), *after)


def prepare_kernel(*refs):
    packed_ref, residual_ref, gain_ref, routes_ref, weights_ref, sems = refs[4:]
    for copy in load(refs[:4], refs[5:9], sems):
        copy.wait()
    row_count, width = residual_ref.shape
    experts = lax.axis_size("ep")
    lanes = packed_ref.shape[1] - width
    wide = residual_ref[...].astype(jnp.float32)
    mean = jnp.mean(wide * wide, axis=1, keepdims=True)
    packed_ref[:, :width] = (wide * lax.rsqrt(mean + 1e-06) * gain_ref[...]).astype(jnp.bfloat16)
    line = lax.broadcasted_iota(jnp.int32, (lanes, row_count), 0)
    expert = lax.rem(line, experts)
    weight = jnp.zeros(line.shape, jnp.float32)
    for k in range(routes_ref.shape[0]):
        weight += jnp.where(routes_ref[k : k + 1, :] == expert, weights_ref[k : k + 1, :], 0.0)
    high = weight.astype(jnp.bfloat16).astype(jnp.float32)
    low = (weight - high).astype(jnp.bfloat16).astype(jnp.float32)
    lowest = weight - high - low
    terms = jnp.where(
        line < experts,
        high,
        jnp.where(line < 2 * experts, low, jnp.where(line < 3 * experts, lowest, 0.0)),
    )
    at = lax.broadcasted_iota(jnp.int32, (row_count, row_count), 0)
    same = at == lax.broadcasted_iota(jnp.int32, (row_count, row_count), 1)
    turned = lax.dot_general(
        same.astype(jnp.bfloat16),
        terms.astype(jnp.bfloat16),
        (((1,), (1,)), ((), ())),
        preferred_element_type=jnp.float32,
    )
    packed_ref[:, width:] = turned.astype(jnp.bfloat16)


def stack_kernel(*refs):
    for i in range(refs[-1].shape[0]):
        refs[-1][i] = refs[i][...]


def relay_kernel(in_ref, *refs):
    refs[-1][...] = in_ref[...]


def ffn_kernel(takes, *refs):
    in_ref, down_ref = refs[4:6]
    near_ref, far_ref = refs[-2:]
    width = down_ref.shape[1]
    packed = jnp.concatenate(
        [refs[i][b] for i, start, stop in takes for b in range(start, stop)], axis=0
    )
    rows = packed[:, :width]
    terms = packed[:, width:].astype(jnp.float32)
    lane = lax.broadcasted_iota(jnp.int32, terms.shape, 1)
    mine = lax.rem(lane, lax.axis_size("ep")) == lax.axis_index("ep")
    weight = jnp.sum(jnp.where(mine, terms, 0.0), axis=1, keepdims=True)
    gate = jnp.dot(rows, in_ref[:width], preferred_element_type=jnp.float32)
    up = jnp.dot(rows, in_ref[width:], preferred_element_type=jnp.float32)
    hidden = (gate / (1.0 + jnp.exp(-gate)) * up).astype(jnp.bfloat16)
    out = jnp.dot(hidden, down_ref[...], preferred_element_type=jnp.float32)
    out = (out * weight).astype(jnp.bfloat16).reshape((2,) + near_ref.shape)
    near_ref[...] = out[0]
    far_ref[...] = out[1]


def pair_kernel(own_ref, other_ref, *refs):
    for i, out_ref in enumerate(refs[-own_ref.shape[0] :]):
        total = own_ref[i].astype(jnp.float32) + other_ref[i].astype(jnp.float32)
        out_ref[...] = total.astype(out_ref.dtype)


def add_kernel(own_ref, other_ref, out_ref):
    out_ref[...] = (own_ref[...] + other_ref[...].astype(jnp.float32)).astype(out_ref.dtype)


def total_kernel(residual_ref, *refs):
    total = residual_ref[...].astype(jnp.float32)
    for ref in refs[:-1]:
        total += ref[...].astype(jnp.float32)
    refs[-1][...] = total.astype(jnp.bfloat16)


def in_vmem(kernel, out_shape, name, arrays, after=(), mebibytes=4, cost_estimate=None):
    return pl.pallas_call(
        kernel,
        out_shape=out_shape,
        in_specs=[HERE] * len(arrays) + [ANYWHERE] * len(after),
        compiler_params=params(mebibytes),
        cost_estimate=cost_estimate,
        name=name,
    )(*arrays, *after)


def layer_gathered(attention, residual, norm_gain, routes, route_weights, expert_in, expert_down):
    row_count, width = residual.shape
    devices = lax.axis_size("ep")
    core, side, line = 1, 2, 4
    extra = -(-3 * devices // 128) * 128
    vmem = pltpu.VMEM
    one = (row_count, width)
    block = vmem((row_count, width + extra), jnp.bfloat16)

    def swap(value, bits):
        return lax.ppermute(value, "ep", [(i, i ^ bits) for i in range(devices)])

    def relay(value, after):
        return in_vmem(relay_kernel, vmem(value.shape, value.dtype), "relay", (value,), after)

    def stack(members, after=()):
        shape = vmem((len(members), row_count, width + extra), jnp.bfloat16)
        return in_vmem(stack_kernel, shape, "stack", members, after)

    packed = from_hbm(
        prepare_kernel,
        block,
        "prepare",
        (residual, norm_gain.reshape(1, -1), routes.T, route_weights.T),
    )
    third, second, first = (swap(packed, d * line) for d in (3, 2, 1))
    across = swap(packed, side)
    along = stack((second, third, first))
    along_side = swap(along, side)
    near = stack((second, third, first, packed, across))
    near_far = swap(near, core)
    held = hold((expert_in, expert_down), (along,))
    along_side_far = swap(relay(along_side, held[:1]), core)

    def ffn(near_takes, side_takes, after=()):
        takes = [(i, *t) for i in (0, 2) for t in near_takes]
        takes[len(near_takes) : len(near_takes)] = [(1, *t) for t in side_takes]
        takes += [(3, *t) for t in side_takes]
        return in_vmem(
            functools.partial(ffn_kernel, takes),
            [vmem((4,) + one, jnp.bfloat16)] * 2,
            "ffn",
            (near, along_side, near_far, along_side_far, *held),
            after,
            mebibytes=16,
            cost_estimate=cost(8 * row_count * 2 * sum(h.size for h in held), 2 * held[0].size),
        )

    def pair_sum(shapes, near_out, far_out, after=()):
        return in_vmem(pair_kernel, shapes, "pair_sum", (near_out, swap(far_out, core)), after)

    early_outs = ffn([(0, 2)], [(0, 2)])
    send = vmem(one, jnp.bfloat16)
    second_sum, third_keep, diagonal_sum, third_send = pair_sum(
        [send, vmem(one, jnp.float32), send, send], *early_outs
    )
    third_sum = in_vmem(add_kernel, send, "side_sum", (third_keep, swap(third_send, side)))
    back = [
        swap(second_sum, 2 * line),
        swap(diagonal_sum, 2 * line + side),
        swap(third_sum, 3 * line),
    ]
    attended = attend(*attention, (third_sum,))
    late_outs = ffn([(3, 5), (2, 3)], [(2, 3)], early_outs[:1])
    own, across_sum, first_sum, first_diagonal_sum = pair_sum(
        [vmem(one, jnp.float32), send, send, send], *late_outs, (second_sum,)
    )
    back += [
        swap(first_diagonal_sum, line + side),
        swap(first_sum, line),
        swap(across_sum, side),
    ]
    moe_out = in_vmem(
        total_kernel,
        jax.ShapeDtypeStruct(one, jnp.bfloat16),
        "total",
        (residual, own, *back),
    )
    return attended, moe_out


def expert_layer_routed(residual, norm_gain, routes, route_weights, expert_in, expert_down):
    row_count, top_count = routes.shape
    expert_count = expert_in.shape[0] * lax.axis_size("ep")
    capacity = min(row_count, max(2, 2 * row_count * top_count // expert_count))
    whole = lax.all_gather(residual, "tp", axis=1, tiled=True)
    width = whole.shape[1]
    half_width = residual.shape[1]
    normed = normalize(whole, norm_gain)
    flat_routes = routes.reshape(-1)
    hits = (flat_routes[:, None] == jnp.arange(expert_count)[None, :]).astype(jnp.int32)
    before = jnp.cumsum(hits, axis=0) - hits
    position = jnp.sum(before * hits, axis=1)
    slot_flat = flat_routes * capacity + position
    placed = (slot_flat[:, None] == jnp.arange(expert_count * capacity)[None, :]).astype(
        jnp.float32
    )
    placed = placed.reshape(row_count, top_count, expert_count * capacity)
    selector = jnp.sum(placed, axis=1).astype(jnp.bfloat16)
    buffer = jnp.einsum("rs,rd->sd", selector, normed, preferred_element_type=jnp.float32)
    buffer = buffer.astype(jnp.bfloat16).reshape(expert_count, capacity, width)
    arrived = lax.all_to_all(buffer, "ep", split_axis=0, concat_axis=0, tiled=True)
    sources = arrived.shape[0]
    flat_rows = arrived.reshape(sources * capacity, width)
    gate_act = jnp.dot(flat_rows, expert_in[0, 0], preferred_element_type=jnp.float32)
    up_act = jnp.dot(flat_rows, expert_in[0, 1], preferred_element_type=jnp.float32)
    hidden = (jax.nn.silu(gate_act) * up_act).astype(jnp.bfloat16)
    partial_value = jnp.dot(hidden, expert_down[0], preferred_element_type=jnp.float32)
    partial_value = partial_value.reshape(sources, capacity, width)
    summed = lax.psum_scatter(partial_value, "tp", scatter_dimension=2, tiled=True).astype(
        jnp.bfloat16
    )
    returned = lax.all_to_all(summed, "ep", split_axis=0, concat_axis=0, tiled=True)
    weighting = jnp.sum(placed * route_weights[:, :, None], axis=1)
    gathered_rows = returned.reshape(expert_count * capacity, half_width).astype(jnp.float32)
    combined = jnp.dot(weighting, gathered_rows, precision=lax.Precision.HIGHEST)
    return (residual.astype(jnp.float32) + combined).astype(jnp.bfloat16)


def per_device(
    queries,
    key_cache,
    value_cache,
    new_key,
    new_value,
    lengths,
    residual,
    norm_gain,
    routes,
    route_weights,
    expert_in,
    expert_down,
):
    devices = lax.axis_size("ep")
    dense = lax.axis_size("tp") == 1 and devices == 16
    attention = (queries, key_cache, value_cache, new_key, new_value, lengths)
    layer = (residual, norm_gain, routes, route_weights)
    if dense:
        return layer_gathered(attention, *layer, expert_in, expert_down)
    attended = attention_block(*attention)
    return (attended, expert_layer_routed(*layer, expert_in, expert_down))


def solution(mesh):
    in_specs = (
        P(("groups", "ep"), "tp", None),
        P(("groups", "ep"), None, "tp", None),
        P(("groups", "ep"), None, "tp", None),
        P(("groups", "ep"), "tp", None),
        P(("groups", "ep"), "tp", None),
        P(("groups", "ep")),
        P(("groups", "ep"), "tp"),
        P(),
        P(("groups", "ep"), None),
        P(("groups", "ep"), None),
        P("ep", None, None, "tp"),
        P("ep", "tp", None),
    )
    out_specs = (P(("groups", "ep"), "tp", None), P(("groups", "ep"), "tp"))
    return jax.shard_map(
        per_device, mesh=mesh, in_specs=in_specs, out_specs=out_specs, check_vma=False
    )
```

```python
import functools

import jax
import jax.numpy as jnp
from jax import lax
from jax.experimental import pallas as pl
from jax.experimental.pallas import tpu as pltpu
from jax.sharding import PartitionSpec as P


def attention_block(queries, key_cache, value_cache, new_key, new_value, lengths):
    rows_here, heads_here, head_size = queries.shape
    kv_here = key_cache.shape[2]
    slots_here = key_cache.shape[1]
    group = heads_here // kv_here
    scale = 1.0 / head_size**0.5
    grouped = queries.reshape(rows_here, kv_here, group, head_size)
    scores = (
        jnp.einsum("akgd,ackd->akgc", grouped, key_cache, preferred_element_type=jnp.float32)
        * scale
    )
    valid = (jnp.arange(slots_here)[None, :] < lengths[:, None])[:, None, None, :]
    scores = jnp.where(valid, scores, -1e30)
    own_score = (
        jnp.einsum("akgd,akd->akg", grouped, new_key, preferred_element_type=jnp.float32) * scale
    )
    largest = jnp.maximum(jnp.max(scores, axis=-1), own_score)
    cache_exp = jnp.exp(scores - largest[..., None])
    own_exp = jnp.exp(own_score - largest)
    total = jnp.sum(cache_exp, axis=-1) + own_exp
    cache_probs = (cache_exp / total[..., None]).astype(jnp.bfloat16)
    own_probs = (own_exp / total).astype(jnp.bfloat16)
    mixed = jnp.einsum(
        "akgc,ackd->akgd", cache_probs, value_cache, preferred_element_type=jnp.float32
    )
    mixed = (
        mixed
        + own_probs.astype(jnp.float32)[..., None] * new_value.astype(jnp.float32)[:, :, None, :]
    )
    return mixed.reshape(rows_here, heads_here, head_size).astype(jnp.bfloat16)


def normalize(residual, norm_gain):
    wide = residual.astype(jnp.float32)
    return (
        wide * lax.rsqrt(jnp.mean(wide * wide, axis=1, keepdims=True) + 1e-06) * norm_gain
    ).astype(jnp.bfloat16)


def load(sources, targets, sems):
    copies = [
        pltpu.make_async_copy(source, target, sems.at[i])
        for i, (source, target) in enumerate(zip(sources, targets))
    ]
    for copy in copies:
        copy.start()
    return copies


def stay(array):
    return pltpu.with_memory_space_constraint(array, pltpu.HBM)


HERE = pl.BlockSpec(memory_space=pltpu.VMEM)
ANYWHERE = pl.BlockSpec(memory_space=pl.ANY)


def params(mebibytes=4):
    return pltpu.CompilerParams(vmem_limit_bytes=mebibytes * 1024 * 1024)


def cost(flops=0, bytes_accessed=0):
    return pl.CostEstimate(flops=flops, bytes_accessed=bytes_accessed, transcendentals=0)


def from_hbm(kernel, out_shape, name, arrays, after=(), cost_estimate=None):
    return pl.pallas_call(
        kernel,
        out_shape=out_shape,
        in_specs=[pl.BlockSpec(memory_space=pltpu.HBM)] * len(arrays) + [ANYWHERE] * len(after),
        scratch_shapes=[
            (pltpu.VMEM if array.ndim > 1 else pltpu.SMEM)(array.shape, array.dtype)
            for array in arrays
        ]
        + [pltpu.SemaphoreType.DMA((len(arrays),))],
        compiler_params=params(),
        cost_estimate=cost_estimate,
        name=name,
    )(*(stay(array) for array in arrays), *after)


def attend_kernel(*refs):
    attended_ref = refs[-8]
    lengths_ref, queries_ref, keys_ref, values_ref, new_keys_ref, new_values_ref = refs[-7:-1]
    copies = load(refs[:6], refs[-7:-1], refs[-1])
    row_count, heads, head_size = queries_ref.shape
    kv_heads = new_keys_ref.shape[0] // row_count
    group = heads // kv_heads
    scale = 1.0 / head_size**0.5
    across = (((1,), (1,)), ((), ()))

    def grids(columns):
        shape = (heads, columns)
        head = lax.broadcasted_iota(jnp.int32, shape, 0) // group
        return head, lax.broadcasted_iota(jnp.int32, shape, 1)

    head, column = grids(keys_ref.shape[1])
    own_head, own_column = grids(new_keys_ref.shape[0])
    same_head = column % kv_heads == head
    slot = column // kv_heads
    for copy in copies:
        copy.wait()
    for a in range(row_count):
        query = queries_ref[a]
        scores = lax.dot_general(query, keys_ref[a], across, preferred_element_type=jnp.float32)
        scores = jnp.where(same_head & (slot < lengths_ref[a]), scores * scale, -1e30)
        own = lax.dot_general(
            query, new_keys_ref[...], across, preferred_element_type=jnp.float32
        )
        own = jnp.where(own_column == own_head + a * kv_heads, own * scale, -1e30)
        largest = jnp.maximum(
            jnp.max(scores, axis=1, keepdims=True), jnp.max(own, axis=1, keepdims=True)
        )
        scores = jnp.exp(scores - largest)
        own = jnp.exp(own - largest)
        total = jnp.sum(scores, axis=1, keepdims=True) + jnp.sum(own, axis=1, keepdims=True)
        mixed = jnp.dot(
            (scores / total).astype(jnp.bfloat16),
            values_ref[a],
            preferred_element_type=jnp.float32,
        ) + jnp.dot(
            (own / total).astype(jnp.bfloat16),
            new_values_ref[...],
            preferred_element_type=jnp.float32,
        )
        attended_ref[a] = mixed.astype(jnp.bfloat16)


def attend(queries, key_cache, value_cache, new_key, new_value, lengths, after):
    rows_here, slots_here, kv_here, head_size = key_cache.shape
    lines = (rows_here, slots_here * kv_here, head_size)
    arrays = (
        lengths,
        queries,
        key_cache.reshape(lines),
        value_cache.reshape(lines),
        new_key.reshape(-1, head_size),
        new_value.reshape(-1, head_size),
    )
    out_shape = jax.ShapeDtypeStruct(queries.shape, jnp.bfloat16)
    work = cost(0, 16 * key_cache.size * key_cache.dtype.itemsize)
    return from_hbm(attend_kernel, out_shape, "attend", arrays, after, work)


def hold_kernel(count, pieces, *refs):
    sources, targets, sems = refs[:count], refs[-1 - count : -1], refs[-1]
    starts, ends = [], []
    for source, target in zip(sources, targets):
        lines = source.shape[0] // pieces
        for i in range(pieces):
            starts.append(source.at[pl.ds(i * lines, lines)])
            ends.append(target.at[pl.ds(i * lines, lines)])
    for copy in load(starts, ends, sems):
        copy.wait()


def hold(arrays, after, pieces=4):
    flat = [array.reshape(-1, array.shape[-1]) for array in arrays]
    size = sum(array.size for array in flat)
    return pl.pallas_call(
        functools.partial(hold_kernel, len(flat), pieces),
        out_shape=[pltpu.VMEM(array.shape, array.dtype) for array in flat],
        in_specs=[pl.BlockSpec(memory_space=pltpu.HBM)] * len(flat) + [ANYWHERE] * len(after),
        scratch_shapes=[pltpu.SemaphoreType.DMA((pieces * len(flat),))],
        cost_estimate=cost(0, 2 * size),
        compiler_params=params(),
        name="hold",
    )(*(stay(array) for array in flat), *after)


def prepare_kernel(*refs):
    packed_ref, residual_ref, gain_ref, routes_ref, weights_ref, sems = refs[4:]
    for copy in load(refs[:4], refs[5:9], sems):
        copy.wait()
    row_count, width = residual_ref.shape
    experts = lax.axis_size("ep")
    lanes = packed_ref.shape[1] - width
    wide = residual_ref[...].astype(jnp.float32)
    mean = jnp.mean(wide * wide, axis=1, keepdims=True)
    packed_ref[:, :width] = (wide * lax.rsqrt(mean + 1e-06) * gain_ref[...]).astype(jnp.bfloat16)
    line = lax.broadcasted_iota(jnp.int32, (lanes, row_count), 0)
    expert = lax.rem(line, experts)
    weight = jnp.zeros(line.shape, jnp.float32)
    for k in range(routes_ref.shape[0]):
        weight += jnp.where(routes_ref[k : k + 1, :] == expert, weights_ref[k : k + 1, :], 0.0)
    high = weight.astype(jnp.bfloat16).astype(jnp.float32)
    low = (weight - high).astype(jnp.bfloat16).astype(jnp.float32)
    lowest = weight - high - low
    terms = jnp.where(
        line < experts,
        high,
        jnp.where(line < 2 * experts, low, jnp.where(line < 3 * experts, lowest, 0.0)),
    )
    at = lax.broadcasted_iota(jnp.int32, (row_count, row_count), 0)
    same = at == lax.broadcasted_iota(jnp.int32, (row_count, row_count), 1)
    turned = lax.dot_general(
        same.astype(jnp.bfloat16),
        terms.astype(jnp.bfloat16),
        (((1,), (1,)), ((), ())),
        preferred_element_type=jnp.float32,
    )
    packed_ref[:, width:] = turned.astype(jnp.bfloat16)


def stack_kernel(*refs):
    for i in range(refs[-1].shape[0]):
        refs[-1][i] = refs[i][...]


def relay_kernel(in_ref, *refs):
    refs[-1][...] = in_ref[...]


def ffn_kernel(takes, *refs):
    in_ref, down_ref = refs[4:6]
    near_ref, far_ref = refs[-2:]
    width = down_ref.shape[1]
    packed = jnp.concatenate(
        [refs[i][b] for i, start, stop in takes for b in range(start, stop)], axis=0
    )
    rows = packed[:, :width]
    terms = packed[:, width:].astype(jnp.float32)
    lane = lax.broadcasted_iota(jnp.int32, terms.shape, 1)
    mine = lax.rem(lane, lax.axis_size("ep")) == lax.axis_index("ep")
    weight = jnp.sum(jnp.where(mine, terms, 0.0), axis=1, keepdims=True)
    gate = jnp.dot(rows, in_ref[:width], preferred_element_type=jnp.float32)
    up = jnp.dot(rows, in_ref[width:], preferred_element_type=jnp.float32)
    hidden = (gate / (1.0 + jnp.exp(-gate)) * up).astype(jnp.bfloat16)
    out = jnp.dot(hidden, down_ref[...], preferred_element_type=jnp.float32)
    out = (out * weight).astype(jnp.bfloat16).reshape((2,) + near_ref.shape)
    near_ref[...] = out[0]
    far_ref[...] = out[1]


def pair_kernel(own_ref, other_ref, *refs):
    for i, out_ref in enumerate(refs[-own_ref.shape[0] :]):
        total = own_ref[i].astype(jnp.float32) + other_ref[i].astype(jnp.float32)
        out_ref[...] = total.astype(out_ref.dtype)


def add_kernel(own_ref, other_ref, out_ref):
    out_ref[...] = (own_ref[...] + other_ref[...].astype(jnp.float32)).astype(out_ref.dtype)


def total_kernel(residual_ref, *refs):
    total = residual_ref[...].astype(jnp.float32)
    for ref in refs[:-1]:
        total += ref[...].astype(jnp.float32)
    refs[-1][...] = total.astype(refs[-1].dtype)


def in_vmem(kernel, out_shape, name, arrays, after=(), mebibytes=4, cost_estimate=None):
    return pl.pallas_call(
        kernel,
        out_shape=out_shape,
        in_specs=[HERE] * len(arrays) + [ANYWHERE] * len(after),
        compiler_params=params(mebibytes),
        cost_estimate=cost_estimate,
        name=name,
    )(*arrays, *after)


def layer_gathered(attention, residual, norm_gain, routes, route_weights, expert_in, expert_down):
    row_count, width = residual.shape
    devices = lax.axis_size("ep")
    core, side, line = 1, 2, 4
    extra = -(-3 * devices // 128) * 128
    vmem = pltpu.VMEM
    one = (row_count, width)
    block = vmem((row_count, width + extra), jnp.bfloat16)

    def swap(value, bits):
        return lax.ppermute(value, "ep", [(i, i ^ bits) for i in range(devices)])

    def relay(value, after):
        return in_vmem(relay_kernel, vmem(value.shape, value.dtype), "relay", (value,), after)

    def stack(members, after=()):
        shape = vmem((len(members), row_count, width + extra), jnp.bfloat16)
        return in_vmem(stack_kernel, shape, "stack", members, after)

    packed = from_hbm(
        prepare_kernel,
        block,
        "prepare",
        (residual, norm_gain.reshape(1, -1), routes.T, route_weights.T),
    )
    third, second, first = (swap(packed, d * line) for d in (3, 2, 1))
    across = swap(packed, side)
    attended = attend(*attention, (packed,))
    along = stack((second, third, first), (stay(attended),))
    along_side = swap(along, side)
    near = stack((second, third, first, packed, across))
    near_far = swap(near, core)
    held = hold((expert_in, expert_down), (along,))
    along_side_far = swap(relay(along_side, held[:1]), core)

    def ffn(near_takes, side_takes, after=()):
        takes = [(i, *t) for i in (0, 2) for t in near_takes]
        takes[len(near_takes) : len(near_takes)] = [(1, *t) for t in side_takes]
        takes += [(3, *t) for t in side_takes]
        return in_vmem(
            functools.partial(ffn_kernel, takes),
            [vmem((4,) + one, jnp.bfloat16)] * 2,
            "ffn",
            (near, along_side, near_far, along_side_far, *held),
            after,
            mebibytes=16,
            cost_estimate=cost(8 * row_count * 2 * sum(h.size for h in held), 2 * held[0].size),
        )

    def pair_sum(shapes, near_out, far_out, after=()):
        return in_vmem(pair_kernel, shapes, "pair_sum", (near_out, swap(far_out, core)), after)

    early_outs = ffn([(0, 2)], [(0, 2)])
    send = vmem(one, jnp.bfloat16)
    second_sum, third_keep, diagonal_sum, third_send = pair_sum(
        [send, vmem(one, jnp.float32), send, send], *early_outs
    )
    third_sum = in_vmem(add_kernel, send, "side_sum", (third_keep, swap(third_send, side)))
    partial_sum = in_vmem(
        total_kernel,
        vmem(one, jnp.float32),
        "partial_sum",
        (
            residual,
            swap(third_sum, 3 * line),
            swap(second_sum, 2 * line),
            swap(diagonal_sum, 2 * line + side),
        ),
    )
    late_outs = ffn([(3, 5), (2, 3)], [(2, 3)], early_outs[:1])
    own, across_sum, first_sum, first_diagonal_sum = pair_sum(
        [vmem(one, jnp.float32), send, send, send], *late_outs, (third_sum,)
    )
    moe_out = in_vmem(
        total_kernel,
        jax.ShapeDtypeStruct(one, jnp.bfloat16),
        "total",
        (
            partial_sum,
            own,
            swap(first_diagonal_sum, line + side),
            swap(first_sum, line),
            swap(across_sum, side),
        ),
    )
    return attended, moe_out


def expert_layer_routed(residual, norm_gain, routes, route_weights, expert_in, expert_down):
    row_count, top_count = routes.shape
    expert_count = expert_in.shape[0] * lax.axis_size("ep")
    capacity = min(row_count, max(2, 2 * row_count * top_count // expert_count))
    whole = lax.all_gather(residual, "tp", axis=1, tiled=True)
    width = whole.shape[1]
    half_width = residual.shape[1]
    normed = normalize(whole, norm_gain)
    flat_routes = routes.reshape(-1)
    hits = (flat_routes[:, None] == jnp.arange(expert_count)[None, :]).astype(jnp.int32)
    before = jnp.cumsum(hits, axis=0) - hits
    position = jnp.sum(before * hits, axis=1)
    slot_flat = flat_routes * capacity + position
    placed = (slot_flat[:, None] == jnp.arange(expert_count * capacity)[None, :]).astype(
        jnp.float32
    )
    placed = placed.reshape(row_count, top_count, expert_count * capacity)
    selector = jnp.sum(placed, axis=1).astype(jnp.bfloat16)
    buffer = jnp.einsum("rs,rd->sd", selector, normed, preferred_element_type=jnp.float32)
    buffer = buffer.astype(jnp.bfloat16).reshape(expert_count, capacity, width)
    arrived = lax.all_to_all(buffer, "ep", split_axis=0, concat_axis=0, tiled=True)
    sources = arrived.shape[0]
    flat_rows = arrived.reshape(sources * capacity, width)
    gate_act = jnp.dot(flat_rows, expert_in[0, 0], preferred_element_type=jnp.float32)
    up_act = jnp.dot(flat_rows, expert_in[0, 1], preferred_element_type=jnp.float32)
    hidden = (jax.nn.silu(gate_act) * up_act).astype(jnp.bfloat16)
    partial_value = jnp.dot(hidden, expert_down[0], preferred_element_type=jnp.float32)
    partial_value = partial_value.reshape(sources, capacity, width)
    summed = lax.psum_scatter(partial_value, "tp", scatter_dimension=2, tiled=True).astype(
        jnp.bfloat16
    )
    returned = lax.all_to_all(summed, "ep", split_axis=0, concat_axis=0, tiled=True)
    weighting = jnp.sum(placed * route_weights[:, :, None], axis=1)
    gathered_rows = returned.reshape(expert_count * capacity, half_width).astype(jnp.float32)
    combined = jnp.dot(weighting, gathered_rows, precision=lax.Precision.HIGHEST)
    return (residual.astype(jnp.float32) + combined).astype(jnp.bfloat16)


def per_device(
    queries,
    key_cache,
    value_cache,
    new_key,
    new_value,
    lengths,
    residual,
    norm_gain,
    routes,
    route_weights,
    expert_in,
    expert_down,
):
    devices = lax.axis_size("ep")
    dense = lax.axis_size("tp") == 1 and devices == 16
    attention = (queries, key_cache, value_cache, new_key, new_value, lengths)
    layer = (residual, norm_gain, routes, route_weights)
    if dense:
        return layer_gathered(attention, *layer, expert_in, expert_down)
    attended = attention_block(*attention)
    return (attended, expert_layer_routed(*layer, expert_in, expert_down))


def solution(mesh):
    in_specs = (
        P(("groups", "ep"), "tp", None),
        P(("groups", "ep"), None, "tp", None),
        P(("groups", "ep"), None, "tp", None),
        P(("groups", "ep"), "tp", None),
        P(("groups", "ep"), "tp", None),
        P(("groups", "ep")),
        P(("groups", "ep"), "tp"),
        P(),
        P(("groups", "ep"), None),
        P(("groups", "ep"), None),
        P("ep", None, None, "tp"),
        P("ep", "tp", None),
    )
    out_specs = (P(("groups", "ep"), "tp", None), P(("groups", "ep"), "tp"))
    return jax.shard_map(
        per_device, mesh=mesh, in_specs=in_specs, out_specs=out_specs, check_vma=False
    )
```

```python
import functools

import jax
import jax.numpy as jnp
from jax import lax
from jax.experimental import pallas as pl
from jax.experimental.pallas import tpu as pltpu
from jax.sharding import PartitionSpec as P


def attention_block(queries, key_cache, value_cache, new_key, new_value, lengths):
    rows_here, heads_here, head_size = queries.shape
    kv_here = key_cache.shape[2]
    slots_here = key_cache.shape[1]
    group = heads_here // kv_here
    scale = 1.0 / head_size**0.5
    grouped = queries.reshape(rows_here, kv_here, group, head_size)
    scores = (
        jnp.einsum("akgd,ackd->akgc", grouped, key_cache, preferred_element_type=jnp.float32)
        * scale
    )
    valid = (jnp.arange(slots_here)[None, :] < lengths[:, None])[:, None, None, :]
    scores = jnp.where(valid, scores, -1e30)
    own_score = (
        jnp.einsum("akgd,akd->akg", grouped, new_key, preferred_element_type=jnp.float32) * scale
    )
    largest = jnp.maximum(jnp.max(scores, axis=-1), own_score)
    cache_exp = jnp.exp(scores - largest[..., None])
    own_exp = jnp.exp(own_score - largest)
    total = jnp.sum(cache_exp, axis=-1) + own_exp
    cache_probs = (cache_exp / total[..., None]).astype(jnp.bfloat16)
    own_probs = (own_exp / total).astype(jnp.bfloat16)
    mixed = jnp.einsum(
        "akgc,ackd->akgd", cache_probs, value_cache, preferred_element_type=jnp.float32
    )
    mixed = (
        mixed
        + own_probs.astype(jnp.float32)[..., None] * new_value.astype(jnp.float32)[:, :, None, :]
    )
    return mixed.reshape(rows_here, heads_here, head_size).astype(jnp.bfloat16)


def normalize(residual, norm_gain):
    wide = residual.astype(jnp.float32)
    return (
        wide * lax.rsqrt(jnp.mean(wide * wide, axis=1, keepdims=True) + 1e-06) * norm_gain
    ).astype(jnp.bfloat16)


def load(sources, targets, sems):
    copies = [
        pltpu.make_async_copy(source, target, sems.at[i])
        for i, (source, target) in enumerate(zip(sources, targets))
    ]
    for copy in copies:
        copy.start()
    return copies


def stay(array):
    return pltpu.with_memory_space_constraint(array, pltpu.HBM)


HERE = pl.BlockSpec(memory_space=pltpu.VMEM)
ANYWHERE = pl.BlockSpec(memory_space=pl.ANY)


def params(mebibytes=4):
    return pltpu.CompilerParams(vmem_limit_bytes=mebibytes * 1024 * 1024)


def cost(flops=0, bytes_accessed=0):
    return pl.CostEstimate(flops=flops, bytes_accessed=bytes_accessed, transcendentals=0)


def from_hbm(kernel, out_shape, name, arrays, after=(), cost_estimate=None):
    return pl.pallas_call(
        kernel,
        out_shape=out_shape,
        in_specs=[pl.BlockSpec(memory_space=pltpu.HBM)] * len(arrays) + [ANYWHERE] * len(after),
        scratch_shapes=[
            (pltpu.VMEM if array.ndim > 1 else pltpu.SMEM)(array.shape, array.dtype)
            for array in arrays
        ]
        + [pltpu.SemaphoreType.DMA((len(arrays),))],
        compiler_params=params(),
        cost_estimate=cost_estimate,
        name=name,
    )(*(stay(array) for array in arrays), *after)


def attend_kernel(*refs):
    attended_ref = refs[-8]
    lengths_ref, queries_ref, keys_ref, values_ref, new_keys_ref, new_values_ref = refs[-7:-1]
    copies = load(refs[:6], refs[-7:-1], refs[-1])
    row_count, heads, head_size = queries_ref.shape
    kv_heads = new_keys_ref.shape[0] // row_count
    group = heads // kv_heads
    scale = 1.0 / head_size**0.5
    across = (((1,), (1,)), ((), ()))

    def grids(columns):
        shape = (heads, columns)
        head = lax.broadcasted_iota(jnp.int32, shape, 0) // group
        return head, lax.broadcasted_iota(jnp.int32, shape, 1)

    head, column = grids(keys_ref.shape[1])
    own_head, own_column = grids(new_keys_ref.shape[0])
    same_head = column % kv_heads == head
    slot = column // kv_heads
    for copy in copies:
        copy.wait()
    for a in range(row_count):
        query = queries_ref[a]
        scores = lax.dot_general(query, keys_ref[a], across, preferred_element_type=jnp.float32)
        scores = jnp.where(same_head & (slot < lengths_ref[a]), scores * scale, -1e30)
        own = lax.dot_general(
            query, new_keys_ref[...], across, preferred_element_type=jnp.float32
        )
        own = jnp.where(own_column == own_head + a * kv_heads, own * scale, -1e30)
        largest = jnp.maximum(
            jnp.max(scores, axis=1, keepdims=True), jnp.max(own, axis=1, keepdims=True)
        )
        scores = jnp.exp(scores - largest)
        own = jnp.exp(own - largest)
        total = jnp.sum(scores, axis=1, keepdims=True) + jnp.sum(own, axis=1, keepdims=True)
        mixed = jnp.dot(
            (scores / total).astype(jnp.bfloat16),
            values_ref[a],
            preferred_element_type=jnp.float32,
        ) + jnp.dot(
            (own / total).astype(jnp.bfloat16),
            new_values_ref[...],
            preferred_element_type=jnp.float32,
        )
        attended_ref[a] = mixed.astype(jnp.bfloat16)


def attend(queries, key_cache, value_cache, new_key, new_value, lengths, after):
    rows_here, slots_here, kv_here, head_size = key_cache.shape
    lines = (rows_here, slots_here * kv_here, head_size)
    arrays = (
        lengths,
        queries,
        key_cache.reshape(lines),
        value_cache.reshape(lines),
        new_key.reshape(-1, head_size),
        new_value.reshape(-1, head_size),
    )
    out_shape = jax.ShapeDtypeStruct(queries.shape, jnp.bfloat16)
    work = cost(0, 16 * key_cache.size * key_cache.dtype.itemsize)
    return from_hbm(attend_kernel, out_shape, "attend", arrays, after, work)


def hold_kernel(count, pieces, *refs):
    sources, targets, sems = refs[:count], refs[-1 - count : -1], refs[-1]
    starts, ends = [], []
    for source, target in zip(sources, targets):
        lines = source.shape[0] // pieces
        for i in range(pieces):
            starts.append(source.at[pl.ds(i * lines, lines)])
            ends.append(target.at[pl.ds(i * lines, lines)])
    for copy in load(starts, ends, sems):
        copy.wait()


def hold(arrays, after, pieces=4):
    flat = [array.reshape(-1, array.shape[-1]) for array in arrays]
    size = sum(array.size for array in flat)
    return pl.pallas_call(
        functools.partial(hold_kernel, len(flat), pieces),
        out_shape=[pltpu.VMEM(array.shape, array.dtype) for array in flat],
        in_specs=[pl.BlockSpec(memory_space=pltpu.HBM)] * len(flat) + [ANYWHERE] * len(after),
        scratch_shapes=[pltpu.SemaphoreType.DMA((pieces * len(flat),))],
        cost_estimate=cost(0, 2 * size),
        compiler_params=params(),
        name="hold",
    )(*(stay(array) for array in flat), *after)


def prepare_kernel(*refs):
    packed_ref, residual_ref, gain_ref, routes_ref, weights_ref, sems = refs[4:]
    for copy in load(refs[:4], refs[5:9], sems):
        copy.wait()
    row_count, width = residual_ref.shape
    experts = lax.axis_size("ep")
    lanes = packed_ref.shape[1] - width
    wide = residual_ref[...].astype(jnp.float32)
    mean = jnp.mean(wide * wide, axis=1, keepdims=True)
    packed_ref[:, :width] = (wide * lax.rsqrt(mean + 1e-06) * gain_ref[...]).astype(jnp.bfloat16)
    line = lax.broadcasted_iota(jnp.int32, (lanes, row_count), 0)
    expert = lax.rem(line, experts)
    weight = jnp.zeros(line.shape, jnp.float32)
    for k in range(routes_ref.shape[0]):
        weight += jnp.where(routes_ref[k : k + 1, :] == expert, weights_ref[k : k + 1, :], 0.0)
    high = weight.astype(jnp.bfloat16).astype(jnp.float32)
    low = (weight - high).astype(jnp.bfloat16).astype(jnp.float32)
    lowest = weight - high - low
    terms = jnp.where(
        line < experts,
        high,
        jnp.where(line < 2 * experts, low, jnp.where(line < 3 * experts, lowest, 0.0)),
    )
    at = lax.broadcasted_iota(jnp.int32, (row_count, row_count), 0)
    same = at == lax.broadcasted_iota(jnp.int32, (row_count, row_count), 1)
    turned = lax.dot_general(
        same.astype(jnp.bfloat16),
        terms.astype(jnp.bfloat16),
        (((1,), (1,)), ((), ())),
        preferred_element_type=jnp.float32,
    )
    packed_ref[:, width:] = turned.astype(jnp.bfloat16)


def stack_kernel(*refs):
    for i in range(refs[-1].shape[0]):
        refs[-1][i] = refs[i][...]


def relay_kernel(in_ref, *refs):
    refs[-1][...] = in_ref[...]


def ffn_kernel(takes, *refs):
    in_ref, down_ref = refs[4:6]
    near_ref, far_ref = refs[-2:]
    width = down_ref.shape[1]
    packed = jnp.concatenate(
        [refs[i][b] for i, start, stop in takes for b in range(start, stop)], axis=0
    )
    rows = packed[:, :width]
    terms = packed[:, width:].astype(jnp.float32)
    lane = lax.broadcasted_iota(jnp.int32, terms.shape, 1)
    mine = lax.rem(lane, lax.axis_size("ep")) == lax.axis_index("ep")
    weight = jnp.sum(jnp.where(mine, terms, 0.0), axis=1, keepdims=True)
    gate = jnp.dot(rows, in_ref[:width], preferred_element_type=jnp.float32)
    up = jnp.dot(rows, in_ref[width:], preferred_element_type=jnp.float32)
    hidden = (gate / (1.0 + jnp.exp(-gate)) * up).astype(jnp.bfloat16)
    out = jnp.dot(hidden, down_ref[...], preferred_element_type=jnp.float32)
    out = (out * weight).astype(jnp.bfloat16).reshape((2,) + near_ref.shape)
    near_ref[...] = out[0]
    far_ref[...] = out[1]


def pair_kernel(own_ref, other_ref, *refs):
    keep_ref, send_ref = refs[-2:]
    half = keep_ref.shape[0]
    keep_ref[...] = own_ref[:half].astype(jnp.float32) + other_ref[:half].astype(jnp.float32)
    send = own_ref[half:].astype(jnp.float32) + other_ref[half:].astype(jnp.float32)
    send_ref[...] = send.astype(jnp.bfloat16)


def square_kernel(own_ref, other_ref, *out_refs):
    for i, out_ref in enumerate(out_refs):
        total = own_ref[i] + other_ref[i].astype(jnp.float32)
        out_ref[...] = total.astype(out_ref.dtype)


def total_kernel(residual_ref, *refs):
    total = residual_ref[...].astype(jnp.float32)
    for ref in refs[:-1]:
        total += ref[...].astype(jnp.float32)
    refs[-1][...] = total.astype(jnp.bfloat16)


def in_vmem(kernel, out_shape, name, arrays, after=(), mebibytes=4, cost_estimate=None):
    return pl.pallas_call(
        kernel,
        out_shape=out_shape,
        in_specs=[HERE] * len(arrays) + [ANYWHERE] * len(after),
        compiler_params=params(mebibytes),
        cost_estimate=cost_estimate,
        name=name,
    )(*arrays, *after)


def layer_gathered(attention, residual, norm_gain, routes, route_weights, expert_in, expert_down):
    row_count, width = residual.shape
    devices = lax.axis_size("ep")
    core, side, line = 1, 2, 4
    extra = -(-3 * devices // 128) * 128
    vmem = pltpu.VMEM
    one = (row_count, width)
    block = vmem((row_count, width + extra), jnp.bfloat16)

    def swap(value, bits):
        return lax.ppermute(value, "ep", [(i, i ^ bits) for i in range(devices)])

    def relay(value, after):
        return in_vmem(relay_kernel, vmem(value.shape, value.dtype), "relay", (value,), after)

    def stack(members, after=()):
        shape = vmem((len(members), row_count, width + extra), jnp.bfloat16)
        return in_vmem(stack_kernel, shape, "stack", members, after)

    packed = from_hbm(
        prepare_kernel,
        block,
        "prepare",
        (residual, norm_gain.reshape(1, -1), routes.T, route_weights.T),
    )
    third, second, first = (swap(packed, d * line) for d in (3, 2, 1))
    across, diagonal = swap(packed, side), swap(packed, line + side)
    along = stack((second, third))
    along_side = swap(along, side)
    near = stack((second, third, packed, across, first, diagonal))
    near_far = swap(near, core)
    held = hold((expert_in, expert_down), (along,))
    along_side_far = swap(relay(along_side, held[:1]), core)

    def ffn(near_takes, side_takes, after=()):
        takes = [(i, *t) for i in (0, 2) for t in near_takes]
        takes[len(near_takes) : len(near_takes)] = [(1, *t) for t in side_takes]
        takes += [(3, *t) for t in side_takes]
        return in_vmem(
            functools.partial(ffn_kernel, takes),
            [vmem((4,) + one, jnp.bfloat16)] * 2,
            "ffn",
            (near, along_side, near_far, along_side_far, *held),
            after,
            mebibytes=16,
            cost_estimate=cost(8 * row_count * 2 * sum(h.size for h in held), 2 * held[0].size),
        )

    def pair_sum(near_out, far_out, after=()):
        shapes = [vmem((2,) + one, jnp.float32), vmem((2,) + one, jnp.bfloat16)]
        return in_vmem(pair_kernel, shapes, "pair_sum", (near_out, swap(far_out, core)), after)

    early_outs = ffn([(0, 2)], [(0, 2)])
    early_keep, early_send = pair_sum(*early_outs)
    early_sums = in_vmem(
        square_kernel,
        [vmem(one, jnp.bfloat16)] * 2,
        "square_sum",
        (early_keep, swap(early_send, side)),
    )
    attended = attend(*attention, tuple(early_sums))
    back = [swap(early_sums[1], 3 * line), swap(early_sums[0], 2 * line)]
    late_outs = ffn([(2, 6)], [], early_outs[:1])
    late_keep, late_send = pair_sum(*late_outs)
    own, across_sum = in_vmem(
        square_kernel,
        [vmem(one, jnp.float32), vmem(one, jnp.bfloat16)],
        "line_sum",
        (late_keep, swap(late_send, line)),
    )
    moe_out = in_vmem(
        total_kernel,
        jax.ShapeDtypeStruct(one, jnp.bfloat16),
        "total",
        (residual, own, *back, swap(across_sum, side)),
    )
    return attended, moe_out


def expert_layer_routed(residual, norm_gain, routes, route_weights, expert_in, expert_down):
    row_count, top_count = routes.shape
    expert_count = expert_in.shape[0] * lax.axis_size("ep")
    capacity = min(row_count, max(2, 2 * row_count * top_count // expert_count))
    whole = lax.all_gather(residual, "tp", axis=1, tiled=True)
    width = whole.shape[1]
    half_width = residual.shape[1]
    normed = normalize(whole, norm_gain)
    flat_routes = routes.reshape(-1)
    hits = (flat_routes[:, None] == jnp.arange(expert_count)[None, :]).astype(jnp.int32)
    before = jnp.cumsum(hits, axis=0) - hits
    position = jnp.sum(before * hits, axis=1)
    slot_flat = flat_routes * capacity + position
    placed = (slot_flat[:, None] == jnp.arange(expert_count * capacity)[None, :]).astype(
        jnp.float32
    )
    placed = placed.reshape(row_count, top_count, expert_count * capacity)
    selector = jnp.sum(placed, axis=1).astype(jnp.bfloat16)
    buffer = jnp.einsum("rs,rd->sd", selector, normed, preferred_element_type=jnp.float32)
    buffer = buffer.astype(jnp.bfloat16).reshape(expert_count, capacity, width)
    arrived = lax.all_to_all(buffer, "ep", split_axis=0, concat_axis=0, tiled=True)
    sources = arrived.shape[0]
    flat_rows = arrived.reshape(sources * capacity, width)
    gate_act = jnp.dot(flat_rows, expert_in[0, 0], preferred_element_type=jnp.float32)
    up_act = jnp.dot(flat_rows, expert_in[0, 1], preferred_element_type=jnp.float32)
    hidden = (jax.nn.silu(gate_act) * up_act).astype(jnp.bfloat16)
    partial_value = jnp.dot(hidden, expert_down[0], preferred_element_type=jnp.float32)
    partial_value = partial_value.reshape(sources, capacity, width)
    summed = lax.psum_scatter(partial_value, "tp", scatter_dimension=2, tiled=True).astype(
        jnp.bfloat16
    )
    returned = lax.all_to_all(summed, "ep", split_axis=0, concat_axis=0, tiled=True)
    weighting = jnp.sum(placed * route_weights[:, :, None], axis=1)
    gathered_rows = returned.reshape(expert_count * capacity, half_width).astype(jnp.float32)
    combined = jnp.dot(weighting, gathered_rows, precision=lax.Precision.HIGHEST)
    return (residual.astype(jnp.float32) + combined).astype(jnp.bfloat16)


def per_device(
    queries,
    key_cache,
    value_cache,
    new_key,
    new_value,
    lengths,
    residual,
    norm_gain,
    routes,
    route_weights,
    expert_in,
    expert_down,
):
    devices = lax.axis_size("ep")
    dense = lax.axis_size("tp") == 1 and devices == 16
    attention = (queries, key_cache, value_cache, new_key, new_value, lengths)
    layer = (residual, norm_gain, routes, route_weights)
    if dense:
        return layer_gathered(attention, *layer, expert_in, expert_down)
    attended = attention_block(*attention)
    return (attended, expert_layer_routed(*layer, expert_in, expert_down))


def solution(mesh):
    in_specs = (
        P(("groups", "ep"), "tp", None),
        P(("groups", "ep"), None, "tp", None),
        P(("groups", "ep"), None, "tp", None),
        P(("groups", "ep"), "tp", None),
        P(("groups", "ep"), "tp", None),
        P(("groups", "ep")),
        P(("groups", "ep"), "tp"),
        P(),
        P(("groups", "ep"), None),
        P(("groups", "ep"), None),
        P("ep", None, None, "tp"),
        P("ep", "tp", None),
    )
    out_specs = (P(("groups", "ep"), "tp", None), P(("groups", "ep"), "tp"))
    return jax.shard_map(
        per_device, mesh=mesh, in_specs=in_specs, out_specs=out_specs, check_vma=False
    )
```

```python
import functools

import jax
import jax.numpy as jnp
from jax import lax
from jax.experimental import pallas as pl
from jax.experimental.pallas import tpu as pltpu
from jax.sharding import PartitionSpec as P


def attention_block(queries, key_cache, value_cache, new_key, new_value, lengths):
    rows_here, heads_here, head_size = queries.shape
    kv_here = key_cache.shape[2]
    slots_here = key_cache.shape[1]
    group = heads_here // kv_here
    scale = 1.0 / head_size**0.5
    grouped = queries.reshape(rows_here, kv_here, group, head_size)
    scores = (
        jnp.einsum("akgd,ackd->akgc", grouped, key_cache, preferred_element_type=jnp.float32)
        * scale
    )
    valid = (jnp.arange(slots_here)[None, :] < lengths[:, None])[:, None, None, :]
    scores = jnp.where(valid, scores, -1e30)
    own_score = (
        jnp.einsum("akgd,akd->akg", grouped, new_key, preferred_element_type=jnp.float32) * scale
    )
    largest = jnp.maximum(jnp.max(scores, axis=-1), own_score)
    cache_exp = jnp.exp(scores - largest[..., None])
    own_exp = jnp.exp(own_score - largest)
    total = jnp.sum(cache_exp, axis=-1) + own_exp
    cache_probs = (cache_exp / total[..., None]).astype(jnp.bfloat16)
    own_probs = (own_exp / total).astype(jnp.bfloat16)
    mixed = jnp.einsum(
        "akgc,ackd->akgd", cache_probs, value_cache, preferred_element_type=jnp.float32
    )
    mixed = (
        mixed
        + own_probs.astype(jnp.float32)[..., None] * new_value.astype(jnp.float32)[:, :, None, :]
    )
    return mixed.reshape(rows_here, heads_here, head_size).astype(jnp.bfloat16)


def normalize(residual, norm_gain):
    wide = residual.astype(jnp.float32)
    return (
        wide * lax.rsqrt(jnp.mean(wide * wide, axis=1, keepdims=True) + 1e-06) * norm_gain
    ).astype(jnp.bfloat16)


def load(sources, targets, sems):
    copies = [
        pltpu.make_async_copy(source, target, sems.at[i])
        for i, (source, target) in enumerate(zip(sources, targets))
    ]
    for copy in copies:
        copy.start()
    return copies


def stay(array):
    return pltpu.with_memory_space_constraint(array, pltpu.HBM)


HERE = pl.BlockSpec(memory_space=pltpu.VMEM)
ANYWHERE = pl.BlockSpec(memory_space=pl.ANY)


def params(mebibytes=4):
    return pltpu.CompilerParams(vmem_limit_bytes=mebibytes * 1024 * 1024)


def cost(flops=0, bytes_accessed=0):
    return pl.CostEstimate(flops=flops, bytes_accessed=bytes_accessed, transcendentals=0)


def from_hbm(kernel, out_shape, name, arrays, after=(), cost_estimate=None):
    return pl.pallas_call(
        kernel,
        out_shape=out_shape,
        in_specs=[pl.BlockSpec(memory_space=pltpu.HBM)] * len(arrays) + [ANYWHERE] * len(after),
        scratch_shapes=[
            (pltpu.VMEM if array.ndim > 1 else pltpu.SMEM)(array.shape, array.dtype)
            for array in arrays
        ]
        + [pltpu.SemaphoreType.DMA((len(arrays),))],
        compiler_params=params(),
        cost_estimate=cost_estimate,
        name=name,
    )(*(stay(array) for array in arrays), *after)


def attend_kernel(*refs):
    attended_ref = refs[-8]
    lengths_ref, queries_ref, keys_ref, values_ref, new_keys_ref, new_values_ref = refs[-7:-1]
    copies = load(refs[:6], refs[-7:-1], refs[-1])
    row_count, heads, head_size = queries_ref.shape
    kv_heads = new_keys_ref.shape[0] // row_count
    group = heads // kv_heads
    scale = 1.0 / head_size**0.5
    across = (((1,), (1,)), ((), ()))

    def grids(columns):
        shape = (heads, columns)
        head = lax.broadcasted_iota(jnp.int32, shape, 0) // group
        return head, lax.broadcasted_iota(jnp.int32, shape, 1)

    head, column = grids(keys_ref.shape[1])
    own_head, own_column = grids(new_keys_ref.shape[0])
    same_head = column % kv_heads == head
    slot = column // kv_heads
    for copy in copies:
        copy.wait()
    for a in range(row_count):
        query = queries_ref[a]
        scores = lax.dot_general(query, keys_ref[a], across, preferred_element_type=jnp.float32)
        scores = jnp.where(same_head & (slot < lengths_ref[a]), scores * scale, -1e30)
        own = lax.dot_general(
            query, new_keys_ref[...], across, preferred_element_type=jnp.float32
        )
        own = jnp.where(own_column == own_head + a * kv_heads, own * scale, -1e30)
        largest = jnp.maximum(
            jnp.max(scores, axis=1, keepdims=True), jnp.max(own, axis=1, keepdims=True)
        )
        scores = jnp.exp(scores - largest)
        own = jnp.exp(own - largest)
        total = jnp.sum(scores, axis=1, keepdims=True) + jnp.sum(own, axis=1, keepdims=True)
        mixed = jnp.dot(
            (scores / total).astype(jnp.bfloat16),
            values_ref[a],
            preferred_element_type=jnp.float32,
        ) + jnp.dot(
            (own / total).astype(jnp.bfloat16),
            new_values_ref[...],
            preferred_element_type=jnp.float32,
        )
        attended_ref[a] = mixed.astype(jnp.bfloat16)


def attend(queries, key_cache, value_cache, new_key, new_value, lengths, after):
    rows_here, slots_here, kv_here, head_size = key_cache.shape
    lines = (rows_here, slots_here * kv_here, head_size)
    arrays = (
        lengths,
        queries,
        key_cache.reshape(lines),
        value_cache.reshape(lines),
        new_key.reshape(-1, head_size),
        new_value.reshape(-1, head_size),
    )
    out_shape = jax.ShapeDtypeStruct(queries.shape, jnp.bfloat16)
    work = cost(0, 16 * key_cache.size * key_cache.dtype.itemsize)
    return from_hbm(attend_kernel, out_shape, "attend", arrays, after, work)


def hold_kernel(count, pieces, *refs):
    sources, targets, sems = refs[:count], refs[-1 - count : -1], refs[-1]
    starts, ends = [], []
    for source, target in zip(sources, targets):
        lines = source.shape[0] // pieces
        for i in range(pieces):
            starts.append(source.at[pl.ds(i * lines, lines)])
            ends.append(target.at[pl.ds(i * lines, lines)])
    for copy in load(starts, ends, sems):
        copy.wait()


def hold(arrays, after, pieces=4):
    flat = [array.reshape(-1, array.shape[-1]) for array in arrays]
    size = sum(array.size for array in flat)
    return pl.pallas_call(
        functools.partial(hold_kernel, len(flat), pieces),
        out_shape=[pltpu.VMEM(array.shape, array.dtype) for array in flat],
        in_specs=[pl.BlockSpec(memory_space=pltpu.HBM)] * len(flat) + [ANYWHERE] * len(after),
        scratch_shapes=[pltpu.SemaphoreType.DMA((pieces * len(flat),))],
        cost_estimate=cost(0, 2 * size),
        compiler_params=params(),
        name="hold",
    )(*(stay(array) for array in flat), *after)


def prepare_kernel(*refs):
    packed_ref, residual_ref, gain_ref, routes_ref, weights_ref, sems = refs[4:]
    for copy in load(refs[:4], refs[5:9], sems):
        copy.wait()
    row_count, width = residual_ref.shape
    experts = lax.axis_size("ep")
    lanes = packed_ref.shape[1] - width
    wide = residual_ref[...].astype(jnp.float32)
    mean = jnp.mean(wide * wide, axis=1, keepdims=True)
    packed_ref[:, :width] = (wide * lax.rsqrt(mean + 1e-06) * gain_ref[...]).astype(jnp.bfloat16)
    line = lax.broadcasted_iota(jnp.int32, (lanes, row_count), 0)
    expert = lax.rem(line, experts)
    weight = jnp.zeros(line.shape, jnp.float32)
    for k in range(routes_ref.shape[0]):
        weight += jnp.where(routes_ref[k : k + 1, :] == expert, weights_ref[k : k + 1, :], 0.0)
    high = weight.astype(jnp.bfloat16).astype(jnp.float32)
    low = (weight - high).astype(jnp.bfloat16).astype(jnp.float32)
    lowest = weight - high - low
    terms = jnp.where(
        line < experts,
        high,
        jnp.where(line < 2 * experts, low, jnp.where(line < 3 * experts, lowest, 0.0)),
    )
    at = lax.broadcasted_iota(jnp.int32, (row_count, row_count), 0)
    same = at == lax.broadcasted_iota(jnp.int32, (row_count, row_count), 1)
    turned = lax.dot_general(
        same.astype(jnp.bfloat16),
        terms.astype(jnp.bfloat16),
        (((1,), (1,)), ((), ())),
        preferred_element_type=jnp.float32,
    )
    packed_ref[:, width:] = turned.astype(jnp.bfloat16)


def stack_kernel(*refs):
    for i in range(refs[-1].shape[0]):
        refs[-1][i] = refs[i][...]


def relay_kernel(in_ref, *refs):
    refs[-1][...] = in_ref[...]


def ffn_kernel(takes, *refs):
    in_ref, down_ref = refs[4:6]
    near_ref, far_ref = refs[-2:]
    width = down_ref.shape[1]
    packed = jnp.concatenate(
        [refs[i][b] for i, start, stop in takes for b in range(start, stop)], axis=0
    )
    rows = packed[:, :width]
    terms = packed[:, width:].astype(jnp.float32)
    lane = lax.broadcasted_iota(jnp.int32, terms.shape, 1)
    mine = lax.rem(lane, lax.axis_size("ep")) == lax.axis_index("ep")
    weight = jnp.sum(jnp.where(mine, terms, 0.0), axis=1, keepdims=True)
    gate = jnp.dot(rows, in_ref[:width], preferred_element_type=jnp.float32)
    up = jnp.dot(rows, in_ref[width:], preferred_element_type=jnp.float32)
    hidden = (gate / (1.0 + jnp.exp(-gate)) * up).astype(jnp.bfloat16)
    out = jnp.dot(hidden, down_ref[...], preferred_element_type=jnp.float32)
    out = (out * weight).astype(jnp.bfloat16).reshape((2,) + near_ref.shape)
    near_ref[...] = out[0]
    far_ref[...] = out[1]


def pair_kernel(own_ref, other_ref, *refs):
    for i, out_ref in enumerate(refs[-own_ref.shape[0] :]):
        total = own_ref[i].astype(jnp.float32) + other_ref[i].astype(jnp.float32)
        out_ref[...] = total.astype(out_ref.dtype)


def add_kernel(own_ref, other_ref, *refs):
    refs[-1][...] = (own_ref[...] + other_ref[...].astype(jnp.float32)).astype(refs[-1].dtype)


def total_kernel(residual_ref, *refs):
    total = residual_ref[...].astype(jnp.float32)
    for ref in refs[:-1]:
        total += ref[...].astype(jnp.float32)
    refs[-1][...] = total.astype(refs[-1].dtype)


def in_vmem(kernel, out_shape, name, arrays, after=(), mebibytes=4, cost_estimate=None):
    return pl.pallas_call(
        kernel,
        out_shape=out_shape,
        in_specs=[HERE] * len(arrays) + [ANYWHERE] * len(after),
        compiler_params=params(mebibytes),
        cost_estimate=cost_estimate,
        name=name,
    )(*arrays, *after)


def layer_gathered(attention, residual, norm_gain, routes, route_weights, expert_in, expert_down):
    row_count, width = residual.shape
    devices = lax.axis_size("ep")
    core, side, line = 1, 2, 4
    extra = -(-3 * devices // 128) * 128
    vmem = pltpu.VMEM
    one = (row_count, width)
    block = vmem((row_count, width + extra), jnp.bfloat16)

    def swap(value, bits):
        return lax.ppermute(value, "ep", [(i, i ^ bits) for i in range(devices)])

    def relay(value, after):
        return in_vmem(relay_kernel, vmem(value.shape, value.dtype), "relay", (value,), after)

    def stack(members, after=()):
        shape = vmem((len(members), row_count, width + extra), jnp.bfloat16)
        return in_vmem(stack_kernel, shape, "stack", members, after)

    packed = from_hbm(
        prepare_kernel,
        block,
        "prepare",
        (residual, norm_gain.reshape(1, -1), routes.T, route_weights.T),
    )
    third, second, first = (swap(packed, d * line) for d in (3, 2, 1))
    across = swap(packed, side)
    along = stack((second, third, first))
    along_side = swap(along, side)
    near = stack((second, third, first, packed, across))
    near_far = swap(near, core)
    held = hold((expert_in, expert_down), (along,))
    along_side_far = swap(relay(along_side, held[:1]), core)

    def ffn(near_takes, side_takes, after=()):
        takes = [(i, *t) for i in (0, 2) for t in near_takes]
        takes[len(near_takes) : len(near_takes)] = [(1, *t) for t in side_takes]
        takes += [(3, *t) for t in side_takes]
        return in_vmem(
            functools.partial(ffn_kernel, takes),
            [vmem((4,) + one, jnp.bfloat16)] * 2,
            "ffn",
            (near, along_side, near_far, along_side_far, *held),
            after,
            mebibytes=16,
            cost_estimate=cost(8 * row_count * 2 * sum(h.size for h in held), 2 * held[0].size),
        )

    early_outs = ffn([(0, 2)], [(0, 2)])
    send = vmem(one, jnp.bfloat16)
    keep_and_send = [vmem(one, jnp.float32)] * 2 + [send] * 2
    second_keep, third_keep, second_send, third_send = in_vmem(
        pair_kernel, keep_and_send, "pair_sum", (early_outs[0], swap(early_outs[1], core))
    )
    third_sum = in_vmem(add_kernel, send, "side_sum", (third_keep, swap(third_send, side)))
    second_sum = in_vmem(
        add_kernel, send, "side_sum", (second_keep, swap(second_send, side)), (third_sum,)
    )
    partial_sum = in_vmem(
        total_kernel,
        vmem(one, jnp.float32),
        "partial_sum",
        (residual, swap(third_sum, 3 * line), swap(second_sum, 2 * line)),
    )
    attended = attend(*attention, (second_sum,))
    late_outs = ffn([(3, 5), (2, 3)], [(2, 3)], early_outs[:1])
    own, across_sum, first_sum, diagonal_sum = in_vmem(
        pair_kernel,
        [vmem(one, jnp.float32), send, send, send],
        "pair_sum",
        (late_outs[0], swap(late_outs[1], core)),
        (third_send,),
    )
    moe_out = in_vmem(
        total_kernel,
        jax.ShapeDtypeStruct(one, jnp.bfloat16),
        "total",
        (
            partial_sum,
            own,
            swap(diagonal_sum, line + side),
            swap(first_sum, line),
            swap(across_sum, side),
        ),
    )
    return attended, moe_out


def expert_layer_routed(residual, norm_gain, routes, route_weights, expert_in, expert_down):
    row_count, top_count = routes.shape
    expert_count = expert_in.shape[0] * lax.axis_size("ep")
    capacity = min(row_count, max(2, 2 * row_count * top_count // expert_count))
    whole = lax.all_gather(residual, "tp", axis=1, tiled=True)
    width = whole.shape[1]
    half_width = residual.shape[1]
    normed = normalize(whole, norm_gain)
    flat_routes = routes.reshape(-1)
    hits = (flat_routes[:, None] == jnp.arange(expert_count)[None, :]).astype(jnp.int32)
    before = jnp.cumsum(hits, axis=0) - hits
    position = jnp.sum(before * hits, axis=1)
    slot_flat = flat_routes * capacity + position
    placed = (slot_flat[:, None] == jnp.arange(expert_count * capacity)[None, :]).astype(
        jnp.float32
    )
    placed = placed.reshape(row_count, top_count, expert_count * capacity)
    selector = jnp.sum(placed, axis=1).astype(jnp.bfloat16)
    buffer = jnp.einsum("rs,rd->sd", selector, normed, preferred_element_type=jnp.float32)
    buffer = buffer.astype(jnp.bfloat16).reshape(expert_count, capacity, width)
    arrived = lax.all_to_all(buffer, "ep", split_axis=0, concat_axis=0, tiled=True)
    sources = arrived.shape[0]
    flat_rows = arrived.reshape(sources * capacity, width)
    gate_act = jnp.dot(flat_rows, expert_in[0, 0], preferred_element_type=jnp.float32)
    up_act = jnp.dot(flat_rows, expert_in[0, 1], preferred_element_type=jnp.float32)
    hidden = (jax.nn.silu(gate_act) * up_act).astype(jnp.bfloat16)
    partial_value = jnp.dot(hidden, expert_down[0], preferred_element_type=jnp.float32)
    partial_value = partial_value.reshape(sources, capacity, width)
    summed = lax.psum_scatter(partial_value, "tp", scatter_dimension=2, tiled=True).astype(
        jnp.bfloat16
    )
    returned = lax.all_to_all(summed, "ep", split_axis=0, concat_axis=0, tiled=True)
    weighting = jnp.sum(placed * route_weights[:, :, None], axis=1)
    gathered_rows = returned.reshape(expert_count * capacity, half_width).astype(jnp.float32)
    combined = jnp.dot(weighting, gathered_rows, precision=lax.Precision.HIGHEST)
    return (residual.astype(jnp.float32) + combined).astype(jnp.bfloat16)


def per_device(
    queries,
    key_cache,
    value_cache,
    new_key,
    new_value,
    lengths,
    residual,
    norm_gain,
    routes,
    route_weights,
    expert_in,
    expert_down,
):
    devices = lax.axis_size("ep")
    dense = lax.axis_size("tp") == 1 and devices == 16
    attention = (queries, key_cache, value_cache, new_key, new_value, lengths)
    layer = (residual, norm_gain, routes, route_weights)
    if dense:
        return layer_gathered(attention, *layer, expert_in, expert_down)
    attended = attention_block(*attention)
    return (attended, expert_layer_routed(*layer, expert_in, expert_down))


def solution(mesh):
    in_specs = (
        P(("groups", "ep"), "tp", None),
        P(("groups", "ep"), None, "tp", None),
        P(("groups", "ep"), None, "tp", None),
        P(("groups", "ep"), "tp", None),
        P(("groups", "ep"), "tp", None),
        P(("groups", "ep")),
        P(("groups", "ep"), "tp"),
        P(),
        P(("groups", "ep"), None),
        P(("groups", "ep"), None),
        P("ep", None, None, "tp"),
        P("ep", "tp", None),
    )
    out_specs = (P(("groups", "ep"), "tp", None), P(("groups", "ep"), "tp"))
    return jax.shard_map(
        per_device, mesh=mesh, in_specs=in_specs, out_specs=out_specs, check_vma=False
    )
```

```python
import functools

import jax
import jax.numpy as jnp
from jax import lax
from jax.experimental import pallas as pl
from jax.experimental.pallas import tpu as pltpu
from jax.sharding import PartitionSpec as P


def attention_block(queries, key_cache, value_cache, new_key, new_value, lengths):
    rows_here, heads_here, head_size = queries.shape
    kv_here = key_cache.shape[2]
    slots_here = key_cache.shape[1]
    group = heads_here // kv_here
    scale = 1.0 / head_size**0.5
    grouped = queries.reshape(rows_here, kv_here, group, head_size)
    scores = (
        jnp.einsum("akgd,ackd->akgc", grouped, key_cache, preferred_element_type=jnp.float32)
        * scale
    )
    valid = (jnp.arange(slots_here)[None, :] < lengths[:, None])[:, None, None, :]
    scores = jnp.where(valid, scores, -1e30)
    own_score = (
        jnp.einsum("akgd,akd->akg", grouped, new_key, preferred_element_type=jnp.float32) * scale
    )
    largest = jnp.maximum(jnp.max(scores, axis=-1), own_score)
    cache_exp = jnp.exp(scores - largest[..., None])
    own_exp = jnp.exp(own_score - largest)
    total = jnp.sum(cache_exp, axis=-1) + own_exp
    cache_probs = (cache_exp / total[..., None]).astype(jnp.bfloat16)
    own_probs = (own_exp / total).astype(jnp.bfloat16)
    mixed = jnp.einsum(
        "akgc,ackd->akgd", cache_probs, value_cache, preferred_element_type=jnp.float32
    )
    mixed = (
        mixed
        + own_probs.astype(jnp.float32)[..., None] * new_value.astype(jnp.float32)[:, :, None, :]
    )
    return mixed.reshape(rows_here, heads_here, head_size).astype(jnp.bfloat16)


def normalize(residual, norm_gain):
    wide = residual.astype(jnp.float32)
    return (
        wide * lax.rsqrt(jnp.mean(wide * wide, axis=1, keepdims=True) + 1e-06) * norm_gain
    ).astype(jnp.bfloat16)


def load(sources, targets, sems):
    copies = [
        pltpu.make_async_copy(source, target, sems.at[i])
        for i, (source, target) in enumerate(zip(sources, targets))
    ]
    for copy in copies:
        copy.start()
    return copies


def stay(array):
    return pltpu.with_memory_space_constraint(array, pltpu.HBM)


HERE = pl.BlockSpec(memory_space=pltpu.VMEM)
ANYWHERE = pl.BlockSpec(memory_space=pl.ANY)


def params(mebibytes=4):
    return pltpu.CompilerParams(vmem_limit_bytes=mebibytes * 1024 * 1024)


def cost(flops=0, bytes_accessed=0):
    return pl.CostEstimate(flops=flops, bytes_accessed=bytes_accessed, transcendentals=0)


def from_hbm(kernel, out_shape, name, arrays, after=(), cost_estimate=None):
    return pl.pallas_call(
        kernel,
        out_shape=out_shape,
        in_specs=[pl.BlockSpec(memory_space=pltpu.HBM)] * len(arrays) + [ANYWHERE] * len(after),
        scratch_shapes=[
            (pltpu.VMEM if array.ndim > 1 else pltpu.SMEM)(array.shape, array.dtype)
            for array in arrays
        ]
        + [pltpu.SemaphoreType.DMA((len(arrays),))],
        compiler_params=params(),
        cost_estimate=cost_estimate,
        name=name,
    )(*(stay(array) for array in arrays), *after)


def attend_kernel(*refs):
    attended_ref = refs[-8]
    lengths_ref, queries_ref, keys_ref, values_ref, new_keys_ref, new_values_ref = refs[-7:-1]
    copies = load(refs[:6], refs[-7:-1], refs[-1])
    row_count, heads, head_size = queries_ref.shape
    kv_heads = new_keys_ref.shape[0] // row_count
    group = heads // kv_heads
    scale = 1.0 / head_size**0.5
    across = (((1,), (1,)), ((), ()))

    def grids(columns):
        shape = (heads, columns)
        head = lax.broadcasted_iota(jnp.int32, shape, 0) // group
        return head, lax.broadcasted_iota(jnp.int32, shape, 1)

    head, column = grids(keys_ref.shape[1])
    own_head, own_column = grids(new_keys_ref.shape[0])
    same_head = column % kv_heads == head
    slot = column // kv_heads
    for copy in copies:
        copy.wait()
    for a in range(row_count):
        query = queries_ref[a]
        scores = lax.dot_general(query, keys_ref[a], across, preferred_element_type=jnp.float32)
        scores = jnp.where(same_head & (slot < lengths_ref[a]), scores * scale, -1e30)
        own = lax.dot_general(
            query, new_keys_ref[...], across, preferred_element_type=jnp.float32
        )
        own = jnp.where(own_column == own_head + a * kv_heads, own * scale, -1e30)
        largest = jnp.maximum(
            jnp.max(scores, axis=1, keepdims=True), jnp.max(own, axis=1, keepdims=True)
        )
        scores = jnp.exp(scores - largest)
        own = jnp.exp(own - largest)
        total = jnp.sum(scores, axis=1, keepdims=True) + jnp.sum(own, axis=1, keepdims=True)
        mixed = jnp.dot(
            (scores / total).astype(jnp.bfloat16),
            values_ref[a],
            preferred_element_type=jnp.float32,
        ) + jnp.dot(
            (own / total).astype(jnp.bfloat16),
            new_values_ref[...],
            preferred_element_type=jnp.float32,
        )
        attended_ref[a] = mixed.astype(jnp.bfloat16)


def attend(queries, key_cache, value_cache, new_key, new_value, lengths, after):
    rows_here, slots_here, kv_here, head_size = key_cache.shape
    lines = (rows_here, slots_here * kv_here, head_size)
    arrays = (
        lengths,
        queries,
        key_cache.reshape(lines),
        value_cache.reshape(lines),
        new_key.reshape(-1, head_size),
        new_value.reshape(-1, head_size),
    )
    out_shape = jax.ShapeDtypeStruct(queries.shape, jnp.bfloat16)
    work = cost(0, 16 * key_cache.size * key_cache.dtype.itemsize)
    return from_hbm(attend_kernel, out_shape, "attend", arrays, after, work)


def hold_kernel(count, pieces, *refs):
    sources, targets, sems = refs[:count], refs[-1 - count : -1], refs[-1]
    starts, ends = [], []
    for source, target in zip(sources, targets):
        lines = source.shape[0] // pieces
        for i in range(pieces):
            starts.append(source.at[pl.ds(i * lines, lines)])
            ends.append(target.at[pl.ds(i * lines, lines)])
    for copy in load(starts, ends, sems):
        copy.wait()


def hold(arrays, after, pieces=4):
    flat = [array.reshape(-1, array.shape[-1]) for array in arrays]
    size = sum(array.size for array in flat)
    return pl.pallas_call(
        functools.partial(hold_kernel, len(flat), pieces),
        out_shape=[pltpu.VMEM(array.shape, array.dtype) for array in flat],
        in_specs=[pl.BlockSpec(memory_space=pltpu.HBM)] * len(flat) + [ANYWHERE] * len(after),
        scratch_shapes=[pltpu.SemaphoreType.DMA((pieces * len(flat),))],
        cost_estimate=cost(0, 2 * size),
        compiler_params=params(),
        name="hold",
    )(*(stay(array) for array in flat), *after)


def prepare_kernel(*refs):
    packed_ref, residual_ref, gain_ref, routes_ref, weights_ref, sems = refs[4:]
    for copy in load(refs[:4], refs[5:9], sems):
        copy.wait()
    row_count, width = residual_ref.shape
    experts = lax.axis_size("ep")
    lanes = packed_ref.shape[1] - width
    wide = residual_ref[...].astype(jnp.float32)
    mean = jnp.mean(wide * wide, axis=1, keepdims=True)
    packed_ref[:, :width] = (wide * lax.rsqrt(mean + 1e-06) * gain_ref[...]).astype(jnp.bfloat16)
    line = lax.broadcasted_iota(jnp.int32, (lanes, row_count), 0)
    expert = lax.rem(line, experts)
    weight = jnp.zeros(line.shape, jnp.float32)
    for k in range(routes_ref.shape[0]):
        weight += jnp.where(routes_ref[k : k + 1, :] == expert, weights_ref[k : k + 1, :], 0.0)
    high = weight.astype(jnp.bfloat16).astype(jnp.float32)
    low = (weight - high).astype(jnp.bfloat16).astype(jnp.float32)
    lowest = weight - high - low
    terms = jnp.where(
        line < experts,
        high,
        jnp.where(line < 2 * experts, low, jnp.where(line < 3 * experts, lowest, 0.0)),
    )
    at = lax.broadcasted_iota(jnp.int32, (row_count, row_count), 0)
    same = at == lax.broadcasted_iota(jnp.int32, (row_count, row_count), 1)
    turned = lax.dot_general(
        same.astype(jnp.bfloat16),
        terms.astype(jnp.bfloat16),
        (((1,), (1,)), ((), ())),
        preferred_element_type=jnp.float32,
    )
    packed_ref[:, width:] = turned.astype(jnp.bfloat16)


def stack_kernel(*refs):
    for i in range(refs[-1].shape[0]):
        refs[-1][i] = refs[i][...]


def relay_kernel(in_ref, *refs):
    refs[-1][...] = in_ref[...]


def ffn_kernel(takes, *refs):
    in_ref, down_ref = refs[4:6]
    near_ref, far_ref = refs[-2:]
    width = down_ref.shape[1]
    packed = jnp.concatenate(
        [refs[i][b] for i, start, stop in takes for b in range(start, stop)], axis=0
    )
    rows = packed[:, :width]
    terms = packed[:, width:].astype(jnp.float32)
    lane = lax.broadcasted_iota(jnp.int32, terms.shape, 1)
    mine = lax.rem(lane, lax.axis_size("ep")) == lax.axis_index("ep")
    weight = jnp.sum(jnp.where(mine, terms, 0.0), axis=1, keepdims=True)
    gate = jnp.dot(rows, in_ref[:width], preferred_element_type=jnp.float32)
    up = jnp.dot(rows, in_ref[width:], preferred_element_type=jnp.float32)
    hidden = (gate / (1.0 + jnp.exp(-gate)) * up).astype(jnp.bfloat16)
    out = jnp.dot(hidden, down_ref[...], preferred_element_type=jnp.float32)
    out = (out * weight).astype(jnp.bfloat16).reshape((2,) + near_ref.shape)
    near_ref[...] = out[0]
    far_ref[...] = out[1]


def pair_kernel(own_ref, other_ref, *refs):
    for i, out_ref in enumerate(refs[-own_ref.shape[0] :]):
        total = own_ref[i].astype(jnp.float32) + other_ref[i].astype(jnp.float32)
        out_ref[...] = total.astype(out_ref.dtype)


def add_kernel(own_ref, other_ref, *refs):
    refs[-1][...] = (own_ref[...] + other_ref[...].astype(jnp.float32)).astype(refs[-1].dtype)


def total_kernel(residual_ref, *refs):
    total = residual_ref[...].astype(jnp.float32)
    for ref in refs[:-1]:
        total += ref[...].astype(jnp.float32)
    refs[-1][...] = total.astype(refs[-1].dtype)


def in_vmem(kernel, out_shape, name, arrays, after=(), mebibytes=4, cost_estimate=None):
    return pl.pallas_call(
        kernel,
        out_shape=out_shape,
        in_specs=[HERE] * len(arrays) + [ANYWHERE] * len(after),
        compiler_params=params(mebibytes),
        cost_estimate=cost_estimate,
        name=name,
    )(*arrays, *after)


def layer_gathered(attention, residual, norm_gain, routes, route_weights, expert_in, expert_down):
    row_count, width = residual.shape
    devices = lax.axis_size("ep")
    core, side, line = 1, 2, 4
    extra = -(-3 * devices // 128) * 128
    vmem = pltpu.VMEM
    one = (row_count, width)
    block = vmem((row_count, width + extra), jnp.bfloat16)

    def swap(value, bits):
        return lax.ppermute(value, "ep", [(i, i ^ bits) for i in range(devices)])

    def relay(value, after):
        return in_vmem(relay_kernel, vmem(value.shape, value.dtype), "relay", (value,), after)

    def stack(members, after=()):
        shape = vmem((len(members), row_count, width + extra), jnp.bfloat16)
        return in_vmem(stack_kernel, shape, "stack", members, after)

    packed = from_hbm(
        prepare_kernel,
        block,
        "prepare",
        (residual, norm_gain.reshape(1, -1), routes.T, route_weights.T),
    )
    third, second, first = (swap(packed, d * line) for d in (3, 2, 1))
    across = swap(packed, side)
    attended = attend(*attention, (packed,))
    along = stack((second, third, first), (stay(attended),))
    along_side = swap(along, side)
    near = stack((second, third, first, packed, across))
    near_far = swap(near, core)
    held = hold((expert_in, expert_down), (along,))
    along_side_far = swap(relay(along_side, held[:1]), core)

    def ffn(near_takes, side_takes, after=()):
        takes = [(i, *t) for i in (0, 2) for t in near_takes]
        takes[len(near_takes) : len(near_takes)] = [(1, *t) for t in side_takes]
        takes += [(3, *t) for t in side_takes]
        return in_vmem(
            functools.partial(ffn_kernel, takes),
            [vmem((4,) + one, jnp.bfloat16)] * 2,
            "ffn",
            (near, along_side, near_far, along_side_far, *held),
            after,
            mebibytes=16,
            cost_estimate=cost(8 * row_count * 2 * sum(h.size for h in held), 2 * held[0].size),
        )

    early_outs = ffn([(0, 2)], [(0, 2)])
    send = vmem(one, jnp.bfloat16)
    keep_and_send = [vmem(one, jnp.float32)] * 2 + [send] * 2
    second_keep, third_keep, second_send, third_send = in_vmem(
        pair_kernel, keep_and_send, "pair_sum", (early_outs[0], swap(early_outs[1], core))
    )
    third_sum = in_vmem(add_kernel, send, "side_sum", (third_keep, swap(third_send, side)))
    second_sum = in_vmem(
        add_kernel, send, "side_sum", (second_keep, swap(second_send, side)), (third_sum,)
    )
    partial_sum = in_vmem(
        total_kernel,
        vmem(one, jnp.float32),
        "partial_sum",
        (residual, swap(third_sum, 3 * line), swap(second_sum, 2 * line)),
    )
    late_outs = ffn([(3, 5), (2, 3)], [(2, 3)], early_outs[:1])
    own, across_sum, first_sum, diagonal_sum = in_vmem(
        pair_kernel,
        [vmem(one, jnp.float32), send, send, send],
        "pair_sum",
        (late_outs[0], swap(late_outs[1], core)),
        (third_send,),
    )
    moe_out = in_vmem(
        total_kernel,
        jax.ShapeDtypeStruct(one, jnp.bfloat16),
        "total",
        (
            partial_sum,
            own,
            swap(diagonal_sum, line + side),
            swap(first_sum, line),
            swap(across_sum, side),
        ),
    )
    return attended, moe_out


def expert_layer_routed(residual, norm_gain, routes, route_weights, expert_in, expert_down):
    row_count, top_count = routes.shape
    expert_count = expert_in.shape[0] * lax.axis_size("ep")
    capacity = min(row_count, max(2, 2 * row_count * top_count // expert_count))
    whole = lax.all_gather(residual, "tp", axis=1, tiled=True)
    width = whole.shape[1]
    half_width = residual.shape[1]
    normed = normalize(whole, norm_gain)
    flat_routes = routes.reshape(-1)
    hits = (flat_routes[:, None] == jnp.arange(expert_count)[None, :]).astype(jnp.int32)
    before = jnp.cumsum(hits, axis=0) - hits
    position = jnp.sum(before * hits, axis=1)
    slot_flat = flat_routes * capacity + position
    placed = (slot_flat[:, None] == jnp.arange(expert_count * capacity)[None, :]).astype(
        jnp.float32
    )
    placed = placed.reshape(row_count, top_count, expert_count * capacity)
    selector = jnp.sum(placed, axis=1).astype(jnp.bfloat16)
    buffer = jnp.einsum("rs,rd->sd", selector, normed, preferred_element_type=jnp.float32)
    buffer = buffer.astype(jnp.bfloat16).reshape(expert_count, capacity, width)
    arrived = lax.all_to_all(buffer, "ep", split_axis=0, concat_axis=0, tiled=True)
    sources = arrived.shape[0]
    flat_rows = arrived.reshape(sources * capacity, width)
    gate_act = jnp.dot(flat_rows, expert_in[0, 0], preferred_element_type=jnp.float32)
    up_act = jnp.dot(flat_rows, expert_in[0, 1], preferred_element_type=jnp.float32)
    hidden = (jax.nn.silu(gate_act) * up_act).astype(jnp.bfloat16)
    partial_value = jnp.dot(hidden, expert_down[0], preferred_element_type=jnp.float32)
    partial_value = partial_value.reshape(sources, capacity, width)
    summed = lax.psum_scatter(partial_value, "tp", scatter_dimension=2, tiled=True).astype(
        jnp.bfloat16
    )
    returned = lax.all_to_all(summed, "ep", split_axis=0, concat_axis=0, tiled=True)
    weighting = jnp.sum(placed * route_weights[:, :, None], axis=1)
    gathered_rows = returned.reshape(expert_count * capacity, half_width).astype(jnp.float32)
    combined = jnp.dot(weighting, gathered_rows, precision=lax.Precision.HIGHEST)
    return (residual.astype(jnp.float32) + combined).astype(jnp.bfloat16)


def per_device(
    queries,
    key_cache,
    value_cache,
    new_key,
    new_value,
    lengths,
    residual,
    norm_gain,
    routes,
    route_weights,
    expert_in,
    expert_down,
):
    devices = lax.axis_size("ep")
    dense = lax.axis_size("tp") == 1 and devices == 16
    attention = (queries, key_cache, value_cache, new_key, new_value, lengths)
    layer = (residual, norm_gain, routes, route_weights)
    if dense:
        return layer_gathered(attention, *layer, expert_in, expert_down)
    attended = attention_block(*attention)
    return (attended, expert_layer_routed(*layer, expert_in, expert_down))


def solution(mesh):
    in_specs = (
        P(("groups", "ep"), "tp", None),
        P(("groups", "ep"), None, "tp", None),
        P(("groups", "ep"), None, "tp", None),
        P(("groups", "ep"), "tp", None),
        P(("groups", "ep"), "tp", None),
        P(("groups", "ep")),
        P(("groups", "ep"), "tp"),
        P(),
        P(("groups", "ep"), None),
        P(("groups", "ep"), None),
        P("ep", None, None, "tp"),
        P("ep", "tp", None),
    )
    out_specs = (P(("groups", "ep"), "tp", None), P(("groups", "ep"), "tp"))
    return jax.shard_map(
        per_device, mesh=mesh, in_specs=in_specs, out_specs=out_specs, check_vma=False
    )
```

```python
import functools

import jax
import jax.numpy as jnp
from jax import lax
from jax.experimental import pallas as pl
from jax.experimental.pallas import tpu as pltpu
from jax.sharding import PartitionSpec as P


def attention_block(queries, key_cache, value_cache, new_key, new_value, lengths):
    rows_here, heads_here, head_size = queries.shape
    kv_here = key_cache.shape[2]
    slots_here = key_cache.shape[1]
    group = heads_here // kv_here
    scale = 1.0 / head_size**0.5
    grouped = queries.reshape(rows_here, kv_here, group, head_size)
    scores = (
        jnp.einsum("akgd,ackd->akgc", grouped, key_cache, preferred_element_type=jnp.float32)
        * scale
    )
    valid = (jnp.arange(slots_here)[None, :] < lengths[:, None])[:, None, None, :]
    scores = jnp.where(valid, scores, -1e30)
    own_score = (
        jnp.einsum("akgd,akd->akg", grouped, new_key, preferred_element_type=jnp.float32) * scale
    )
    largest = jnp.maximum(jnp.max(scores, axis=-1), own_score)
    cache_exp = jnp.exp(scores - largest[..., None])
    own_exp = jnp.exp(own_score - largest)
    total = jnp.sum(cache_exp, axis=-1) + own_exp
    cache_probs = (cache_exp / total[..., None]).astype(jnp.bfloat16)
    own_probs = (own_exp / total).astype(jnp.bfloat16)
    mixed = jnp.einsum(
        "akgc,ackd->akgd", cache_probs, value_cache, preferred_element_type=jnp.float32
    )
    mixed = (
        mixed
        + own_probs.astype(jnp.float32)[..., None] * new_value.astype(jnp.float32)[:, :, None, :]
    )
    return mixed.reshape(rows_here, heads_here, head_size).astype(jnp.bfloat16)


def normalize(residual, norm_gain):
    wide = residual.astype(jnp.float32)
    return (
        wide * lax.rsqrt(jnp.mean(wide * wide, axis=1, keepdims=True) + 1e-06) * norm_gain
    ).astype(jnp.bfloat16)


def load(sources, targets, sems):
    copies = [
        pltpu.make_async_copy(source, target, sems.at[i])
        for i, (source, target) in enumerate(zip(sources, targets))
    ]
    for copy in copies:
        copy.start()
    return copies


def stay(array):
    return pltpu.with_memory_space_constraint(array, pltpu.HBM)


HERE = pl.BlockSpec(memory_space=pltpu.VMEM)
ANYWHERE = pl.BlockSpec(memory_space=pl.ANY)


def params(mebibytes=4):
    return pltpu.CompilerParams(vmem_limit_bytes=mebibytes * 1024 * 1024)


def cost(flops=0, bytes_accessed=0):
    return pl.CostEstimate(flops=flops, bytes_accessed=bytes_accessed, transcendentals=0)


def from_hbm(kernel, out_shape, name, arrays, after=(), cost_estimate=None):
    return pl.pallas_call(
        kernel,
        out_shape=out_shape,
        in_specs=[pl.BlockSpec(memory_space=pltpu.HBM)] * len(arrays) + [ANYWHERE] * len(after),
        scratch_shapes=[
            (pltpu.VMEM if array.ndim > 1 else pltpu.SMEM)(array.shape, array.dtype)
            for array in arrays
        ]
        + [pltpu.SemaphoreType.DMA((len(arrays),))],
        compiler_params=params(),
        cost_estimate=cost_estimate,
        name=name,
    )(*(stay(array) for array in arrays), *after)


def attend_kernel(*refs):
    attended_ref = refs[-8]
    lengths_ref, queries_ref, keys_ref, values_ref, new_keys_ref, new_values_ref = refs[-7:-1]
    copies = load(refs[:6], refs[-7:-1], refs[-1])
    row_count, heads, head_size = queries_ref.shape
    kv_heads = new_keys_ref.shape[0] // row_count
    group = heads // kv_heads
    scale = 1.0 / head_size**0.5
    across = (((1,), (1,)), ((), ()))

    def grids(columns):
        shape = (heads, columns)
        head = lax.broadcasted_iota(jnp.int32, shape, 0) // group
        return head, lax.broadcasted_iota(jnp.int32, shape, 1)

    head, column = grids(keys_ref.shape[1])
    own_head, own_column = grids(new_keys_ref.shape[0])
    same_head = column % kv_heads == head
    slot = column // kv_heads
    for copy in copies:
        copy.wait()
    for a in range(row_count):
        query = queries_ref[a]
        scores = lax.dot_general(query, keys_ref[a], across, preferred_element_type=jnp.float32)
        scores = jnp.where(same_head & (slot < lengths_ref[a]), scores * scale, -1e30)
        own = lax.dot_general(
            query, new_keys_ref[...], across, preferred_element_type=jnp.float32
        )
        own = jnp.where(own_column == own_head + a * kv_heads, own * scale, -1e30)
        largest = jnp.maximum(
            jnp.max(scores, axis=1, keepdims=True), jnp.max(own, axis=1, keepdims=True)
        )
        scores = jnp.exp(scores - largest)
        own = jnp.exp(own - largest)
        total = jnp.sum(scores, axis=1, keepdims=True) + jnp.sum(own, axis=1, keepdims=True)
        mixed = jnp.dot(
            (scores / total).astype(jnp.bfloat16),
            values_ref[a],
            preferred_element_type=jnp.float32,
        ) + jnp.dot(
            (own / total).astype(jnp.bfloat16),
            new_values_ref[...],
            preferred_element_type=jnp.float32,
        )
        attended_ref[a] = mixed.astype(jnp.bfloat16)


def attend(queries, key_cache, value_cache, new_key, new_value, lengths, after):
    rows_here, slots_here, kv_here, head_size = key_cache.shape
    lines = (rows_here, slots_here * kv_here, head_size)
    arrays = (
        lengths,
        queries,
        key_cache.reshape(lines),
        value_cache.reshape(lines),
        new_key.reshape(-1, head_size),
        new_value.reshape(-1, head_size),
    )
    out_shape = jax.ShapeDtypeStruct(queries.shape, jnp.bfloat16)
    work = cost(0, 16 * key_cache.size * key_cache.dtype.itemsize)
    return from_hbm(attend_kernel, out_shape, "attend", arrays, after, work)


def hold_kernel(count, pieces, *refs):
    sources, targets, sems = refs[:count], refs[-1 - count : -1], refs[-1]
    starts, ends = [], []
    for source, target in zip(sources, targets):
        lines = source.shape[0] // pieces
        for i in range(pieces):
            starts.append(source.at[pl.ds(i * lines, lines)])
            ends.append(target.at[pl.ds(i * lines, lines)])
    for copy in load(starts, ends, sems):
        copy.wait()


def hold(arrays, after, pieces=4):
    flat = [array.reshape(-1, array.shape[-1]) for array in arrays]
    size = sum(array.size for array in flat)
    return pl.pallas_call(
        functools.partial(hold_kernel, len(flat), pieces),
        out_shape=[pltpu.VMEM(array.shape, array.dtype) for array in flat],
        in_specs=[pl.BlockSpec(memory_space=pltpu.HBM)] * len(flat) + [ANYWHERE] * len(after),
        scratch_shapes=[pltpu.SemaphoreType.DMA((pieces * len(flat),))],
        cost_estimate=cost(0, 2 * size),
        compiler_params=params(),
        name="hold",
    )(*(stay(array) for array in flat), *after)


def prepare_kernel(*refs):
    packed_ref, residual_ref, gain_ref, routes_ref, weights_ref, sems = refs[4:]
    for copy in load(refs[:4], refs[5:9], sems):
        copy.wait()
    row_count, width = residual_ref.shape
    experts = lax.axis_size("ep")
    lanes = packed_ref.shape[1] - width
    wide = residual_ref[...].astype(jnp.float32)
    mean = jnp.mean(wide * wide, axis=1, keepdims=True)
    packed_ref[:, :width] = (wide * lax.rsqrt(mean + 1e-06) * gain_ref[...]).astype(jnp.bfloat16)
    line = lax.broadcasted_iota(jnp.int32, (lanes, row_count), 0)
    expert = lax.rem(line, experts)
    weight = jnp.zeros(line.shape, jnp.float32)
    for k in range(routes_ref.shape[0]):
        weight += jnp.where(routes_ref[k : k + 1, :] == expert, weights_ref[k : k + 1, :], 0.0)
    high = weight.astype(jnp.bfloat16).astype(jnp.float32)
    low = (weight - high).astype(jnp.bfloat16).astype(jnp.float32)
    lowest = weight - high - low
    terms = jnp.where(
        line < experts,
        high,
        jnp.where(line < 2 * experts, low, jnp.where(line < 3 * experts, lowest, 0.0)),
    )
    at = lax.broadcasted_iota(jnp.int32, (row_count, row_count), 0)
    same = at == lax.broadcasted_iota(jnp.int32, (row_count, row_count), 1)
    turned = lax.dot_general(
        same.astype(jnp.bfloat16),
        terms.astype(jnp.bfloat16),
        (((1,), (1,)), ((), ())),
        preferred_element_type=jnp.float32,
    )
    packed_ref[:, width:] = turned.astype(jnp.bfloat16)


def stack_kernel(*refs):
    for i in range(refs[-1].shape[0]):
        refs[-1][i] = refs[i][...]


def relay_kernel(in_ref, *refs):
    refs[-1][...] = in_ref[...]


def ffn_kernel(takes, *refs):
    in_ref, down_ref = refs[4:6]
    near_ref, far_ref = refs[-2:]
    width = down_ref.shape[1]
    packed = jnp.concatenate(
        [refs[i][b] for i, start, stop in takes for b in range(start, stop)], axis=0
    )
    rows = packed[:, :width]
    terms = packed[:, width:].astype(jnp.float32)
    lane = lax.broadcasted_iota(jnp.int32, terms.shape, 1)
    mine = lax.rem(lane, lax.axis_size("ep")) == lax.axis_index("ep")
    weight = jnp.sum(jnp.where(mine, terms, 0.0), axis=1, keepdims=True)
    gate = jnp.dot(rows, in_ref[:width], preferred_element_type=jnp.float32)
    up = jnp.dot(rows, in_ref[width:], preferred_element_type=jnp.float32)
    hidden = (gate / (1.0 + jnp.exp(-gate)) * up).astype(jnp.bfloat16)
    out = jnp.dot(hidden, down_ref[...], preferred_element_type=jnp.float32)
    out = (out * weight).astype(jnp.bfloat16).reshape((2,) + near_ref.shape)
    near_ref[...] = out[0]
    far_ref[...] = out[1]


def pair_kernel(own_ref, other_ref, *refs):
    for i, out_ref in enumerate(refs[-own_ref.shape[0] :]):
        total = own_ref[i].astype(jnp.float32) + other_ref[i].astype(jnp.float32)
        out_ref[...] = total.astype(out_ref.dtype)


def add_kernel(own_ref, other_ref, *refs):
    refs[-1][...] = (own_ref[...] + other_ref[...].astype(jnp.float32)).astype(refs[-1].dtype)


def total_kernel(residual_ref, *refs):
    total = residual_ref[...].astype(jnp.float32)
    for ref in refs[:-1]:
        total += ref[...].astype(jnp.float32)
    refs[-1][...] = total.astype(refs[-1].dtype)


def in_vmem(kernel, out_shape, name, arrays, after=(), mebibytes=4, cost_estimate=None):
    return pl.pallas_call(
        kernel,
        out_shape=out_shape,
        in_specs=[HERE] * len(arrays) + [ANYWHERE] * len(after),
        compiler_params=params(mebibytes),
        cost_estimate=cost_estimate,
        name=name,
    )(*arrays, *after)


def layer_gathered(attention, residual, norm_gain, routes, route_weights, expert_in, expert_down):
    row_count, width = residual.shape
    devices = lax.axis_size("ep")
    core, side, line = 1, 2, 4
    extra = -(-3 * devices // 128) * 128
    vmem = pltpu.VMEM
    one = (row_count, width)
    block = vmem((row_count, width + extra), jnp.bfloat16)

    def swap(value, bits):
        return lax.ppermute(value, "ep", [(i, i ^ bits) for i in range(devices)])

    def relay(value, after):
        return in_vmem(relay_kernel, vmem(value.shape, value.dtype), "relay", (value,), after)

    def stack(members, after=()):
        shape = vmem((len(members), row_count, width + extra), jnp.bfloat16)
        return in_vmem(stack_kernel, shape, "stack", members, after)

    packed = from_hbm(
        prepare_kernel,
        block,
        "prepare",
        (residual, norm_gain.reshape(1, -1), routes.T, route_weights.T),
    )
    third, second, first = (swap(packed, d * line) for d in (3, 2, 1))
    across = swap(packed, side)
    attended = attend(*attention, (packed,))
    along = stack((second, third, first), (stay(attended),))
    along_side = swap(along, side)
    near = stack((second, third, first, packed, across))
    near_far = swap(near, core)
    held = hold((expert_in, expert_down), (along,))
    along_side_far = swap(relay(along_side, held[:1]), core)

    def ffn(near_takes, side_takes, after=()):
        takes = [(i, *t) for i in (0, 2) for t in near_takes]
        takes[len(near_takes) : len(near_takes)] = [(1, *t) for t in side_takes]
        takes += [(3, *t) for t in side_takes]
        return in_vmem(
            functools.partial(ffn_kernel, takes),
            [vmem((4,) + one, jnp.bfloat16)] * 2,
            "ffn",
            (near, along_side, near_far, along_side_far, *held),
            after,
            mebibytes=16,
            cost_estimate=cost(8 * row_count * 2 * sum(h.size for h in held), 2 * held[0].size),
        )

    early_outs = ffn([(0, 2)], [(0, 2)])
    send = vmem(one, jnp.bfloat16)
    keep_and_send = [vmem(one, jnp.float32)] * 2 + [send] * 2
    second_keep, third_keep, second_send, third_send = in_vmem(
        pair_kernel, keep_and_send, "pair_sum", (early_outs[0], swap(early_outs[1], core))
    )
    third_sum = in_vmem(add_kernel, send, "side_sum", (third_keep, swap(third_send, side)))
    second_sum = in_vmem(
        add_kernel, send, "side_sum", (second_keep, swap(second_send, side)), (third_sum,)
    )
    partial_sum = in_vmem(
        total_kernel,
        vmem(one, jnp.float32),
        "partial_sum",
        (residual, swap(third_sum, 3 * line), swap(second_sum, 2 * line)),
    )
    late_outs = ffn([(3, 5), (2, 3)], [(2, 3)], early_outs[:1])
    own, across_sum, first_sum, diagonal_sum = in_vmem(
        pair_kernel,
        [vmem(one, jnp.float32), send, send, send],
        "pair_sum",
        (late_outs[0], swap(late_outs[1], core)),
        (second_sum,),
    )
    moe_out = in_vmem(
        total_kernel,
        jax.ShapeDtypeStruct(one, jnp.bfloat16),
        "total",
        (
            partial_sum,
            own,
            swap(diagonal_sum, line + side),
            swap(first_sum, line),
            swap(across_sum, side),
        ),
    )
    return attended, moe_out


def expert_layer_routed(residual, norm_gain, routes, route_weights, expert_in, expert_down):
    row_count, top_count = routes.shape
    expert_count = expert_in.shape[0] * lax.axis_size("ep")
    capacity = min(row_count, max(2, 2 * row_count * top_count // expert_count))
    whole = lax.all_gather(residual, "tp", axis=1, tiled=True)
    width = whole.shape[1]
    half_width = residual.shape[1]
    normed = normalize(whole, norm_gain)
    flat_routes = routes.reshape(-1)
    hits = (flat_routes[:, None] == jnp.arange(expert_count)[None, :]).astype(jnp.int32)
    before = jnp.cumsum(hits, axis=0) - hits
    position = jnp.sum(before * hits, axis=1)
    slot_flat = flat_routes * capacity + position
    placed = (slot_flat[:, None] == jnp.arange(expert_count * capacity)[None, :]).astype(
        jnp.float32
    )
    placed = placed.reshape(row_count, top_count, expert_count * capacity)
    selector = jnp.sum(placed, axis=1).astype(jnp.bfloat16)
    buffer = jnp.einsum("rs,rd->sd", selector, normed, preferred_element_type=jnp.float32)
    buffer = buffer.astype(jnp.bfloat16).reshape(expert_count, capacity, width)
    arrived = lax.all_to_all(buffer, "ep", split_axis=0, concat_axis=0, tiled=True)
    sources = arrived.shape[0]
    flat_rows = arrived.reshape(sources * capacity, width)
    gate_act = jnp.dot(flat_rows, expert_in[0, 0], preferred_element_type=jnp.float32)
    up_act = jnp.dot(flat_rows, expert_in[0, 1], preferred_element_type=jnp.float32)
    hidden = (jax.nn.silu(gate_act) * up_act).astype(jnp.bfloat16)
    partial_value = jnp.dot(hidden, expert_down[0], preferred_element_type=jnp.float32)
    partial_value = partial_value.reshape(sources, capacity, width)
    summed = lax.psum_scatter(partial_value, "tp", scatter_dimension=2, tiled=True).astype(
        jnp.bfloat16
    )
    returned = lax.all_to_all(summed, "ep", split_axis=0, concat_axis=0, tiled=True)
    weighting = jnp.sum(placed * route_weights[:, :, None], axis=1)
    gathered_rows = returned.reshape(expert_count * capacity, half_width).astype(jnp.float32)
    combined = jnp.dot(weighting, gathered_rows, precision=lax.Precision.HIGHEST)
    return (residual.astype(jnp.float32) + combined).astype(jnp.bfloat16)


def per_device(
    queries,
    key_cache,
    value_cache,
    new_key,
    new_value,
    lengths,
    residual,
    norm_gain,
    routes,
    route_weights,
    expert_in,
    expert_down,
):
    devices = lax.axis_size("ep")
    dense = lax.axis_size("tp") == 1 and devices == 16
    attention = (queries, key_cache, value_cache, new_key, new_value, lengths)
    layer = (residual, norm_gain, routes, route_weights)
    if dense:
        return layer_gathered(attention, *layer, expert_in, expert_down)
    attended = attention_block(*attention)
    return (attended, expert_layer_routed(*layer, expert_in, expert_down))


def solution(mesh):
    in_specs = (
        P(("groups", "ep"), "tp", None),
        P(("groups", "ep"), None, "tp", None),
        P(("groups", "ep"), None, "tp", None),
        P(("groups", "ep"), "tp", None),
        P(("groups", "ep"), "tp", None),
        P(("groups", "ep")),
        P(("groups", "ep"), "tp"),
        P(),
        P(("groups", "ep"), None),
        P(("groups", "ep"), None),
        P("ep", None, None, "tp"),
        P("ep", "tp", None),
    )
    out_specs = (P(("groups", "ep"), "tp", None), P(("groups", "ep"), "tp"))
    return jax.shard_map(
        per_device, mesh=mesh, in_specs=in_specs, out_specs=out_specs, check_vma=False
    )
```

```python
import functools

import jax
import jax.numpy as jnp
from jax import lax
from jax.experimental import pallas as pl
from jax.experimental.pallas import tpu as pltpu
from jax.sharding import PartitionSpec as P


def attention_block(queries, key_cache, value_cache, new_key, new_value, lengths):
    rows_here, heads_here, head_size = queries.shape
    kv_here = key_cache.shape[2]
    slots_here = key_cache.shape[1]
    group = heads_here // kv_here
    scale = 1.0 / head_size**0.5
    grouped = queries.reshape(rows_here, kv_here, group, head_size)
    scores = (
        jnp.einsum("akgd,ackd->akgc", grouped, key_cache, preferred_element_type=jnp.float32)
        * scale
    )
    valid = (jnp.arange(slots_here)[None, :] < lengths[:, None])[:, None, None, :]
    scores = jnp.where(valid, scores, -1e30)
    own_score = (
        jnp.einsum("akgd,akd->akg", grouped, new_key, preferred_element_type=jnp.float32) * scale
    )
    largest = jnp.maximum(jnp.max(scores, axis=-1), own_score)
    cache_exp = jnp.exp(scores - largest[..., None])
    own_exp = jnp.exp(own_score - largest)
    total = jnp.sum(cache_exp, axis=-1) + own_exp
    cache_probs = (cache_exp / total[..., None]).astype(jnp.bfloat16)
    own_probs = (own_exp / total).astype(jnp.bfloat16)
    mixed = jnp.einsum(
        "akgc,ackd->akgd", cache_probs, value_cache, preferred_element_type=jnp.float32
    )
    mixed = (
        mixed
        + own_probs.astype(jnp.float32)[..., None] * new_value.astype(jnp.float32)[:, :, None, :]
    )
    return mixed.reshape(rows_here, heads_here, head_size).astype(jnp.bfloat16)


def normalize(residual, norm_gain):
    wide = residual.astype(jnp.float32)
    return (
        wide * lax.rsqrt(jnp.mean(wide * wide, axis=1, keepdims=True) + 1e-06) * norm_gain
    ).astype(jnp.bfloat16)


def load(sources, targets, sems):
    copies = [
        pltpu.make_async_copy(source, target, sems.at[i])
        for i, (source, target) in enumerate(zip(sources, targets))
    ]
    for copy in copies:
        copy.start()
    return copies


def stay(array):
    return pltpu.with_memory_space_constraint(array, pltpu.HBM)


HERE = pl.BlockSpec(memory_space=pltpu.VMEM)
ANYWHERE = pl.BlockSpec(memory_space=pl.ANY)


def params(mebibytes=4):
    return pltpu.CompilerParams(vmem_limit_bytes=mebibytes * 1024 * 1024)


def cost(flops=0, bytes_accessed=0):
    return pl.CostEstimate(flops=flops, bytes_accessed=bytes_accessed, transcendentals=0)


def from_hbm(kernel, out_shape, name, arrays, after=(), cost_estimate=None):
    return pl.pallas_call(
        kernel,
        out_shape=out_shape,
        in_specs=[pl.BlockSpec(memory_space=pltpu.HBM)] * len(arrays) + [ANYWHERE] * len(after),
        scratch_shapes=[
            (pltpu.VMEM if array.ndim > 1 else pltpu.SMEM)(array.shape, array.dtype)
            for array in arrays
        ]
        + [pltpu.SemaphoreType.DMA((len(arrays),))],
        compiler_params=params(),
        cost_estimate=cost_estimate,
        name=name,
    )(*(stay(array) for array in arrays), *after)


def attend_kernel(*refs):
    attended_ref = refs[-8]
    lengths_ref, queries_ref, keys_ref, values_ref, new_keys_ref, new_values_ref = refs[-7:-1]
    copies = load(refs[:6], refs[-7:-1], refs[-1])
    row_count, heads, head_size = queries_ref.shape
    kv_heads = new_keys_ref.shape[0] // row_count
    group = heads // kv_heads
    scale = 1.0 / head_size**0.5
    across = (((1,), (1,)), ((), ()))

    def grids(columns):
        shape = (heads, columns)
        head = lax.broadcasted_iota(jnp.int32, shape, 0) // group
        return head, lax.broadcasted_iota(jnp.int32, shape, 1)

    head, column = grids(keys_ref.shape[1])
    own_head, own_column = grids(new_keys_ref.shape[0])
    same_head = column % kv_heads == head
    slot = column // kv_heads
    for copy in copies:
        copy.wait()
    for a in range(row_count):
        query = queries_ref[a]
        scores = lax.dot_general(query, keys_ref[a], across, preferred_element_type=jnp.float32)
        scores = jnp.where(same_head & (slot < lengths_ref[a]), scores * scale, -1e30)
        own = lax.dot_general(
            query, new_keys_ref[...], across, preferred_element_type=jnp.float32
        )
        own = jnp.where(own_column == own_head + a * kv_heads, own * scale, -1e30)
        largest = jnp.maximum(
            jnp.max(scores, axis=1, keepdims=True), jnp.max(own, axis=1, keepdims=True)
        )
        scores = jnp.exp(scores - largest)
        own = jnp.exp(own - largest)
        total = jnp.sum(scores, axis=1, keepdims=True) + jnp.sum(own, axis=1, keepdims=True)
        mixed = jnp.dot(
            (scores / total).astype(jnp.bfloat16),
            values_ref[a],
            preferred_element_type=jnp.float32,
        ) + jnp.dot(
            (own / total).astype(jnp.bfloat16),
            new_values_ref[...],
            preferred_element_type=jnp.float32,
        )
        attended_ref[a] = mixed.astype(jnp.bfloat16)


def attend(queries, key_cache, value_cache, new_key, new_value, lengths, after):
    rows_here, slots_here, kv_here, head_size = key_cache.shape
    lines = (rows_here, slots_here * kv_here, head_size)
    arrays = (
        lengths,
        queries,
        key_cache.reshape(lines),
        value_cache.reshape(lines),
        new_key.reshape(-1, head_size),
        new_value.reshape(-1, head_size),
    )
    out_shape = jax.ShapeDtypeStruct(queries.shape, jnp.bfloat16)
    work = cost(0, 16 * key_cache.size * key_cache.dtype.itemsize)
    return from_hbm(attend_kernel, out_shape, "attend", arrays, after, work)


def hold_kernel(count, pieces, *refs):
    sources, targets, sems = refs[:count], refs[-1 - count : -1], refs[-1]
    starts, ends = [], []
    for source, target in zip(sources, targets):
        lines = source.shape[0] // pieces
        for i in range(pieces):
            starts.append(source.at[pl.ds(i * lines, lines)])
            ends.append(target.at[pl.ds(i * lines, lines)])
    for copy in load(starts, ends, sems):
        copy.wait()


def hold(arrays, after, pieces=4):
    flat = [array.reshape(-1, array.shape[-1]) for array in arrays]
    size = sum(array.size for array in flat)
    return pl.pallas_call(
        functools.partial(hold_kernel, len(flat), pieces),
        out_shape=[pltpu.VMEM(array.shape, array.dtype) for array in flat],
        in_specs=[pl.BlockSpec(memory_space=pltpu.HBM)] * len(flat) + [ANYWHERE] * len(after),
        scratch_shapes=[pltpu.SemaphoreType.DMA((pieces * len(flat),))],
        cost_estimate=cost(0, 2 * size),
        compiler_params=params(),
        name="hold",
    )(*(stay(array) for array in flat), *after)


def prepare_kernel(*refs):
    packed_ref, residual_ref, gain_ref, routes_ref, weights_ref, sems = refs[4:]
    for copy in load(refs[:4], refs[5:9], sems):
        copy.wait()
    row_count, width = residual_ref.shape
    experts = lax.axis_size("ep")
    lanes = packed_ref.shape[1] - width
    wide = residual_ref[...].astype(jnp.float32)
    mean = jnp.mean(wide * wide, axis=1, keepdims=True)
    packed_ref[:, :width] = (wide * lax.rsqrt(mean + 1e-06) * gain_ref[...]).astype(jnp.bfloat16)
    line = lax.broadcasted_iota(jnp.int32, (lanes, row_count), 0)
    expert = lax.rem(line, experts)
    weight = jnp.zeros(line.shape, jnp.float32)
    for k in range(routes_ref.shape[0]):
        weight += jnp.where(routes_ref[k : k + 1, :] == expert, weights_ref[k : k + 1, :], 0.0)
    high = weight.astype(jnp.bfloat16).astype(jnp.float32)
    low = (weight - high).astype(jnp.bfloat16).astype(jnp.float32)
    lowest = weight - high - low
    terms = jnp.where(
        line < experts,
        high,
        jnp.where(line < 2 * experts, low, jnp.where(line < 3 * experts, lowest, 0.0)),
    )
    at = lax.broadcasted_iota(jnp.int32, (row_count, row_count), 0)
    same = at == lax.broadcasted_iota(jnp.int32, (row_count, row_count), 1)
    turned = lax.dot_general(
        same.astype(jnp.bfloat16),
        terms.astype(jnp.bfloat16),
        (((1,), (1,)), ((), ())),
        preferred_element_type=jnp.float32,
    )
    packed_ref[:, width:] = turned.astype(jnp.bfloat16)


def stack_kernel(*refs):
    for i in range(refs[-1].shape[0]):
        refs[-1][i] = refs[i][...]


def relay_kernel(in_ref, *refs):
    refs[-1][...] = in_ref[...]


def expert(packed, in_ref, down_ref):
    width = down_ref.shape[1]
    rows = packed[:, :width]
    terms = packed[:, width:].astype(jnp.float32)
    lane = lax.broadcasted_iota(jnp.int32, terms.shape, 1)
    mine = lax.rem(lane, lax.axis_size("ep")) == lax.axis_index("ep")
    weight = jnp.sum(jnp.where(mine, terms, 0.0), axis=1, keepdims=True)
    gate = jnp.dot(rows, in_ref[:width], preferred_element_type=jnp.float32)
    up = jnp.dot(rows, in_ref[width:], preferred_element_type=jnp.float32)
    hidden = (gate / (1.0 + jnp.exp(-gate)) * up).astype(jnp.bfloat16)
    out = jnp.dot(hidden, down_ref[...], preferred_element_type=jnp.float32)
    return (out * weight).astype(jnp.bfloat16)


def ffn_kernel(count, takes, *refs):
    in_ref, down_ref = refs[count : count + 2]
    packed = jnp.concatenate([refs[i][b] for i, b in takes], axis=0)
    out = expert(packed, in_ref, down_ref)
    row_count = out.shape[0] // len(takes)
    near_ref, far_ref = refs[-2:]
    half = near_ref.shape[0]
    near_ref[...] = out[: half * row_count].reshape(near_ref.shape)
    far_ref[...] = out[half * row_count :].reshape(far_ref.shape)


def rest_kernel(blocks_ref, before_ref, in_ref, down_ref, out_ref):
    packed = jnp.concatenate([blocks_ref[0], blocks_ref[1]], axis=0)
    out_ref[:2] = before_ref[...]
    out_ref[2:] = expert(packed, in_ref, down_ref).reshape(before_ref.shape)


def pair_kernel(own_ref, other_ref, *refs):
    for i, out_ref in enumerate(refs[-own_ref.shape[0] :]):
        total = own_ref[i].astype(jnp.float32) + other_ref[i].astype(jnp.float32)
        out_ref[...] = total.astype(out_ref.dtype)


def add_kernel(own_ref, other_ref, *refs):
    refs[-1][...] = (own_ref[...] + other_ref[...].astype(jnp.float32)).astype(refs[-1].dtype)


def total_kernel(residual_ref, *refs):
    total = residual_ref[...].astype(jnp.float32)
    for ref in refs[:-1]:
        total += ref[...].astype(jnp.float32)
    refs[-1][...] = total.astype(refs[-1].dtype)


def in_vmem(kernel, out_shape, name, arrays, after=(), mebibytes=4, cost_estimate=None):
    return pl.pallas_call(
        kernel,
        out_shape=out_shape,
        in_specs=[HERE] * len(arrays) + [ANYWHERE] * len(after),
        compiler_params=params(mebibytes),
        cost_estimate=cost_estimate,
        name=name,
    )(*arrays, *after)


def layer_gathered(attention, residual, norm_gain, routes, route_weights, expert_in, expert_down):
    row_count, width = residual.shape
    devices = lax.axis_size("ep")
    core, side, line = 1, 2, 4
    extra = -(-3 * devices // 128) * 128
    vmem = pltpu.VMEM
    one = (row_count, width)
    block = vmem((row_count, width + extra), jnp.bfloat16)

    def swap(value, bits):
        return lax.ppermute(value, "ep", [(i, i ^ bits) for i in range(devices)])

    def relay(value, after):
        return in_vmem(relay_kernel, vmem(value.shape, value.dtype), "relay", (value,), after)

    def stack(members, after=()):
        shape = vmem((len(members), row_count, width + extra), jnp.bfloat16)
        return in_vmem(stack_kernel, shape, "stack", members, after)

    packed = from_hbm(
        prepare_kernel,
        block,
        "prepare",
        (residual, norm_gain.reshape(1, -1), routes.T, route_weights.T),
    )
    third, second, first = (swap(packed, d * line) for d in (3, 2, 1))
    across = swap(packed, side)
    attended = attend(*attention, (packed,))
    along = stack((second, third, first), (stay(attended),))
    along_side = swap(along, side)
    near = stack((second, third, first, packed, across))
    near_far = swap(near, core)
    held = hold((expert_in, expert_down), (along,))
    along_side_far = swap(relay(along_side, held[:1]), core)

    def ffn(kernel, operands, rows, out_shape, after=()):
        flops = 2 * rows * sum(h.size for h in held)
        work = cost(flops, 2 * held[0].size)
        return in_vmem(kernel, out_shape, "ffn", (*operands, *held), after, 16, work)

    takes = [(i, b) for i in range(3) for b in range(2)]
    early_near, early_part = ffn(
        functools.partial(ffn_kernel, 3, takes),
        (near, along_side, near_far),
        6 * row_count,
        [vmem((n,) + one, jnp.bfloat16) for n in (4, 2)],
    )
    early_far = ffn(
        rest_kernel,
        (along_side_far, early_part),
        2 * row_count,
        vmem((4,) + one, jnp.bfloat16),
    )
    send = vmem(one, jnp.bfloat16)
    keep_and_send = [vmem(one, jnp.float32)] * 2 + [send] * 2
    second_keep, third_keep, second_send, third_send = in_vmem(
        pair_kernel, keep_and_send, "pair_sum", (early_near, swap(early_far, core))
    )
    third_sum = in_vmem(add_kernel, send, "side_sum", (third_keep, swap(third_send, side)))
    second_sum = in_vmem(
        add_kernel, send, "side_sum", (second_keep, swap(second_send, side)), (third_sum,)
    )
    partial_sum = in_vmem(
        total_kernel,
        vmem(one, jnp.float32),
        "partial_sum",
        (residual, swap(third_sum, 3 * line), swap(second_sum, 2 * line)),
    )
    takes = [(i, b) for i in (0, 2) for b in (3, 4, 2)]
    takes[3:3] = [(1, 2)]
    late_outs = ffn(
        functools.partial(ffn_kernel, 4, takes + [(3, 2)]),
        (near, along_side, near_far, along_side_far),
        8 * row_count,
        [vmem((4,) + one, jnp.bfloat16)] * 2,
        (early_far,),
    )
    own, across_sum, first_sum, diagonal_sum = in_vmem(
        pair_kernel,
        [vmem(one, jnp.float32), send, send, send],
        "pair_sum",
        (late_outs[0], swap(late_outs[1], core)),
        (third_send,),
    )
    moe_out = in_vmem(
        total_kernel,
        jax.ShapeDtypeStruct(one, jnp.bfloat16),
        "total",
        (
            partial_sum,
            own,
            swap(diagonal_sum, line + side),
            swap(first_sum, line),
            swap(across_sum, side),
        ),
    )
    return attended, moe_out


def expert_layer_routed(residual, norm_gain, routes, route_weights, expert_in, expert_down):
    row_count, top_count = routes.shape
    expert_count = expert_in.shape[0] * lax.axis_size("ep")
    capacity = min(row_count, max(2, 2 * row_count * top_count // expert_count))
    whole = lax.all_gather(residual, "tp", axis=1, tiled=True)
    width = whole.shape[1]
    half_width = residual.shape[1]
    normed = normalize(whole, norm_gain)
    flat_routes = routes.reshape(-1)
    hits = (flat_routes[:, None] == jnp.arange(expert_count)[None, :]).astype(jnp.int32)
    before = jnp.cumsum(hits, axis=0) - hits
    position = jnp.sum(before * hits, axis=1)
    slot_flat = flat_routes * capacity + position
    placed = (slot_flat[:, None] == jnp.arange(expert_count * capacity)[None, :]).astype(
        jnp.float32
    )
    placed = placed.reshape(row_count, top_count, expert_count * capacity)
    selector = jnp.sum(placed, axis=1).astype(jnp.bfloat16)
    buffer = jnp.einsum("rs,rd->sd", selector, normed, preferred_element_type=jnp.float32)
    buffer = buffer.astype(jnp.bfloat16).reshape(expert_count, capacity, width)
    arrived = lax.all_to_all(buffer, "ep", split_axis=0, concat_axis=0, tiled=True)
    sources = arrived.shape[0]
    flat_rows = arrived.reshape(sources * capacity, width)
    gate_act = jnp.dot(flat_rows, expert_in[0, 0], preferred_element_type=jnp.float32)
    up_act = jnp.dot(flat_rows, expert_in[0, 1], preferred_element_type=jnp.float32)
    hidden = (jax.nn.silu(gate_act) * up_act).astype(jnp.bfloat16)
    partial_value = jnp.dot(hidden, expert_down[0], preferred_element_type=jnp.float32)
    partial_value = partial_value.reshape(sources, capacity, width)
    summed = lax.psum_scatter(partial_value, "tp", scatter_dimension=2, tiled=True).astype(
        jnp.bfloat16
    )
    returned = lax.all_to_all(summed, "ep", split_axis=0, concat_axis=0, tiled=True)
    weighting = jnp.sum(placed * route_weights[:, :, None], axis=1)
    gathered_rows = returned.reshape(expert_count * capacity, half_width).astype(jnp.float32)
    combined = jnp.dot(weighting, gathered_rows, precision=lax.Precision.HIGHEST)
    return (residual.astype(jnp.float32) + combined).astype(jnp.bfloat16)


def per_device(
    queries,
    key_cache,
    value_cache,
    new_key,
    new_value,
    lengths,
    residual,
    norm_gain,
    routes,
    route_weights,
    expert_in,
    expert_down,
):
    devices = lax.axis_size("ep")
    dense = lax.axis_size("tp") == 1 and devices == 16
    attention = (queries, key_cache, value_cache, new_key, new_value, lengths)
    layer = (residual, norm_gain, routes, route_weights)
    if dense:
        return layer_gathered(attention, *layer, expert_in, expert_down)
    attended = attention_block(*attention)
    return (attended, expert_layer_routed(*layer, expert_in, expert_down))


def solution(mesh):
    in_specs = (
        P(("groups", "ep"), "tp", None),
        P(("groups", "ep"), None, "tp", None),
        P(("groups", "ep"), None, "tp", None),
        P(("groups", "ep"), "tp", None),
        P(("groups", "ep"), "tp", None),
        P(("groups", "ep")),
        P(("groups", "ep"), "tp"),
        P(),
        P(("groups", "ep"), None),
        P(("groups", "ep"), None),
        P("ep", None, None, "tp"),
        P("ep", "tp", None),
    )
    out_specs = (P(("groups", "ep"), "tp", None), P(("groups", "ep"), "tp"))
    return jax.shard_map(
        per_device, mesh=mesh, in_specs=in_specs, out_specs=out_specs, check_vma=False
    )
```

```python
import functools

import jax
import jax.numpy as jnp
from jax import lax
from jax.experimental import pallas as pl
from jax.experimental.pallas import tpu as pltpu
from jax.sharding import PartitionSpec as P


def attention_block(queries, key_cache, value_cache, new_key, new_value, lengths):
    rows_here, heads_here, head_size = queries.shape
    kv_here = key_cache.shape[2]
    slots_here = key_cache.shape[1]
    group = heads_here // kv_here
    scale = 1.0 / head_size**0.5
    grouped = queries.reshape(rows_here, kv_here, group, head_size)
    scores = (
        jnp.einsum("akgd,ackd->akgc", grouped, key_cache, preferred_element_type=jnp.float32)
        * scale
    )
    valid = (jnp.arange(slots_here)[None, :] < lengths[:, None])[:, None, None, :]
    scores = jnp.where(valid, scores, -1e30)
    own_score = (
        jnp.einsum("akgd,akd->akg", grouped, new_key, preferred_element_type=jnp.float32) * scale
    )
    largest = jnp.maximum(jnp.max(scores, axis=-1), own_score)
    cache_exp = jnp.exp(scores - largest[..., None])
    own_exp = jnp.exp(own_score - largest)
    total = jnp.sum(cache_exp, axis=-1) + own_exp
    cache_probs = (cache_exp / total[..., None]).astype(jnp.bfloat16)
    own_probs = (own_exp / total).astype(jnp.bfloat16)
    mixed = jnp.einsum(
        "akgc,ackd->akgd", cache_probs, value_cache, preferred_element_type=jnp.float32
    )
    mixed = (
        mixed
        + own_probs.astype(jnp.float32)[..., None] * new_value.astype(jnp.float32)[:, :, None, :]
    )
    return mixed.reshape(rows_here, heads_here, head_size).astype(jnp.bfloat16)


def normalize(residual, norm_gain):
    wide = residual.astype(jnp.float32)
    return (
        wide * lax.rsqrt(jnp.mean(wide * wide, axis=1, keepdims=True) + 1e-06) * norm_gain
    ).astype(jnp.bfloat16)


def load(sources, targets, sems):
    copies = [
        pltpu.make_async_copy(source, target, sems.at[i])
        for i, (source, target) in enumerate(zip(sources, targets))
    ]
    for copy in copies:
        copy.start()
    return copies


def stay(array):
    return pltpu.with_memory_space_constraint(array, pltpu.HBM)


HERE = pl.BlockSpec(memory_space=pltpu.VMEM)
ANYWHERE = pl.BlockSpec(memory_space=pl.ANY)


def params(mebibytes=4):
    return pltpu.CompilerParams(vmem_limit_bytes=mebibytes * 1024 * 1024)


def cost(flops=0, bytes_accessed=0):
    return pl.CostEstimate(flops=flops, bytes_accessed=bytes_accessed, transcendentals=0)


def from_hbm(kernel, out_shape, name, arrays, after=(), cost_estimate=None):
    return pl.pallas_call(
        kernel,
        out_shape=out_shape,
        in_specs=[pl.BlockSpec(memory_space=pltpu.HBM)] * len(arrays) + [ANYWHERE] * len(after),
        scratch_shapes=[
            (pltpu.VMEM if array.ndim > 1 else pltpu.SMEM)(array.shape, array.dtype)
            for array in arrays
        ]
        + [pltpu.SemaphoreType.DMA((len(arrays),))],
        compiler_params=params(),
        cost_estimate=cost_estimate,
        name=name,
    )(*(stay(array) for array in arrays), *after)


def attend_kernel(*refs):
    attended_ref = refs[-8]
    lengths_ref, queries_ref, keys_ref, values_ref, new_keys_ref, new_values_ref = refs[-7:-1]
    copies = load(refs[:6], refs[-7:-1], refs[-1])
    row_count, heads, head_size = queries_ref.shape
    kv_heads = new_keys_ref.shape[0] // row_count
    group = heads // kv_heads
    scale = 1.0 / head_size**0.5
    across = (((1,), (1,)), ((), ()))

    def grids(columns):
        shape = (heads, columns)
        head = lax.broadcasted_iota(jnp.int32, shape, 0) // group
        return head, lax.broadcasted_iota(jnp.int32, shape, 1)

    head, column = grids(keys_ref.shape[1])
    own_head, own_column = grids(new_keys_ref.shape[0])
    same_head = column % kv_heads == head
    slot = column // kv_heads
    for copy in copies:
        copy.wait()
    for a in range(row_count):
        query = queries_ref[a]
        scores = lax.dot_general(query, keys_ref[a], across, preferred_element_type=jnp.float32)
        scores = jnp.where(same_head & (slot < lengths_ref[a]), scores * scale, -1e30)
        own = lax.dot_general(
            query, new_keys_ref[...], across, preferred_element_type=jnp.float32
        )
        own = jnp.where(own_column == own_head + a * kv_heads, own * scale, -1e30)
        largest = jnp.maximum(
            jnp.max(scores, axis=1, keepdims=True), jnp.max(own, axis=1, keepdims=True)
        )
        scores = jnp.exp(scores - largest)
        own = jnp.exp(own - largest)
        total = jnp.sum(scores, axis=1, keepdims=True) + jnp.sum(own, axis=1, keepdims=True)
        mixed = jnp.dot(
            (scores / total).astype(jnp.bfloat16),
            values_ref[a],
            preferred_element_type=jnp.float32,
        ) + jnp.dot(
            (own / total).astype(jnp.bfloat16),
            new_values_ref[...],
            preferred_element_type=jnp.float32,
        )
        attended_ref[a] = mixed.astype(jnp.bfloat16)


def attend(queries, key_cache, value_cache, new_key, new_value, lengths, after):
    rows_here, slots_here, kv_here, head_size = key_cache.shape
    lines = (rows_here, slots_here * kv_here, head_size)
    arrays = (
        lengths,
        queries,
        key_cache.reshape(lines),
        value_cache.reshape(lines),
        new_key.reshape(-1, head_size),
        new_value.reshape(-1, head_size),
    )
    out_shape = jax.ShapeDtypeStruct(queries.shape, jnp.bfloat16)
    work = cost(0, 16 * key_cache.size * key_cache.dtype.itemsize)
    return from_hbm(attend_kernel, out_shape, "attend", arrays, after, work)


def hold_kernel(count, pieces, *refs):
    sources, targets, sems = refs[:count], refs[-1 - count : -1], refs[-1]
    starts, ends = [], []
    for source, target in zip(sources, targets):
        lines = source.shape[0] // pieces
        for i in range(pieces):
            starts.append(source.at[pl.ds(i * lines, lines)])
            ends.append(target.at[pl.ds(i * lines, lines)])
    for copy in load(starts, ends, sems):
        copy.wait()


def hold(arrays, after, pieces=4):
    flat = [array.reshape(-1, array.shape[-1]) for array in arrays]
    size = sum(array.size for array in flat)
    return pl.pallas_call(
        functools.partial(hold_kernel, len(flat), pieces),
        out_shape=[pltpu.VMEM(array.shape, array.dtype) for array in flat],
        in_specs=[pl.BlockSpec(memory_space=pltpu.HBM)] * len(flat) + [ANYWHERE] * len(after),
        scratch_shapes=[pltpu.SemaphoreType.DMA((pieces * len(flat),))],
        cost_estimate=cost(0, 2 * size),
        compiler_params=params(),
        name="hold",
    )(*(stay(array) for array in flat), *after)


def prepare_kernel(*refs):
    packed_ref, residual_ref, gain_ref, routes_ref, weights_ref, sems = refs[4:]
    for copy in load(refs[:4], refs[5:9], sems):
        copy.wait()
    row_count, width = residual_ref.shape
    experts = lax.axis_size("ep")
    lanes = packed_ref.shape[1] - width
    wide = residual_ref[...].astype(jnp.float32)
    mean = jnp.mean(wide * wide, axis=1, keepdims=True)
    packed_ref[:, :width] = (wide * lax.rsqrt(mean + 1e-06) * gain_ref[...]).astype(jnp.bfloat16)
    line = lax.broadcasted_iota(jnp.int32, (lanes, row_count), 0)
    expert = lax.rem(line, experts)
    weight = jnp.zeros(line.shape, jnp.float32)
    for k in range(routes_ref.shape[0]):
        weight += jnp.where(routes_ref[k : k + 1, :] == expert, weights_ref[k : k + 1, :], 0.0)
    high = weight.astype(jnp.bfloat16).astype(jnp.float32)
    low = (weight - high).astype(jnp.bfloat16).astype(jnp.float32)
    lowest = weight - high - low
    terms = jnp.where(
        line < experts,
        high,
        jnp.where(line < 2 * experts, low, jnp.where(line < 3 * experts, lowest, 0.0)),
    )
    at = lax.broadcasted_iota(jnp.int32, (row_count, row_count), 0)
    same = at == lax.broadcasted_iota(jnp.int32, (row_count, row_count), 1)
    turned = lax.dot_general(
        same.astype(jnp.bfloat16),
        terms.astype(jnp.bfloat16),
        (((1,), (1,)), ((), ())),
        preferred_element_type=jnp.float32,
    )
    packed_ref[:, width:] = turned.astype(jnp.bfloat16)


def stack_kernel(*refs):
    for i in range(refs[-1].shape[0]):
        refs[-1][i] = refs[i][...]


def relay_kernel(in_ref, *refs):
    refs[-1][...] = in_ref[...]


def ffn_kernel(takes, *refs):
    in_ref, down_ref = refs[4:6]
    near_ref, far_ref = refs[-2:]
    width = down_ref.shape[1]
    packed = jnp.concatenate(
        [refs[i][b] for i, start, stop in takes for b in range(start, stop)], axis=0
    )
    rows = packed[:, :width]
    terms = packed[:, width:].astype(jnp.float32)
    lane = lax.broadcasted_iota(jnp.int32, terms.shape, 1)
    mine = lax.rem(lane, lax.axis_size("ep")) == lax.axis_index("ep")
    weight = jnp.sum(jnp.where(mine, terms, 0.0), axis=1, keepdims=True)
    gate = jnp.dot(rows, in_ref[:width], preferred_element_type=jnp.float32)
    up = jnp.dot(rows, in_ref[width:], preferred_element_type=jnp.float32)
    hidden = (gate / (1.0 + jnp.exp(-gate)) * up).astype(jnp.bfloat16)
    out = jnp.dot(hidden, down_ref[...], preferred_element_type=jnp.float32)
    out = (out * weight).astype(jnp.bfloat16).reshape((2,) + near_ref.shape)
    near_ref[...] = out[0]
    far_ref[...] = out[1]


def pair_kernel(own_ref, other_ref, *refs):
    for i, out_ref in enumerate(refs[-own_ref.shape[0] :]):
        total = own_ref[i].astype(jnp.float32) + other_ref[i].astype(jnp.float32)
        out_ref[...] = total.astype(out_ref.dtype)


def half_kernel(own_ref, other_ref, keep_ref, send_ref):
    half = keep_ref.shape[0]
    keep_ref[...] = own_ref[:half].astype(jnp.float32) + other_ref[:half].astype(jnp.float32)
    send = own_ref[half:].astype(jnp.float32) + other_ref[half:].astype(jnp.float32)
    send_ref[...] = send.astype(jnp.bfloat16)


def side_kernel(own_ref, other_ref, *out_refs):
    for i, out_ref in enumerate(out_refs):
        total = own_ref[i] + other_ref[i].astype(jnp.float32)
        out_ref[...] = total.astype(out_ref.dtype)


def total_kernel(residual_ref, *refs):
    total = residual_ref[...].astype(jnp.float32)
    for ref in refs[:-1]:
        total += ref[...].astype(jnp.float32)
    refs[-1][...] = total.astype(refs[-1].dtype)


def in_vmem(kernel, out_shape, name, arrays, after=(), mebibytes=4, cost_estimate=None):
    return pl.pallas_call(
        kernel,
        out_shape=out_shape,
        in_specs=[HERE] * len(arrays) + [ANYWHERE] * len(after),
        compiler_params=params(mebibytes),
        cost_estimate=cost_estimate,
        name=name,
    )(*arrays, *after)


def layer_gathered(attention, residual, norm_gain, routes, route_weights, expert_in, expert_down):
    row_count, width = residual.shape
    devices = lax.axis_size("ep")
    core, side, line = 1, 2, 4
    extra = -(-3 * devices // 128) * 128
    vmem = pltpu.VMEM
    one = (row_count, width)
    block = vmem((row_count, width + extra), jnp.bfloat16)

    def swap(value, bits):
        return lax.ppermute(value, "ep", [(i, i ^ bits) for i in range(devices)])

    def relay(value, after):
        return in_vmem(relay_kernel, vmem(value.shape, value.dtype), "relay", (value,), after)

    def stack(members, after=()):
        shape = vmem((len(members), row_count, width + extra), jnp.bfloat16)
        return in_vmem(stack_kernel, shape, "stack", members, after)

    packed = from_hbm(
        prepare_kernel,
        block,
        "prepare",
        (residual, norm_gain.reshape(1, -1), routes.T, route_weights.T),
    )
    third, second, first = (swap(packed, d * line) for d in (3, 2, 1))
    across = swap(packed, side)
    attended = attend(*attention, (packed,))
    along = stack((second, third, first), (stay(attended),))
    along_side = swap(along, side)
    near = stack((second, third, first, packed, across))
    near_far = swap(near, core)
    held = hold((expert_in, expert_down), (along,))
    along_side_far = swap(relay(along_side, held[:1]), core)

    def ffn(near_takes, side_takes, after=()):
        takes = [(i, *t) for i in (0, 2) for t in near_takes]
        takes[len(near_takes) : len(near_takes)] = [(1, *t) for t in side_takes]
        takes += [(3, *t) for t in side_takes]
        return in_vmem(
            functools.partial(ffn_kernel, takes),
            [vmem((4,) + one, jnp.bfloat16)] * 2,
            "ffn",
            (near, along_side, near_far, along_side_far, *held),
            after,
            mebibytes=16,
            cost_estimate=cost(8 * row_count * 2 * sum(h.size for h in held), 2 * held[0].size),
        )

    early_outs = ffn([(0, 2)], [(0, 2)])
    send = vmem(one, jnp.bfloat16)
    early_keep, early_send = in_vmem(
        half_kernel,
        [vmem((2,) + one, jnp.float32), vmem((2,) + one, jnp.bfloat16)],
        "pair_sum",
        (early_outs[0], swap(early_outs[1], core)),
    )
    second_sum, third_sum = in_vmem(
        side_kernel, [send] * 2, "side_sum", (early_keep, swap(early_send, side))
    )
    partial_sum = in_vmem(
        total_kernel,
        vmem(one, jnp.float32),
        "partial_sum",
        (residual, swap(third_sum, 3 * line), swap(second_sum, 2 * line)),
    )
    late_outs = ffn([(3, 5), (2, 3)], [(2, 3)], early_outs[:1])
    own, across_sum, first_sum, diagonal_sum = in_vmem(
        pair_kernel,
        [vmem(one, jnp.float32), send, send, send],
        "pair_sum",
        (late_outs[0], swap(late_outs[1], core)),
        (early_send,),
    )
    moe_out = in_vmem(
        total_kernel,
        jax.ShapeDtypeStruct(one, jnp.bfloat16),
        "total",
        (
            partial_sum,
            own,
            swap(diagonal_sum, line + side),
            swap(first_sum, line),
            swap(across_sum, side),
        ),
    )
    return attended, moe_out


def expert_layer_routed(residual, norm_gain, routes, route_weights, expert_in, expert_down):
    row_count, top_count = routes.shape
    expert_count = expert_in.shape[0] * lax.axis_size("ep")
    capacity = min(row_count, max(2, 2 * row_count * top_count // expert_count))
    whole = lax.all_gather(residual, "tp", axis=1, tiled=True)
    width = whole.shape[1]
    half_width = residual.shape[1]
    normed = normalize(whole, norm_gain)
    flat_routes = routes.reshape(-1)
    hits = (flat_routes[:, None] == jnp.arange(expert_count)[None, :]).astype(jnp.int32)
    before = jnp.cumsum(hits, axis=0) - hits
    position = jnp.sum(before * hits, axis=1)
    slot_flat = flat_routes * capacity + position
    placed = (slot_flat[:, None] == jnp.arange(expert_count * capacity)[None, :]).astype(
        jnp.float32
    )
    placed = placed.reshape(row_count, top_count, expert_count * capacity)
    selector = jnp.sum(placed, axis=1).astype(jnp.bfloat16)
    buffer = jnp.einsum("rs,rd->sd", selector, normed, preferred_element_type=jnp.float32)
    buffer = buffer.astype(jnp.bfloat16).reshape(expert_count, capacity, width)
    arrived = lax.all_to_all(buffer, "ep", split_axis=0, concat_axis=0, tiled=True)
    sources = arrived.shape[0]
    flat_rows = arrived.reshape(sources * capacity, width)
    gate_act = jnp.dot(flat_rows, expert_in[0, 0], preferred_element_type=jnp.float32)
    up_act = jnp.dot(flat_rows, expert_in[0, 1], preferred_element_type=jnp.float32)
    hidden = (jax.nn.silu(gate_act) * up_act).astype(jnp.bfloat16)
    partial_value = jnp.dot(hidden, expert_down[0], preferred_element_type=jnp.float32)
    partial_value = partial_value.reshape(sources, capacity, width)
    summed = lax.psum_scatter(partial_value, "tp", scatter_dimension=2, tiled=True).astype(
        jnp.bfloat16
    )
    returned = lax.all_to_all(summed, "ep", split_axis=0, concat_axis=0, tiled=True)
    weighting = jnp.sum(placed * route_weights[:, :, None], axis=1)
    gathered_rows = returned.reshape(expert_count * capacity, half_width).astype(jnp.float32)
    combined = jnp.dot(weighting, gathered_rows, precision=lax.Precision.HIGHEST)
    return (residual.astype(jnp.float32) + combined).astype(jnp.bfloat16)


def per_device(
    queries,
    key_cache,
    value_cache,
    new_key,
    new_value,
    lengths,
    residual,
    norm_gain,
    routes,
    route_weights,
    expert_in,
    expert_down,
):
    devices = lax.axis_size("ep")
    dense = lax.axis_size("tp") == 1 and devices == 16
    attention = (queries, key_cache, value_cache, new_key, new_value, lengths)
    layer = (residual, norm_gain, routes, route_weights)
    if dense:
        return layer_gathered(attention, *layer, expert_in, expert_down)
    attended = attention_block(*attention)
    return (attended, expert_layer_routed(*layer, expert_in, expert_down))


def solution(mesh):
    in_specs = (
        P(("groups", "ep"), "tp", None),
        P(("groups", "ep"), None, "tp", None),
        P(("groups", "ep"), None, "tp", None),
        P(("groups", "ep"), "tp", None),
        P(("groups", "ep"), "tp", None),
        P(("groups", "ep")),
        P(("groups", "ep"), "tp"),
        P(),
        P(("groups", "ep"), None),
        P(("groups", "ep"), None),
        P("ep", None, None, "tp"),
        P("ep", "tp", None),
    )
    out_specs = (P(("groups", "ep"), "tp", None), P(("groups", "ep"), "tp"))
    return jax.shard_map(
        per_device, mesh=mesh, in_specs=in_specs, out_specs=out_specs, check_vma=False
    )
```

```python
import functools

import jax
import jax.numpy as jnp
from jax import lax
from jax.experimental import pallas as pl
from jax.experimental.pallas import tpu as pltpu
from jax.sharding import PartitionSpec as P


def attention_block(queries, key_cache, value_cache, new_key, new_value, lengths):
    rows_here, heads_here, head_size = queries.shape
    kv_here = key_cache.shape[2]
    slots_here = key_cache.shape[1]
    group = heads_here // kv_here
    scale = 1.0 / head_size**0.5
    grouped = queries.reshape(rows_here, kv_here, group, head_size)
    scores = (
        jnp.einsum("akgd,ackd->akgc", grouped, key_cache, preferred_element_type=jnp.float32)
        * scale
    )
    valid = (jnp.arange(slots_here)[None, :] < lengths[:, None])[:, None, None, :]
    scores = jnp.where(valid, scores, -1e30)
    own_score = (
        jnp.einsum("akgd,akd->akg", grouped, new_key, preferred_element_type=jnp.float32) * scale
    )
    largest = jnp.maximum(jnp.max(scores, axis=-1), own_score)
    cache_exp = jnp.exp(scores - largest[..., None])
    own_exp = jnp.exp(own_score - largest)
    total = jnp.sum(cache_exp, axis=-1) + own_exp
    cache_probs = (cache_exp / total[..., None]).astype(jnp.bfloat16)
    own_probs = (own_exp / total).astype(jnp.bfloat16)
    mixed = jnp.einsum(
        "akgc,ackd->akgd", cache_probs, value_cache, preferred_element_type=jnp.float32
    )
    mixed = (
        mixed
        + own_probs.astype(jnp.float32)[..., None] * new_value.astype(jnp.float32)[:, :, None, :]
    )
    return mixed.reshape(rows_here, heads_here, head_size).astype(jnp.bfloat16)


def normalize(residual, norm_gain):
    wide = residual.astype(jnp.float32)
    return (
        wide * lax.rsqrt(jnp.mean(wide * wide, axis=1, keepdims=True) + 1e-06) * norm_gain
    ).astype(jnp.bfloat16)


def load(sources, targets, sems):
    copies = [
        pltpu.make_async_copy(source, target, sems.at[i])
        for i, (source, target) in enumerate(zip(sources, targets))
    ]
    for copy in copies:
        copy.start()
    return copies


def stay(array):
    return pltpu.with_memory_space_constraint(array, pltpu.HBM)


HERE = pl.BlockSpec(memory_space=pltpu.VMEM)
ANYWHERE = pl.BlockSpec(memory_space=pl.ANY)


def params(mebibytes=4):
    return pltpu.CompilerParams(vmem_limit_bytes=mebibytes * 1024 * 1024)


def cost(flops=0, bytes_accessed=0):
    return pl.CostEstimate(flops=flops, bytes_accessed=bytes_accessed, transcendentals=0)


def from_hbm(kernel, out_shape, name, arrays, after=(), cost_estimate=None):
    return pl.pallas_call(
        kernel,
        out_shape=out_shape,
        in_specs=[pl.BlockSpec(memory_space=pltpu.HBM)] * len(arrays) + [ANYWHERE] * len(after),
        scratch_shapes=[
            (pltpu.VMEM if array.ndim > 1 else pltpu.SMEM)(array.shape, array.dtype)
            for array in arrays
        ]
        + [pltpu.SemaphoreType.DMA((len(arrays),))],
        compiler_params=params(),
        cost_estimate=cost_estimate,
        name=name,
    )(*(stay(array) for array in arrays), *after)


def attend_kernel(*refs):
    attended_ref = refs[-8]
    lengths_ref, queries_ref, keys_ref, values_ref, new_keys_ref, new_values_ref = refs[-7:-1]
    copies = load(refs[:6], refs[-7:-1], refs[-1])
    row_count, heads, head_size = queries_ref.shape
    kv_heads = new_keys_ref.shape[0] // row_count
    group = heads // kv_heads
    scale = 1.0 / head_size**0.5
    across = (((1,), (1,)), ((), ()))

    def grids(columns):
        shape = (heads, columns)
        head = lax.broadcasted_iota(jnp.int32, shape, 0) // group
        return head, lax.broadcasted_iota(jnp.int32, shape, 1)

    head, column = grids(keys_ref.shape[1])
    own_head, own_column = grids(new_keys_ref.shape[0])
    same_head = column % kv_heads == head
    slot = column // kv_heads
    for copy in copies:
        copy.wait()
    for a in range(row_count):
        query = queries_ref[a]
        scores = lax.dot_general(query, keys_ref[a], across, preferred_element_type=jnp.float32)
        scores = jnp.where(same_head & (slot < lengths_ref[a]), scores * scale, -1e30)
        own = lax.dot_general(
            query, new_keys_ref[...], across, preferred_element_type=jnp.float32
        )
        own = jnp.where(own_column == own_head + a * kv_heads, own * scale, -1e30)
        largest = jnp.maximum(
            jnp.max(scores, axis=1, keepdims=True), jnp.max(own, axis=1, keepdims=True)
        )
        scores = jnp.exp(scores - largest)
        own = jnp.exp(own - largest)
        total = jnp.sum(scores, axis=1, keepdims=True) + jnp.sum(own, axis=1, keepdims=True)
        mixed = jnp.dot(
            (scores / total).astype(jnp.bfloat16),
            values_ref[a],
            preferred_element_type=jnp.float32,
        ) + jnp.dot(
            (own / total).astype(jnp.bfloat16),
            new_values_ref[...],
            preferred_element_type=jnp.float32,
        )
        attended_ref[a] = mixed.astype(jnp.bfloat16)


def attend(queries, key_cache, value_cache, new_key, new_value, lengths, after):
    rows_here, slots_here, kv_here, head_size = key_cache.shape
    lines = (rows_here, slots_here * kv_here, head_size)
    arrays = (
        lengths,
        queries,
        key_cache.reshape(lines),
        value_cache.reshape(lines),
        new_key.reshape(-1, head_size),
        new_value.reshape(-1, head_size),
    )
    out_shape = jax.ShapeDtypeStruct(queries.shape, jnp.bfloat16)
    work = cost(0, 16 * key_cache.size * key_cache.dtype.itemsize)
    return from_hbm(attend_kernel, out_shape, "attend", arrays, after, work)


def hold_kernel(count, pieces, *refs):
    sources, targets, sems = refs[:count], refs[-1 - count : -1], refs[-1]
    starts, ends = [], []
    for source, target in zip(sources, targets):
        lines = source.shape[0] // pieces
        for i in range(pieces):
            starts.append(source.at[pl.ds(i * lines, lines)])
            ends.append(target.at[pl.ds(i * lines, lines)])
    for copy in load(starts, ends, sems):
        copy.wait()


def hold(arrays, after, pieces=4):
    flat = [array.reshape(-1, array.shape[-1]) for array in arrays]
    size = sum(array.size for array in flat)
    return pl.pallas_call(
        functools.partial(hold_kernel, len(flat), pieces),
        out_shape=[pltpu.VMEM(array.shape, array.dtype) for array in flat],
        in_specs=[pl.BlockSpec(memory_space=pltpu.HBM)] * len(flat) + [ANYWHERE] * len(after),
        scratch_shapes=[pltpu.SemaphoreType.DMA((pieces * len(flat),))],
        cost_estimate=cost(0, 2 * size),
        compiler_params=params(),
        name="hold",
    )(*(stay(array) for array in flat), *after)


def prepare_kernel(*refs):
    packed_ref, residual_ref, gain_ref, routes_ref, weights_ref, sems = refs[4:]
    for copy in load(refs[:4], refs[5:9], sems):
        copy.wait()
    row_count, width = residual_ref.shape
    experts = lax.axis_size("ep")
    lanes = packed_ref.shape[1] - width
    wide = residual_ref[...].astype(jnp.float32)
    mean = jnp.mean(wide * wide, axis=1, keepdims=True)
    packed_ref[:, :width] = (wide * lax.rsqrt(mean + 1e-06) * gain_ref[...]).astype(jnp.bfloat16)
    line = lax.broadcasted_iota(jnp.int32, (lanes, row_count), 0)
    expert = lax.rem(line, experts)
    weight = jnp.zeros(line.shape, jnp.float32)
    for k in range(routes_ref.shape[0]):
        weight += jnp.where(routes_ref[k : k + 1, :] == expert, weights_ref[k : k + 1, :], 0.0)
    high = weight.astype(jnp.bfloat16).astype(jnp.float32)
    low = (weight - high).astype(jnp.bfloat16).astype(jnp.float32)
    lowest = weight - high - low
    terms = jnp.where(
        line < experts,
        high,
        jnp.where(line < 2 * experts, low, jnp.where(line < 3 * experts, lowest, 0.0)),
    )
    at = lax.broadcasted_iota(jnp.int32, (row_count, row_count), 0)
    same = at == lax.broadcasted_iota(jnp.int32, (row_count, row_count), 1)
    turned = lax.dot_general(
        same.astype(jnp.bfloat16),
        terms.astype(jnp.bfloat16),
        (((1,), (1,)), ((), ())),
        preferred_element_type=jnp.float32,
    )
    packed_ref[:, width:] = turned.astype(jnp.bfloat16)


def stack_kernel(*refs):
    for i in range(refs[-1].shape[0]):
        refs[-1][i] = refs[i][...]


def relay_kernel(in_ref, *refs):
    refs[-1][...] = in_ref[...]


def ffn_kernel(takes, *refs):
    in_ref, down_ref = refs[4:6]
    near_ref, far_ref = refs[-2:]
    width = down_ref.shape[1]
    packed = jnp.concatenate(
        [refs[i][b] for i, start, stop in takes for b in range(start, stop)], axis=0
    )
    rows = packed[:, :width]
    terms = packed[:, width:].astype(jnp.float32)
    lane = lax.broadcasted_iota(jnp.int32, terms.shape, 1)
    mine = lax.rem(lane, lax.axis_size("ep")) == lax.axis_index("ep")
    weight = jnp.sum(jnp.where(mine, terms, 0.0), axis=1, keepdims=True)
    gate = jnp.dot(rows, in_ref[:width], preferred_element_type=jnp.float32)
    up = jnp.dot(rows, in_ref[width:], preferred_element_type=jnp.float32)
    hidden = (gate / (1.0 + jnp.exp(-gate)) * up).astype(jnp.bfloat16)
    out = jnp.dot(hidden, down_ref[...], preferred_element_type=jnp.float32)
    out = (out * weight).astype(jnp.bfloat16).reshape((2,) + near_ref.shape)
    near_ref[...] = out[0]
    far_ref[...] = out[1]


def pair_kernel(own_ref, other_ref, *refs):
    for i, out_ref in enumerate(refs[-own_ref.shape[0] :]):
        total = own_ref[i].astype(jnp.float32) + other_ref[i].astype(jnp.float32)
        out_ref[...] = total.astype(out_ref.dtype)


def add_kernel(own_ref, other_ref, *refs):
    refs[-1][...] = (own_ref[...] + other_ref[...].astype(jnp.float32)).astype(refs[-1].dtype)


def total_kernel(residual_ref, *refs):
    total = residual_ref[...].astype(jnp.float32)
    for ref in refs[:-1]:
        total += ref[...].astype(jnp.float32)
    refs[-1][...] = total.astype(refs[-1].dtype)


def in_vmem(kernel, out_shape, name, arrays, after=(), mebibytes=4, cost_estimate=None):
    return pl.pallas_call(
        kernel,
        out_shape=out_shape,
        in_specs=[HERE] * len(arrays) + [ANYWHERE] * len(after),
        compiler_params=params(mebibytes),
        cost_estimate=cost_estimate,
        name=name,
    )(*arrays, *after)


def layer_gathered(attention, residual, norm_gain, routes, route_weights, expert_in, expert_down):
    row_count, width = residual.shape
    devices = lax.axis_size("ep")
    core, side, line = 1, 2, 4
    extra = -(-3 * devices // 128) * 128
    vmem = pltpu.VMEM
    one = (row_count, width)
    block = vmem((row_count, width + extra), jnp.bfloat16)

    def swap(value, bits):
        return lax.ppermute(value, "ep", [(i, i ^ bits) for i in range(devices)])

    def relay(value, after):
        return in_vmem(relay_kernel, vmem(value.shape, value.dtype), "relay", (value,), after)

    def stack(members, after=()):
        shape = vmem((len(members), row_count, width + extra), jnp.bfloat16)
        return in_vmem(stack_kernel, shape, "stack", members, after)

    packed = from_hbm(
        prepare_kernel,
        block,
        "prepare",
        (residual, norm_gain.reshape(1, -1), routes.T, route_weights.T),
    )
    third, second, first = (swap(packed, d * line) for d in (3, 2, 1))
    across = swap(packed, side)
    attended = attend(*attention, (packed,))
    along = stack((second, third, first), (stay(attended),))
    along_side = swap(along, side)
    near = stack((second, third, first, packed, across))
    near_far = swap(near, core)
    held = hold((expert_in, expert_down), (along,))
    along_side_far = swap(relay(along_side, held[:1]), core)

    def ffn(near_takes, side_takes, after=()):
        takes = [(i, *t) for i in (0, 2) for t in near_takes]
        takes[len(near_takes) : len(near_takes)] = [(1, *t) for t in side_takes]
        takes += [(3, *t) for t in side_takes]
        return in_vmem(
            functools.partial(ffn_kernel, takes),
            [vmem((4,) + one, jnp.bfloat16)] * 2,
            "ffn",
            (near, along_side, near_far, along_side_far, *held),
            after,
            mebibytes=16,
            cost_estimate=cost(8 * row_count * 2 * sum(h.size for h in held), 2 * held[0].size),
        )

    early_outs = ffn([(0, 2)], [(0, 2)])
    send = vmem(one, jnp.bfloat16)
    keep_and_send = [vmem(one, jnp.float32)] * 2 + [send] * 2
    second_keep, third_keep, second_send, third_send = in_vmem(
        pair_kernel, keep_and_send, "pair_sum", (early_outs[0], swap(early_outs[1], core))
    )
    second_sum = in_vmem(add_kernel, send, "side_sum", (second_keep, swap(second_send, side)))
    third_sum = in_vmem(
        add_kernel, send, "side_sum", (third_keep, swap(third_send, side)), (second_sum,)
    )
    partial_sum = in_vmem(
        total_kernel,
        vmem(one, jnp.float32),
        "partial_sum",
        (residual, swap(second_sum, 2 * line), swap(third_sum, 3 * line)),
    )
    late_outs = ffn([(3, 5), (2, 3)], [(2, 3)], early_outs[:1])
    own, across_sum, first_sum, diagonal_sum = in_vmem(
        pair_kernel,
        [vmem(one, jnp.float32), send, send, send],
        "pair_sum",
        (late_outs[0], swap(late_outs[1], core)),
        (third_send,),
    )
    moe_out = in_vmem(
        total_kernel,
        jax.ShapeDtypeStruct(one, jnp.bfloat16),
        "total",
        (
            partial_sum,
            own,
            swap(diagonal_sum, line + side),
            swap(first_sum, line),
            swap(across_sum, side),
        ),
    )
    return attended, moe_out


def expert_layer_routed(residual, norm_gain, routes, route_weights, expert_in, expert_down):
    row_count, top_count = routes.shape
    expert_count = expert_in.shape[0] * lax.axis_size("ep")
    capacity = min(row_count, max(2, 2 * row_count * top_count // expert_count))
    whole = lax.all_gather(residual, "tp", axis=1, tiled=True)
    width = whole.shape[1]
    half_width = residual.shape[1]
    normed = normalize(whole, norm_gain)
    flat_routes = routes.reshape(-1)
    hits = (flat_routes[:, None] == jnp.arange(expert_count)[None, :]).astype(jnp.int32)
    before = jnp.cumsum(hits, axis=0) - hits
    position = jnp.sum(before * hits, axis=1)
    slot_flat = flat_routes * capacity + position
    placed = (slot_flat[:, None] == jnp.arange(expert_count * capacity)[None, :]).astype(
        jnp.float32
    )
    placed = placed.reshape(row_count, top_count, expert_count * capacity)
    selector = jnp.sum(placed, axis=1).astype(jnp.bfloat16)
    buffer = jnp.einsum("rs,rd->sd", selector, normed, preferred_element_type=jnp.float32)
    buffer = buffer.astype(jnp.bfloat16).reshape(expert_count, capacity, width)
    arrived = lax.all_to_all(buffer, "ep", split_axis=0, concat_axis=0, tiled=True)
    sources = arrived.shape[0]
    flat_rows = arrived.reshape(sources * capacity, width)
    gate_act = jnp.dot(flat_rows, expert_in[0, 0], preferred_element_type=jnp.float32)
    up_act = jnp.dot(flat_rows, expert_in[0, 1], preferred_element_type=jnp.float32)
    hidden = (jax.nn.silu(gate_act) * up_act).astype(jnp.bfloat16)
    partial_value = jnp.dot(hidden, expert_down[0], preferred_element_type=jnp.float32)
    partial_value = partial_value.reshape(sources, capacity, width)
    summed = lax.psum_scatter(partial_value, "tp", scatter_dimension=2, tiled=True).astype(
        jnp.bfloat16
    )
    returned = lax.all_to_all(summed, "ep", split_axis=0, concat_axis=0, tiled=True)
    weighting = jnp.sum(placed * route_weights[:, :, None], axis=1)
    gathered_rows = returned.reshape(expert_count * capacity, half_width).astype(jnp.float32)
    combined = jnp.dot(weighting, gathered_rows, precision=lax.Precision.HIGHEST)
    return (residual.astype(jnp.float32) + combined).astype(jnp.bfloat16)


def per_device(
    queries,
    key_cache,
    value_cache,
    new_key,
    new_value,
    lengths,
    residual,
    norm_gain,
    routes,
    route_weights,
    expert_in,
    expert_down,
):
    devices = lax.axis_size("ep")
    dense = lax.axis_size("tp") == 1 and devices == 16
    attention = (queries, key_cache, value_cache, new_key, new_value, lengths)
    layer = (residual, norm_gain, routes, route_weights)
    if dense:
        return layer_gathered(attention, *layer, expert_in, expert_down)
    attended = attention_block(*attention)
    return (attended, expert_layer_routed(*layer, expert_in, expert_down))


def solution(mesh):
    in_specs = (
        P(("groups", "ep"), "tp", None),
        P(("groups", "ep"), None, "tp", None),
        P(("groups", "ep"), None, "tp", None),
        P(("groups", "ep"), "tp", None),
        P(("groups", "ep"), "tp", None),
        P(("groups", "ep")),
        P(("groups", "ep"), "tp"),
        P(),
        P(("groups", "ep"), None),
        P(("groups", "ep"), None),
        P("ep", None, None, "tp"),
        P("ep", "tp", None),
    )
    out_specs = (P(("groups", "ep"), "tp", None), P(("groups", "ep"), "tp"))
    return jax.shard_map(
        per_device, mesh=mesh, in_specs=in_specs, out_specs=out_specs, check_vma=False
    )
```
